256 devices in a mesh: grp: 2 (over core), fsdp: 16 (over z_hi, x), tp: 8 (over z_lo, y).
Axes of the slice: x: 4, y: 4, z: 8 (z_hi: 4, z_lo: 2; z = z_hi * 2 + z_lo), core: 2. Of those that a mesh axis runs over, the one named last changes fastest.
Arguments:
- normed_inputs: bfloat16 [24576, 8192], P(('grp', 'fsdp')), may hold values from -6 to 6
- value_cotangent: bfloat16 [24576, 1024], P(('grp', 'fsdp'), 'tp'), may hold values from -0.0390625 to 0.0390625
- value_weight: bfloat16 [8192, 1024], P(('grp', 'fsdp'), 'tp'), may hold values from -0.0625 to 0.0625
- decode_inputs: bfloat16 [512, 4, 8192], P(('grp', 'fsdp'), None, 'tp'), may hold values from -6 to 6
- queries: bfloat16 [512, 4, 8192], P(('grp', 'fsdp'), None, 'tp')
- new_keys: bfloat16 [512, 4, 1024], P(('grp', 'fsdp'), None, 'tp'), may hold values from -6 to 6
- cache_keys: bfloat16 [512, 128, 1024], P(('grp', 'fsdp'), None, 'tp')
- cache_values: bfloat16 [512, 128, 1024], P(('grp', 'fsdp'), None, 'tp'), may hold values from -6 to 6
- lengths: int32 [512], P(('grp', 'fsdp')), may hold values from 2 to 128, as said below
Outputs:
- gradient: float32 [8192, 1024], P(('grp', 'fsdp'), 'tp')
- new_values: bfloat16 [512, 4, 1024], P(('grp', 'fsdp'), None, 'tp')
- attended: bfloat16 [512, 4, 8192], P(('grp', 'fsdp'), None, 'tp')
The draws below stay inside these ranges and needn't reach their ends.
Inputs may be any that keep to these rules, and one draw needn't show every extreme that they name: `lengths`: at least 2 and at most 128; some row has exactly 128.
All inputs are finite; a program needn't handle non-finite values.
Results may differ from the reference program's by a relative error of at most 0.0052.
Values may be sent and summed in bfloat16 or wider, within the bound.
No kernel may reach another device: no remote copies, remote signals or barrier semaphores. Data moves between devices by JAX's collectives and lax.ppermute only.
A program may use at most 64 MiB of HBM per device.

```python
import math
import jax
import jax.numpy as jnp
from jax import lax

D = 8192
QH = 64
KVH = 8
HD = 128
CTX = 128
STEPS = 4
TOKENS = 24576
ROWS = 512


def draw_cache_keys(key, part):
    key = jax.random.fold_in(key, 3)
    drawn = jax.random.normal(key, (ROWS, CTX, KVH * HD), jnp.float32)
    return drawn.astype(jnp.bfloat16)


def draw_queries(key, part):
    key = jax.random.fold_in(key, 7)
    drawn = jax.random.normal(key, (ROWS, STEPS, QH * HD), jnp.float32)
    return drawn.astype(jnp.bfloat16)


def draw_lengths(key, part):
    key = jax.random.fold_in(key, 13)
    drawn = jax.random.randint(key, (ROWS,), 2, CTX + 1)
    return drawn.at[0].set(CTX).astype(jnp.int32)


def shard_levels(own_key, extent, cuts, least, high):
    def one(dim, parts):
        draws = jax.random.uniform(jax.random.fold_in(jax.random.fold_in(own_key, 6), dim), (parts,), jnp.float32, least / len(cuts), high / len(cuts))
        return jnp.repeat(jnp.exp(draws), extent[dim] // parts).reshape((-1,) + (1,) * (len(extent) - dim - 1))

    loudness = one(*cuts[0])
    for cut in cuts[1:]:
        loudness = loudness * one(*cut)
    return loudness


def scatter_about(rng, shape, spread, reach, pieces=(), held_as=jnp.bfloat16):
    factor_of = shard_levels(rng, shape, pieces, -0.22, 0.18) if pieces else 1.0
    array = jax.random.normal(rng, shape, jnp.float32) * spread * factor_of
    return jnp.minimum(jnp.maximum(array, -reach), reach).astype(held_as)


def setup_inputs(seed: int = 0) -> dict:
    key_of = jax.random.split(jax.random.key(seed), 10)
    return {
        "normed_inputs": scatter_about(key_of[0], (TOKENS, D), 1.0, 6.0, ((0, 32),)),
        "value_cotangent": scatter_about(key_of[1], (TOKENS, KVH * HD), TOKENS ** -0.5, 0.0390625, ((0, 32), (1, 8))),
        "value_weight": scatter_about(key_of[2], (D, KVH * HD), D ** -0.5, 0.0625, ((0, 32), (1, 8))),
        "decode_inputs": scatter_about(key_of[3], (ROWS, STEPS, D), 1.0, 6.0, ((0, 32), (2, 8))),
        "queries": draw_queries(jax.random.fold_in(key_of[9], 71), 0),
        "new_keys": scatter_about(key_of[5], (ROWS, STEPS, KVH * HD), 1.0, 6.0, ((0, 32), (2, 8))),
        "cache_keys": draw_cache_keys(jax.random.fold_in(key_of[9], 71), 0),
        "cache_values": scatter_about(key_of[7], (ROWS, CTX, KVH * HD), 1.0, 6.0, ((0, 32), (2, 8))),
        "lengths": draw_lengths(jax.random.fold_in(key_of[9], 71), 0),
    }


def attend_rows(queries, new_keys, new_values, cache_keys, cache_values, lengths):
    row_count = queries.shape[0]
    step_count = queries.shape[1]
    slot_count = cache_keys.shape[1]
    group_count = cache_keys.shape[2] // HD
    per_group = QH // KVH
    factor = 1.0 / math.sqrt(HD)
    query_heads = queries.reshape(row_count, step_count, group_count, per_group, HD).astype(jnp.float32)
    cached_keys = cache_keys.reshape(row_count, slot_count, group_count, HD).astype(jnp.float32)
    cached_values = cache_values.reshape(row_count, slot_count, group_count, HD).astype(jnp.float32)
    fresh_keys = new_keys.reshape(row_count, step_count, group_count, HD).astype(jnp.float32)
    fresh_values = new_values.reshape(row_count, step_count, group_count, HD).astype(jnp.float32)
    cache_scores = jnp.einsum('rsgqd,rpgd->rsgqp', query_heads, cached_keys) * factor
    live_slots = jnp.arange(slot_count, dtype=jnp.int32)[None, :] < lengths[:, None]
    cache_scores = jnp.where(live_slots[:, None, None, None, :], cache_scores, -1e+30)
    fresh_scores = jnp.einsum('rsgqd,rugd->rsgqu', query_heads, fresh_keys) * factor
    causal = jnp.arange(step_count, dtype=jnp.int32)[None, :] <= jnp.arange(step_count, dtype=jnp.int32)[:, None]
    fresh_scores = jnp.where(causal[None, :, None, None, :], fresh_scores, -1e+30)
    highest = jnp.maximum(lax.optimization_barrier(jnp.max(cache_scores, axis=-1)), lax.optimization_barrier(jnp.max(fresh_scores, axis=-1)))
    cache_exp = jnp.exp(cache_scores - highest[..., None])
    fresh_exp = jnp.exp(fresh_scores - highest[..., None])
    denominator = lax.optimization_barrier(jnp.sum(cache_exp, axis=-1)) + lax.optimization_barrier(jnp.sum(fresh_exp, axis=-1))
    cache_weights = (cache_exp / denominator[..., None]).astype(jnp.bfloat16)
    fresh_weights = (fresh_exp / denominator[..., None]).astype(jnp.bfloat16)
    mixed = jnp.einsum('rsgqp,rpgd->rsgqd', cache_weights.astype(jnp.float32), cached_values)
    mixed = mixed + jnp.einsum('rsgqu,rugd->rsgqd', fresh_weights.astype(jnp.float32), fresh_values)
    return mixed.astype(jnp.bfloat16).reshape(row_count, step_count, group_count * per_group * HD)

def reference(normed_inputs, value_cotangent, value_weight, decode_inputs, queries, new_keys, cache_keys, cache_values, lengths):
    gradient = lax.dot_general(normed_inputs, value_cotangent, (((0,), (0,)), ((), ())), preferred_element_type=jnp.float32)
    step_size = 0.4 / math.sqrt(D)
    updated = (value_weight.astype(jnp.float32) - step_size * gradient).astype(jnp.bfloat16)
    row_count = decode_inputs.shape[0]
    step_count = decode_inputs.shape[1]
    flat_inputs = decode_inputs.reshape(row_count * step_count, D)
    new_values = jnp.dot(flat_inputs, updated, preferred_element_type=jnp.float32).astype(jnp.bfloat16)
    new_values = new_values.reshape(row_count, step_count, updated.shape[1])
    attended = attend_rows(queries, new_keys, new_values, cache_keys, cache_values, lengths)
    return (gradient, new_values, attended)
```

```python
import math

import jax
import jax.numpy as jnp
import numpy as np
from jax import lax
from jax.experimental import pallas as pl
from jax.experimental.pallas import tpu as pltpu
from jax.sharding import Mesh, PartitionSpec as P

D = 8192
QH = 64
KVH = 8
HD = 128
SIZES = {"c": 2, "zh": 4, "x": 4, "zl": 2, "y": 4}
NAMES = tuple(SIZES)
STEP = 0.4 / math.sqrt(D)
MIB = 1 << 20


def shift(value, axis, by):
    n = SIZES[axis]
    return lax.ppermute(value, axis, [(i, (i + by) % n) for i in range(n)])


def swap_axes(value):
    names = ("c", "zh", "zl", "y")
    sizes = [SIZES[n] for n in names]
    pairs = []
    for c, zh, zl, y in np.ndindex(*sizes):
        source = int(np.ravel_multi_index((c, zh, zl, y), sizes))
        target = int(np.ravel_multi_index((zl, y, c, zh), sizes))
        pairs.append((source, target))
    return lax.ppermute(value, names, pairs)


def partial_kernel(place, x_ref, v_ref, out_ref):
    product = lax.dot_general(
        v_ref[...], x_ref[...], (((0,), (0,)), ((), ())), preferred_element_type=jnp.float32
    )
    for block in range(4):
        rows = product[:, block * 256 : (block + 1) * 256].T
        out_ref[lax.rem(block + 4 - place[2], 4), 0] = rows.astype(out_ref.dtype)


def partial_gradient(place, normed_inputs, value_cotangent):
    tokens = normed_inputs.shape[0]
    return pl.pallas_call(
        partial_kernel,
        grid_spec=pltpu.PrefetchScalarGridSpec(
            num_scalar_prefetch=1,
            grid=(4,),
            in_specs=[
                pl.BlockSpec(
                    (tokens, 1024), lambda e, place: (0, place[0] * 4 + lax.rem(place[1] + e, 4))
                ),
                pl.BlockSpec((tokens, HD), lambda e, place: (0, 0)),
            ],
            out_specs=pl.BlockSpec((4, 1, 256, HD), lambda e, place: (0, e, 0, 0)),
        ),
        out_shape=jax.ShapeDtypeStruct((4, 4, 256, HD), jnp.bfloat16),
        compiler_params=pltpu.CompilerParams(vmem_limit_bytes=56 * MIB),
        cost_estimate=pl.CostEstimate(
            flops=2 * tokens * 4096 * HD, bytes_accessed=tokens * 4096 * 2, transcendentals=0
        ),
    )(place, normed_inputs, value_cotangent)


def project_kernel(place, d0, d1, d2, d3, u0, u1, u2, u3, out_ref, rows):
    core, x, low, y = place[0], place[1], place[2], place[3]
    for d, u in enumerate((u0, u1, u2, u3)):
        rows[pl.ds(pl.multiple_of(lax.rem(x + d, 4) * 256, 256), 256), :] = u[...]
    for d, piece in enumerate((d0, d1, d2, d3)):
        for j in range(2):
            product = jnp.dot(piece[j], rows[...], preferred_element_type=jnp.float32)
            other = lax.rem(low + j + core, 2)
            out_ref[other, lax.rem(y + d, 4)] = product.astype(out_ref.dtype)


def project(place, pieces, updated):
    whole = pl.BlockSpec(memory_space=pltpu.VMEM)
    return pl.pallas_call(
        project_kernel,
        in_specs=[pl.BlockSpec(memory_space=pltpu.SMEM)] + [whole] * 8,
        out_specs=whole,
        out_shape=jax.ShapeDtypeStruct((2, 4, 64, HD), jnp.bfloat16),
        scratch_shapes=[pltpu.VMEM((1024, HD), jnp.bfloat16)],
        compiler_params=pltpu.CompilerParams(vmem_limit_bytes=16 * MIB),
        cost_estimate=pl.CostEstimate(
            flops=2 * 512 * 1024 * HD, bytes_accessed=3 * MIB // 2, transcendentals=0
        ),
    )(place, *pieces, *updated)


def attend_cache(queries, new_keys, cache_keys, cache_values, lengths):
    row_count, step_count = queries.shape[0], queries.shape[1]
    slot_count = cache_keys.shape[1]
    factor = 1.0 / math.sqrt(HD)
    heads = queries.reshape(row_count, step_count, QH // KVH, HD)
    cache_scores = (
        jnp.einsum("rsqd,rpd->rsqp", heads, cache_keys, preferred_element_type=jnp.float32) * factor
    )
    live = jnp.arange(slot_count, dtype=jnp.int32)[None, :] < lengths[:, None]
    cache_scores = jnp.where(live[:, None, None, :], cache_scores, -1e30)
    fresh_scores = (
        jnp.einsum("rsqd,rud->rsqu", heads, new_keys, preferred_element_type=jnp.float32) * factor
    )
    steps = jnp.arange(step_count, dtype=jnp.int32)
    causal = steps[None, :] <= steps[:, None]
    fresh_scores = jnp.where(causal[None, :, None, :], fresh_scores, -1e30)
    highest = jnp.maximum(jnp.max(cache_scores, axis=-1), jnp.max(fresh_scores, axis=-1))
    cache_exp = jnp.exp(cache_scores - highest[..., None])
    fresh_exp = jnp.exp(fresh_scores - highest[..., None])
    denominator = jnp.sum(cache_exp, axis=-1) + jnp.sum(fresh_exp, axis=-1)
    cache_weights = (cache_exp / denominator[..., None]).astype(jnp.bfloat16)
    fresh_weights = (fresh_exp / denominator[..., None]).astype(jnp.bfloat16)
    mixed = jnp.einsum(
        "rsqp,rpd->rsqd", cache_weights, cache_values, preferred_element_type=jnp.float32
    )
    return mixed, fresh_weights


def shards(
    normed_inputs,
    value_cotangent,
    value_weight,
    decode_inputs,
    queries,
    new_keys,
    cache_keys,
    cache_values,
    lengths,
):
    core, high, x, low, y = (lax.axis_index(n) for n in NAMES)
    row_count, step_count = decode_inputs.shape[0], decode_inputs.shape[1]
    f32 = jnp.float32

    swapped = swap_axes(decode_inputs.reshape(row_count * step_count, -1))

    theirs = partial_gradient(jnp.stack([1 - core, high, x]), normed_inputs, value_cotangent)
    received = shift(theirs, "c", 1)
    mine = partial_gradient(jnp.stack([core, high, x]), normed_inputs, value_cotangent)

    both = jnp.stack([swapped, shift(swapped, "zl", 1)])

    sums = [mine[d].astype(f32) + received[d].astype(f32) for d in range(4)]
    along_x = sums[0]
    for d in (2, 1, 3):
        along_x += shift(sums[d].astype(jnp.bfloat16), "x", d).astype(f32)

    pieces = [both] + [shift(both, "y", -d) for d in (1, 2, 3)]

    gradient = along_x[0]
    for e in (2, 1, 3):
        gradient += shift(along_x[e].astype(jnp.bfloat16), "zh", e).astype(f32)
    updated = (value_weight.astype(f32) - STEP * gradient).astype(jnp.bfloat16)

    gathered = [updated] + [shift(updated, "x", -d) for d in (1, 2, 3)]
    partial = project(jnp.stack([core, x, low, y]), pieces, gathered)
    pair = partial[0].astype(f32) + shift(partial[1], "c", 1).astype(f32)
    exchanged = lax.all_to_all(pair.astype(jnp.bfloat16), "zh", 0, 0, tiled=True)
    new_values = jnp.sum(exchanged.astype(f32), axis=0).astype(jnp.bfloat16)
    new_values = new_values.reshape(row_count, step_count, HD)

    mixed, fresh_weights = attend_cache(queries, new_keys, cache_keys, cache_values, lengths)
    mixed = mixed + jnp.einsum(
        "rsqu,rud->rsqd", fresh_weights, new_values, preferred_element_type=f32
    )
    attended = mixed.astype(jnp.bfloat16).reshape(row_count, step_count, -1)
    return (gradient, new_values, attended)


def solution(mesh):
    inner = Mesh(mesh.devices.reshape(tuple(SIZES.values())), NAMES)
    rows, columns = ("c", "zh", "x"), ("zl", "y")
    return jax.shard_map(
        shards,
        mesh=inner,
        in_specs=(
            P(rows, None),
            P(rows, columns),
            P(rows, columns),
            P(rows, None, columns),
            P(rows, None, columns),
            P(rows, None, columns),
            P(rows, None, columns),
            P(rows, None, columns),
            P(rows),
        ),
        out_specs=(
            P(rows, columns),
            P(rows, None, columns),
            P(rows, None, columns),
        ),
        check_vma=False,
    )
```

```python
import math

import jax
import jax.numpy as jnp
import numpy as np
from jax import lax
from jax.experimental import pallas as pl
from jax.experimental.pallas import tpu as pltpu
from jax.sharding import Mesh, PartitionSpec as P

D = 8192
HEADS = 8
HD = 128
SIZES = {"c": 2, "zh": 4, "x": 4, "zl": 2, "y": 4}
NAMES = tuple(SIZES)
STEP = 0.4 / math.sqrt(D)
MIB = 1 << 20
F32 = jnp.float32
BF16 = jnp.bfloat16
VMEM = pl.BlockSpec(memory_space=pltpu.VMEM)
SMEM = pl.BlockSpec(memory_space=pltpu.SMEM)
HBM = pl.BlockSpec(memory_space=pltpu.HBM)


def shift(value, axis, by):
    n = SIZES[axis]
    return lax.ppermute(value, axis, [(i, (i + by) % n) for i in range(n)])


def swap_high(value):
    pairs = [(zh * 4 + y, y * 4 + zh) for zh in range(4) for y in range(4)]
    return lax.ppermute(value, ("zh", "y"), pairs)


def after(value, *others):
    return lax.optimization_barrier((value, *others))[0]


def partial_kernel(own, place, x_hbm, v_ref, out_ref, chunks, sems):
    half = place[0] if own else 1 - place[0]
    copies = []
    for e in range(4):
        column = (half * 4 + lax.rem(place[1] + e, 4)) * 1024
        copy = pltpu.make_async_copy(
            x_hbm.at[:, pl.ds(pl.multiple_of(column, 1024), 1024)], chunks.at[e], sems.at[e]
        )
        copy.start()
        copies.append(copy)
    for e in range(4):
        copies[e].wait()
        product = lax.dot_general(
            v_ref[...], chunks[e], (((0,), (0,)), ((), ())), preferred_element_type=F32
        )
        for block in range(4):
            rows = product[:, block * 256 : (block + 1) * 256].T
            out_ref[lax.rem(block + 4 - place[2], 4), e] = rows.astype(out_ref.dtype)


def partial_gradient(own, place, normed_inputs, value_cotangent):
    tokens = normed_inputs.shape[0]

    def kernel(*refs):
        partial_kernel(own, *refs)

    return pl.pallas_call(
        kernel,
        in_specs=[SMEM, HBM, VMEM],
        out_specs=VMEM,
        out_shape=jax.ShapeDtypeStruct((4, 4, 256, HD), BF16),
        scratch_shapes=[pltpu.VMEM((4, tokens, 1024), BF16), pltpu.SemaphoreType.DMA((4,))],
        compiler_params=pltpu.CompilerParams(vmem_limit_bytes=24 * MIB),
        cost_estimate=pl.CostEstimate(
            flops=2 * tokens * 4096 * HD, bytes_accessed=tokens * 4096 * 2, transcendentals=0
        ),
    )(place, normed_inputs, value_cotangent)


def attend_kernel(lengths, queries, new_keys, cache_keys, cache_values, mixed_ref, weights_ref):
    rows = cache_keys.shape[0]
    slots = cache_keys.shape[1]
    steps = queries.shape[0] // rows
    every = HEADS * queries.shape[0]
    factor = 1.0 / math.sqrt(HD)
    heads = jnp.concatenate([queries[:, q * HD : (q + 1) * HD] for q in range(HEADS)], axis=0)
    place = lax.broadcasted_iota(jnp.int32, (every, slots), 0) % (rows * steps)
    lane = lax.broadcasted_iota(jnp.int32, (every, slots), 1)
    row = place // steps
    contract = (((1,), (1,)), ((), ()))
    scores = jnp.full((every, slots), -1e30, F32)
    for r in range(rows):
        product = lax.dot_general(heads, cache_keys[r], contract, preferred_element_type=F32)
        scores = jnp.where((row == r) & (lane < lengths[r]), product * factor, scores)
    fresh = lax.dot_general(heads, new_keys[...], contract, preferred_element_type=F32) * factor
    from_place, to_place = place[:, : rows * steps], lane[:, : rows * steps]
    visible = (from_place // steps == to_place // steps) & (to_place <= from_place)
    fresh = jnp.where(visible, fresh, -1e30)
    highest = jnp.maximum(
        jnp.max(scores, axis=1, keepdims=True), jnp.max(fresh, axis=1, keepdims=True)
    )
    cache_exp = jnp.exp(scores - highest)
    fresh_exp = jnp.exp(fresh - highest)
    total = jnp.sum(cache_exp, axis=1, keepdims=True) + jnp.sum(fresh_exp, axis=1, keepdims=True)
    cache_weights = (cache_exp / total).astype(BF16)
    weights_ref[...] = (fresh_exp / total).astype(BF16)
    mixed = jnp.zeros((every, HD), F32)
    for r in range(rows):
        product = jnp.dot(cache_weights, cache_values[r], preferred_element_type=F32)
        mixed = jnp.where(row == r, product, mixed)
    mixed_ref[...] = mixed


def attend_cache(lengths, queries, new_keys, cache_keys, cache_values):
    places = queries.shape[0]
    return pl.pallas_call(
        attend_kernel,
        in_specs=[SMEM] + [VMEM] * 4,
        out_specs=[VMEM, VMEM],
        out_shape=[
            jax.ShapeDtypeStruct((HEADS * places, HD), F32),
            jax.ShapeDtypeStruct((HEADS * places, places), BF16),
        ],
        compiler_params=pltpu.CompilerParams(vmem_limit_bytes=16 * MIB),
        cost_estimate=pl.CostEstimate(
            flops=2 * 16 * 512 * 256 * HD, bytes_accessed=2 * MIB, transcendentals=512 * 192
        ),
    )(lengths, queries, new_keys, cache_keys, cache_values)


def project_kernel(place, own, d0, d1, d2, d3, u0, u1, u2, u3, start, out_ref, rows):
    x, y = place[2], place[3]
    for d, u in enumerate((u0, u1, u2, u3)):
        rows[pl.ds(pl.multiple_of(lax.rem(x + d, 4) * 256, 256), 256), :] = u[...]
    for d, piece in enumerate((d0, d1, d2, d3)):
        zh = lax.rem(y + d, 4)
        product = jnp.dot(piece[own], rows[...], preferred_element_type=F32)
        if start is not None:
            product += start[zh]
        out_ref[zh] = product.astype(out_ref.dtype)


def project(place, pieces, updated, start=None):
    first = start is None

    def kernel(place, *refs):
        core, low = place[0], place[4]
        own = jnp.where(core == low, 0, 1) if first else jnp.where(core == low, 1, 0)
        if first:
            refs = refs[:8] + (None,) + refs[8:]
        project_kernel(place, own, *refs)

    return pl.pallas_call(
        kernel,
        in_specs=[SMEM] + [VMEM] * (8 if first else 9),
        out_specs=VMEM,
        out_shape=jax.ShapeDtypeStruct((4, 64, HD), F32 if first else BF16),
        scratch_shapes=[pltpu.VMEM((1024, HD), BF16)],
        compiler_params=pltpu.CompilerParams(vmem_limit_bytes=16 * MIB),
        cost_estimate=pl.CostEstimate(
            flops=2 * 256 * 1024 * HD, bytes_accessed=3 * MIB // 4, transcendentals=0
        ),
    )(place, *pieces, *updated, *(() if first else (start,)))


def finish_kernel(parts, mixed, weights, values_ref, attended_ref):
    steps = values_ref.shape[1]
    total = parts[0].astype(F32)
    for i in range(1, 4):
        total += parts[i].astype(F32)
    values = total.astype(BF16)
    for r in range(values_ref.shape[0]):
        values_ref[r] = values[r * steps : (r + 1) * steps]
    places = values.shape[0]
    for q in range(HEADS):
        span = slice(q * places, (q + 1) * places)
        head = mixed[span] + jnp.dot(weights[span], values, preferred_element_type=F32)
        head = head.astype(BF16)
        for r in range(values_ref.shape[0]):
            attended_ref[r, :, q * HD : (q + 1) * HD] = head[r * steps : (r + 1) * steps]


def finish(parts, mixed, weights, rows, steps):
    return pl.pallas_call(
        finish_kernel,
        in_specs=[VMEM] * 3,
        out_specs=[VMEM, VMEM],
        out_shape=[
            jax.ShapeDtypeStruct((rows, steps, HD), BF16),
            jax.ShapeDtypeStruct((rows, steps, HEADS * HD), BF16),
        ],
        compiler_params=pltpu.CompilerParams(vmem_limit_bytes=16 * MIB),
    )(parts, mixed, weights)


def shards(
    normed_inputs,
    value_cotangent,
    value_weight,
    decode_inputs,
    queries,
    new_keys,
    cache_keys,
    cache_values,
    lengths,
):
    core, high, x, low, y = (lax.axis_index(n) for n in NAMES)
    row_count, step_count = decode_inputs.shape[0], decode_inputs.shape[1]
    places = row_count * step_count
    place = jnp.stack([core, high, x, y, low])

    theirs = partial_gradient(False, place, normed_inputs, value_cotangent)
    received = shift(theirs, "c", 1)

    own_inputs = after(decode_inputs.reshape(places, -1), theirs)
    both = jnp.stack([own_inputs, shift(own_inputs, "zl", 1)])

    mine = partial_gradient(True, place, normed_inputs, value_cotangent)
    sums = [mine[d].astype(F32) + received[d].astype(F32) for d in range(4)]
    sent = [s.astype(BF16) for s in sums]

    both = after(both, sent[1])
    both = swap_high(both)

    along_x = sums[0]
    for d in (2, 1, 3):
        along_x += shift(sent[d], "x", d).astype(F32)

    attended_cache, fresh_weights = attend_cache(
        lengths,
        after(queries.reshape(places, -1), sent[1]),
        new_keys.reshape(places, HD),
        cache_keys,
        cache_values,
    )

    gradient = along_x[0]
    sent = [along_x[e].astype(BF16) for e in range(4)]
    both = after(both, sent[1])
    pieces = [both] + [shift(both, "y", -d) for d in (1, 2, 3)]
    for e in (2, 1, 3):
        gradient += shift(sent[e], "zh", e).astype(F32)
    updated = (value_weight.astype(F32) - STEP * gradient).astype(BF16)

    gathered = [updated] + [shift(updated, "x", -d) for d in (1, 2, 3)]
    other = shift(jnp.stack(gathered), "c", 1)
    partial = project(place, pieces, gathered)
    partial = project(place, pieces, [other[d] for d in range(4)], partial)
    exchanged = lax.all_to_all(partial, "zh", 0, 0, tiled=True)
    new_values, attended = finish(
        exchanged, attended_cache, fresh_weights, row_count, step_count
    )
    return (gradient, new_values, attended)


def solution(mesh):
    inner = Mesh(mesh.devices.reshape(tuple(SIZES.values())), NAMES)
    rows, columns = ("c", "zh", "x"), ("zl", "y")
    return jax.shard_map(
        shards,
        mesh=inner,
        in_specs=(
            P(rows, None),
            P(rows, columns),
            P(rows, columns),
            P(rows, None, columns),
            P(rows, None, columns),
            P(rows, None, columns),
            P(rows, None, columns),
            P(rows, None, columns),
            P(rows),
        ),
        out_specs=(
            P(rows, columns),
            P(rows, None, columns),
            P(rows, None, columns),
        ),
        check_vma=False,
    )
```

```python
import math

import jax
import jax.numpy as jnp
import numpy as np
from jax import lax
from jax.experimental import pallas as pl
from jax.experimental.pallas import tpu as pltpu
from jax.sharding import Mesh, PartitionSpec as P

D = 8192
HEADS = 8
HD = 128
SIZES = {"c": 2, "zh": 4, "x": 4, "zl": 2, "y": 4}
NAMES = tuple(SIZES)
STEP = 0.4 / math.sqrt(D)
MIB = 1 << 20
F32 = jnp.float32
BF16 = jnp.bfloat16
VMEM = pl.BlockSpec(memory_space=pltpu.VMEM)
SMEM = pl.BlockSpec(memory_space=pltpu.SMEM)
HBM = pl.BlockSpec(memory_space=pltpu.HBM)


def shift(value, axis, by):
    n = SIZES[axis]
    return lax.ppermute(value, axis, [(i, (i + by) % n) for i in range(n)])


def swap_high(value):
    pairs = [(zh * 4 + y, y * 4 + zh) for zh in range(4) for y in range(4)]
    return lax.ppermute(value, ("zh", "y"), pairs)


def after(value, *others):
    return lax.optimization_barrier((value, *others))[0]


def partial_kernel(place, x_hbm, v_hbm, theirs_ref, mine_ref, chunks, v_ref, sems):
    core, high, x = place[0], place[1], place[2]
    order = [(1 - core, theirs_ref, e) for e in range(4)] + [(core, mine_ref, e) for e in range(4)]
    copies = [pltpu.make_async_copy(v_hbm, v_ref, sems.at[8])]
    copies[0].start()
    for i, (half, _, e) in enumerate(order):
        column = (half * 4 + lax.rem(high + e, 4)) * 1024
        copies.append(
            pltpu.make_async_copy(
                x_hbm.at[:, pl.ds(pl.multiple_of(column, 1024), 1024)], chunks.at[i], sems.at[i]
            )
        )
        copies[-1].start()
    copies[0].wait()
    for i, (_, out_ref, e) in enumerate(order):
        copies[i + 1].wait()
        product = lax.dot_general(
            v_ref[...], chunks[i], (((0,), (0,)), ((), ())), preferred_element_type=F32
        )
        for block in range(4):
            rows = product[:, block * 256 : (block + 1) * 256].T
            out_ref[lax.rem(block + 4 - x, 4), e] = rows.astype(out_ref.dtype)


def partial_gradient(place, normed_inputs, value_cotangent):
    tokens = normed_inputs.shape[0]
    return pl.pallas_call(
        partial_kernel,
        in_specs=[SMEM, HBM, HBM],
        out_specs=[VMEM, VMEM],
        out_shape=[jax.ShapeDtypeStruct((4, 4, 256, HD), BF16)] * 2,
        scratch_shapes=[
            pltpu.VMEM((8, tokens, 1024), BF16),
            pltpu.VMEM((tokens, HD), BF16),
            pltpu.SemaphoreType.DMA((9,)),
        ],
        compiler_params=pltpu.CompilerParams(vmem_limit_bytes=48 * MIB),
        cost_estimate=pl.CostEstimate(
            flops=2 * tokens * D * HD, bytes_accessed=tokens * D * 2, transcendentals=0
        ),
    )(place, normed_inputs, value_cotangent)


def small_call(kernel, outs, *args):
    return pl.pallas_call(
        kernel,
        in_specs=[VMEM] * len(args),
        out_specs=[VMEM] * len(outs),
        out_shape=[jax.ShapeDtypeStruct(shape, dtype) for shape, dtype in outs],
        compiler_params=pltpu.CompilerParams(vmem_limit_bytes=16 * MIB),
        cost_estimate=pl.CostEstimate(flops=MIB, bytes_accessed=2 * MIB, transcendentals=0),
    )(*args)


def core_sum_kernel(mine, received, o0, o1, o2, o3):
    for d, out in enumerate((o0, o1, o2, o3)):
        out[...] = (mine[d].astype(F32) + received[d].astype(F32)).astype(out.dtype)


def x_sum_kernel(own, r1, r2, r3, o0, o1, o2, o3):
    for e, out in enumerate((o0, o1, o2, o3)):
        total = own[e] + r1[e].astype(F32) + r2[e].astype(F32) + r3[e].astype(F32)
        out[...] = total.astype(out.dtype)


def update_kernel(weight, own, r1, r2, r3, gradient, updated):
    total = own[...] + r1[...].astype(F32) + r2[...].astype(F32) + r3[...].astype(F32)
    gradient[...] = total
    updated[...] = (weight[...].astype(F32) - STEP * total).astype(BF16)


def attend_kernel(lengths, queries, new_keys, cache_keys, cache_values, mixed_ref, weights_ref):
    rows = cache_keys.shape[0]
    slots = cache_keys.shape[1]
    steps = queries.shape[0] // rows
    every = HEADS * queries.shape[0]
    factor = 1.0 / math.sqrt(HD)
    heads = jnp.concatenate([queries[:, q * HD : (q + 1) * HD] for q in range(HEADS)], axis=0)
    place = lax.broadcasted_iota(jnp.int32, (every, slots), 0) % (rows * steps)
    lane = lax.broadcasted_iota(jnp.int32, (every, slots), 1)
    row = place // steps
    contract = (((1,), (1,)), ((), ()))
    scores = jnp.full((every, slots), -1e30, F32)
    for r in range(rows):
        product = lax.dot_general(heads, cache_keys[r], contract, preferred_element_type=F32)
        scores = jnp.where((row == r) & (lane < lengths[r]), product * factor, scores)
    fresh = lax.dot_general(heads, new_keys[...], contract, preferred_element_type=F32) * factor
    from_place, to_place = place[:, : rows * steps], lane[:, : rows * steps]
    visible = (from_place // steps == to_place // steps) & (to_place <= from_place)
    fresh = jnp.where(visible, fresh, -1e30)
    highest = jnp.maximum(
        jnp.max(scores, axis=1, keepdims=True), jnp.max(fresh, axis=1, keepdims=True)
    )
    cache_exp = jnp.exp(scores - highest)
    fresh_exp = jnp.exp(fresh - highest)
    total = jnp.sum(cache_exp, axis=1, keepdims=True) + jnp.sum(fresh_exp, axis=1, keepdims=True)
    cache_weights = (cache_exp / total).astype(BF16)
    weights_ref[...] = (fresh_exp / total).astype(BF16)
    mixed = jnp.zeros((every, HD), F32)
    for r in range(rows):
        product = jnp.dot(cache_weights, cache_values[r], preferred_element_type=F32)
        mixed = jnp.where(row == r, product, mixed)
    mixed_ref[...] = mixed


def attend_cache(lengths, queries, new_keys, cache_keys, cache_values):
    places = queries.shape[0]
    return pl.pallas_call(
        attend_kernel,
        in_specs=[SMEM] + [VMEM] * 4,
        out_specs=[VMEM, VMEM],
        out_shape=[
            jax.ShapeDtypeStruct((HEADS * places, HD), F32),
            jax.ShapeDtypeStruct((HEADS * places, places), BF16),
        ],
        compiler_params=pltpu.CompilerParams(vmem_limit_bytes=16 * MIB),
        cost_estimate=pl.CostEstimate(
            flops=2 * 16 * 512 * 256 * HD, bytes_accessed=2 * MIB, transcendentals=512 * 192
        ),
    )(lengths, queries, new_keys, cache_keys, cache_values)


def project_kernel(first, place, d0, d1, d2, d3, u, *refs):
    core, x, y, low = place[0], place[2], place[3], place[4]
    start, out_ref, rows = (None, *refs) if first else refs
    own = jnp.where(core == low, 0, 1) if first else jnp.where(core == low, 1, 0)
    for d in range(4):
        rows[pl.ds(pl.multiple_of(lax.rem(x + d, 4) * 256, 256), 256), :] = u[d]
    for d, piece in enumerate((d0, d1, d2, d3)):
        zh = lax.rem(y + d, 4)
        product = jnp.dot(piece[own], rows[...], preferred_element_type=F32)
        if start is not None:
            product += start[zh]
        out_ref[zh] = product.astype(out_ref.dtype)


def project(place, pieces, updated, start=None):
    first = start is None

    def kernel(*refs):
        project_kernel(first, *refs)

    args = (*pieces, updated) if first else (*pieces, updated, start)
    return pl.pallas_call(
        kernel,
        in_specs=[SMEM] + [VMEM] * len(args),
        out_specs=VMEM,
        out_shape=jax.ShapeDtypeStruct((4, 64, HD), F32 if first else BF16),
        scratch_shapes=[pltpu.VMEM((1024, HD), BF16)],
        compiler_params=pltpu.CompilerParams(vmem_limit_bytes=16 * MIB),
        cost_estimate=pl.CostEstimate(
            flops=2 * 256 * 1024 * HD, bytes_accessed=3 * MIB // 4, transcendentals=0
        ),
    )(place, *args)


def finish_kernel(parts, mixed, weights, values_ref, attended_ref):
    steps = values_ref.shape[1]
    total = parts[0].astype(F32)
    for i in range(1, 4):
        total += parts[i].astype(F32)
    values = total.astype(BF16)
    for r in range(values_ref.shape[0]):
        values_ref[r] = values[r * steps : (r + 1) * steps]
    places = values.shape[0]
    for q in range(HEADS):
        span = slice(q * places, (q + 1) * places)
        head = mixed[span] + jnp.dot(weights[span], values, preferred_element_type=F32)
        head = head.astype(BF16)
        for r in range(values_ref.shape[0]):
            attended_ref[r, :, q * HD : (q + 1) * HD] = head[r * steps : (r + 1) * steps]


def finish(parts, mixed, weights, rows, steps):
    return pl.pallas_call(
        finish_kernel,
        in_specs=[VMEM] * 3,
        out_specs=[VMEM, VMEM],
        out_shape=[
            jax.ShapeDtypeStruct((rows, steps, HD), BF16),
            jax.ShapeDtypeStruct((rows, steps, HEADS * HD), BF16),
        ],
        compiler_params=pltpu.CompilerParams(vmem_limit_bytes=16 * MIB),
    )(parts, mixed, weights)


def shards(
    normed_inputs,
    value_cotangent,
    value_weight,
    decode_inputs,
    queries,
    new_keys,
    cache_keys,
    cache_values,
    lengths,
):
    core, high, x, low, y = (lax.axis_index(n) for n in NAMES)
    row_count, step_count = decode_inputs.shape[0], decode_inputs.shape[1]
    places = row_count * step_count
    place = jnp.stack([core, high, x, y, low])

    theirs, mine = partial_gradient(place, normed_inputs, value_cotangent)
    received = shift(theirs, "c", 1)

    swapped = swap_high(after(decode_inputs.reshape(places, -1), theirs))

    rows = (4, 256, HD)
    own, *sent = small_call(
        core_sum_kernel, [(rows, F32)] + [(rows, BF16)] * 3, mine, received
    )
    along_x = [shift(sent[d - 1], "x", d) for d in (2, 1, 3)]

    swapped = after(swapped, own)
    both = jnp.stack([swapped, shift(swapped, "zl", 1)])
    attended_cache, fresh_weights = attend_cache(
        lengths,
        after(queries.reshape(places, -1), own),
        new_keys.reshape(places, HD),
        cache_keys,
        cache_values,
    )

    own, *along_x, both, attended_cache, fresh_weights = lax.optimization_barrier(
        (own, *along_x, both, attended_cache, fresh_weights)
    )
    rows = (256, HD)
    own, *sent = small_call(
        x_sum_kernel, [(rows, F32)] + [(rows, BF16)] * 3, own, *along_x
    )
    along_z = [shift(sent[e - 1], "zh", e) for e in (2, 1, 3)]
    both = after(both, own)
    pieces = [both] + [shift(both, "y", -d) for d in (1, 2, 3)]
    own, *along_z, pieces[1], pieces[3] = lax.optimization_barrier(
        (own, *along_z, pieces[1], pieces[3])
    )
    gradient, updated = small_call(
        update_kernel, [(rows, F32), (rows, BF16)], value_weight, own, *along_z
    )

    gathered = jnp.stack([updated] + [shift(updated, "x", -d) for d in (1, 2, 3)])
    other = shift(gathered, "c", 1)
    partial = project(place, pieces, gathered)
    partial = project(place, pieces, other, partial)
    exchanged = lax.all_to_all(partial, "zh", 0, 0, tiled=True)
    new_values, attended = finish(
        exchanged, attended_cache, fresh_weights, row_count, step_count
    )
    return (gradient, new_values, attended)


def solution(mesh):
    inner = Mesh(mesh.devices.reshape(tuple(SIZES.values())), NAMES)
    rows, columns = ("c", "zh", "x"), ("zl", "y")
    return jax.shard_map(
        shards,
        mesh=inner,
        in_specs=(
            P(rows, None),
            P(rows, columns),
            P(rows, columns),
            P(rows, None, columns),
            P(rows, None, columns),
            P(rows, None, columns),
            P(rows, None, columns),
            P(rows, None, columns),
            P(rows),
        ),
        out_specs=(
            P(rows, columns),
            P(rows, None, columns),
            P(rows, None, columns),
        ),
        check_vma=False,
    )
```

```python
import math

import jax
import jax.numpy as jnp
import numpy as np
from jax import lax
from jax.experimental import pallas as pl
from jax.experimental.pallas import tpu as pltpu
from jax.sharding import Mesh, PartitionSpec as P

D = 8192
HEADS = 8
HD = 128
SIZES = {"c": 2, "zh": 4, "x": 4, "zl": 2, "y": 4}
NAMES = tuple(SIZES)
STEP = 0.4 / math.sqrt(D)
MIB = 1 << 20
F32 = jnp.float32
BF16 = jnp.bfloat16
VMEM = pl.BlockSpec(memory_space=pltpu.VMEM)
SMEM = pl.BlockSpec(memory_space=pltpu.SMEM)
HBM = pl.BlockSpec(memory_space=pltpu.HBM)


def shift(value, axis, by):
    n = SIZES[axis]
    return lax.ppermute(value, axis, [(i, (i + by) % n) for i in range(n)])


def swap_high(value):
    pairs = [(zh * 4 + y, y * 4 + zh) for zh in range(4) for y in range(4)]
    return lax.ppermute(value, ("zh", "y"), pairs)


def after(value, *others):
    return lax.optimization_barrier((value, *others))[0]


def partial_kernel(place, x_hbm, v_hbm, theirs_ref, mine_ref, chunks, v_ref, sems):
    core, high, x = place[0], place[1], place[2]
    order = [(1 - core, theirs_ref, e) for e in range(4)] + [(core, mine_ref, e) for e in range(4)]
    copies = [pltpu.make_async_copy(v_hbm, v_ref, sems.at[8])]
    copies[0].start()
    for i, (half, _, e) in enumerate(order):
        column = (half * 4 + lax.rem(high + e, 4)) * 1024
        copies.append(
            pltpu.make_async_copy(
                x_hbm.at[:, pl.ds(pl.multiple_of(column, 1024), 1024)], chunks.at[i], sems.at[i]
            )
        )
        copies[-1].start()
    copies[0].wait()
    for i, (_, out_ref, e) in enumerate(order):
        copies[i + 1].wait()
        product = lax.dot_general(
            v_ref[...], chunks[i], (((0,), (0,)), ((), ())), preferred_element_type=F32
        )
        for block in range(4):
            rows = product[:, block * 256 : (block + 1) * 256].T
            out_ref[lax.rem(block + 4 - x, 4), e] = rows.astype(out_ref.dtype)


def partial_gradient(place, normed_inputs, value_cotangent):
    tokens = normed_inputs.shape[0]
    return pl.pallas_call(
        partial_kernel,
        in_specs=[SMEM, HBM, HBM],
        out_specs=[VMEM, VMEM],
        out_shape=[jax.ShapeDtypeStruct((4, 4, 256, HD), BF16)] * 2,
        scratch_shapes=[
            pltpu.VMEM((8, tokens, 1024), BF16),
            pltpu.VMEM((tokens, HD), BF16),
            pltpu.SemaphoreType.DMA((9,)),
        ],
        compiler_params=pltpu.CompilerParams(vmem_limit_bytes=48 * MIB),
        cost_estimate=pl.CostEstimate(
            flops=2 * tokens * D * HD, bytes_accessed=tokens * D * 2, transcendentals=0
        ),
    )(place, normed_inputs, value_cotangent)


def small_call(kernel, outs, *args):
    return pl.pallas_call(
        kernel,
        in_specs=[VMEM] * len(args),
        out_specs=[VMEM] * len(outs),
        out_shape=[jax.ShapeDtypeStruct(shape, dtype) for shape, dtype in outs],
        compiler_params=pltpu.CompilerParams(vmem_limit_bytes=16 * MIB),
        cost_estimate=pl.CostEstimate(flops=MIB, bytes_accessed=2 * MIB, transcendentals=0),
    )(*args)


def core_sum_kernel(mine, received, o0, o1, o2, o3):
    o0[...] = mine[0].astype(F32) + received[0].astype(F32)
    for d, out in ((1, o1), (2, o2), (3, o3)):
        out[...] = mine[d] + received[d]


def join_kernel(first, second, out):
    rows, steps = first.shape[0], first.shape[1]
    for i, ref in enumerate((first, second)):
        for r in range(rows):
            out[i, r * steps : (r + 1) * steps] = ref[r]


def x_sum_kernel(own, r1, r2, r3, o0, o1, o2, o3):
    for e, out in enumerate((o0, o1, o2, o3)):
        total = own[e] + r1[e].astype(F32) + r2[e].astype(F32) + r3[e].astype(F32)
        out[...] = total.astype(out.dtype)


def total_of(own, r1, r2, r3):
    return own[...] + r1[...].astype(F32) + r2[...].astype(F32) + r3[...].astype(F32)


def update_kernel(weight, own, r1, r2, r3, updated):
    total = total_of(own, r1, r2, r3)
    updated[...] = (weight[...].astype(F32) - STEP * total).astype(BF16)


def gradient_kernel(own, r1, r2, r3, gradient):
    gradient[...] = total_of(own, r1, r2, r3)


def attend_kernel(lengths, queries, new_keys, cache_keys, cache_values, mixed_ref, weights_ref):
    rows = cache_keys.shape[0]
    slots = cache_keys.shape[1]
    steps = queries.shape[0] // rows
    every = HEADS * queries.shape[0]
    factor = 1.0 / math.sqrt(HD)
    heads = jnp.concatenate([queries[:, q * HD : (q + 1) * HD] for q in range(HEADS)], axis=0)
    place = lax.broadcasted_iota(jnp.int32, (every, slots), 0) % (rows * steps)
    lane = lax.broadcasted_iota(jnp.int32, (every, slots), 1)
    row = place // steps
    contract = (((1,), (1,)), ((), ()))
    scores = jnp.full((every, slots), -1e30, F32)
    for r in range(rows):
        product = lax.dot_general(heads, cache_keys[r], contract, preferred_element_type=F32)
        scores = jnp.where((row == r) & (lane < lengths[r]), product * factor, scores)
    fresh = lax.dot_general(heads, new_keys[...], contract, preferred_element_type=F32) * factor
    from_place, to_place = place[:, : rows * steps], lane[:, : rows * steps]
    visible = (from_place // steps == to_place // steps) & (to_place <= from_place)
    fresh = jnp.where(visible, fresh, -1e30)
    highest = jnp.maximum(
        jnp.max(scores, axis=1, keepdims=True), jnp.max(fresh, axis=1, keepdims=True)
    )
    cache_exp = jnp.exp(scores - highest)
    fresh_exp = jnp.exp(fresh - highest)
    total = jnp.sum(cache_exp, axis=1, keepdims=True) + jnp.sum(fresh_exp, axis=1, keepdims=True)
    cache_weights = (cache_exp / total).astype(BF16)
    weights_ref[...] = (fresh_exp / total).astype(BF16)
    mixed = jnp.zeros((every, HD), F32)
    for r in range(rows):
        product = jnp.dot(cache_weights, cache_values[r], preferred_element_type=F32)
        mixed = jnp.where(row == r, product, mixed)
    mixed_ref[...] = mixed


def attend_cache(lengths, queries, new_keys, cache_keys, cache_values):
    places = queries.shape[0]
    return pl.pallas_call(
        attend_kernel,
        in_specs=[SMEM] + [VMEM] * 4,
        out_specs=[VMEM, VMEM],
        out_shape=[
            jax.ShapeDtypeStruct((HEADS * places, HD), F32),
            jax.ShapeDtypeStruct((HEADS * places, places), BF16),
        ],
        compiler_params=pltpu.CompilerParams(vmem_limit_bytes=16 * MIB),
        cost_estimate=pl.CostEstimate(
            flops=2 * 16 * 512 * 256 * HD, bytes_accessed=2 * MIB, transcendentals=512 * 192
        ),
    )(lengths, queries, new_keys, cache_keys, cache_values)


def project_kernel(first, place, d0, d1, d2, d3, u, *refs):
    core, x, y, low = place[0], place[2], place[3], place[4]
    start, out_ref, rows = (None, *refs) if first else refs
    own = jnp.where(core == low, 0, 1) if first else jnp.where(core == low, 1, 0)
    for d in range(4):
        rows[pl.ds(pl.multiple_of(lax.rem(x + d, 4) * 256, 256), 256), :] = u[d]
    for d, piece in enumerate((d0, d1, d2, d3)):
        zh = lax.rem(y + d, 4)
        product = jnp.dot(piece[own], rows[...], preferred_element_type=F32)
        if start is not None:
            product += start[zh]
        out_ref[zh] = product.astype(out_ref.dtype)


def project(place, pieces, updated, start=None):
    first = start is None

    def kernel(*refs):
        project_kernel(first, *refs)

    args = (*pieces, updated) if first else (*pieces, updated, start)
    return pl.pallas_call(
        kernel,
        in_specs=[SMEM] + [VMEM] * len(args),
        out_specs=VMEM,
        out_shape=jax.ShapeDtypeStruct((4, 64, HD), F32 if first else BF16),
        scratch_shapes=[pltpu.VMEM((1024, HD), BF16)],
        compiler_params=pltpu.CompilerParams(vmem_limit_bytes=16 * MIB),
        cost_estimate=pl.CostEstimate(
            flops=2 * 256 * 1024 * HD, bytes_accessed=3 * MIB // 4, transcendentals=0
        ),
    )(place, *args)


def finish_kernel(parts, mixed, weights, values_ref, attended_ref):
    steps = values_ref.shape[1]
    total = parts[0].astype(F32)
    for i in range(1, 4):
        total += parts[i].astype(F32)
    values = total.astype(BF16)
    for r in range(values_ref.shape[0]):
        values_ref[r] = values[r * steps : (r + 1) * steps]
    places = values.shape[0]
    for q in range(HEADS):
        span = slice(q * places, (q + 1) * places)
        head = mixed[span] + jnp.dot(weights[span], values, preferred_element_type=F32)
        head = head.astype(BF16)
        for r in range(values_ref.shape[0]):
            attended_ref[r, :, q * HD : (q + 1) * HD] = head[r * steps : (r + 1) * steps]


def finish(parts, mixed, weights, rows, steps):
    return pl.pallas_call(
        finish_kernel,
        in_specs=[VMEM] * 3,
        out_specs=[VMEM, VMEM],
        out_shape=[
            jax.ShapeDtypeStruct((rows, steps, HD), BF16),
            jax.ShapeDtypeStruct((rows, steps, HEADS * HD), BF16),
        ],
        compiler_params=pltpu.CompilerParams(vmem_limit_bytes=16 * MIB),
    )(parts, mixed, weights)


def shards(
    normed_inputs,
    value_cotangent,
    value_weight,
    decode_inputs,
    queries,
    new_keys,
    cache_keys,
    cache_values,
    lengths,
):
    core, high, x, low, y = (lax.axis_index(n) for n in NAMES)
    row_count, step_count = decode_inputs.shape[0], decode_inputs.shape[1]
    places = row_count * step_count
    place = jnp.stack([core, high, x, y, low])

    swapped = swap_high(decode_inputs)
    theirs, mine = partial_gradient(place, normed_inputs, value_cotangent)
    theirs, mine, swapped = lax.optimization_barrier((theirs, mine, swapped))
    received = shift(theirs, "c", 1)

    rows = (4, 256, HD)
    own, *sent = small_call(
        core_sum_kernel, [(rows, F32)] + [(rows, BF16)] * 3, mine, received
    )
    along_x = [shift(sent[d - 1], "x", d) for d in (2, 1, 3)]

    swapped = after(swapped, own)
    second = shift(swapped, "zl", 1)
    attended_cache, fresh_weights = attend_cache(
        lengths,
        after(queries.reshape(places, -1), own),
        new_keys.reshape(places, HD),
        cache_keys,
        cache_values,
    )
    swapped = after(swapped, attended_cache)
    (both,) = small_call(join_kernel, [((2, places, D // 8), BF16)], swapped, second)
    pieces = [both] + [shift(both, "y", -d) for d in (1, 2, 3)]

    own, *along_x, attended_cache, fresh_weights = lax.optimization_barrier(
        (own, *along_x, attended_cache, fresh_weights)
    )
    rows = (256, HD)
    own, *sent = small_call(
        x_sum_kernel, [(rows, F32)] + [(rows, BF16)] * 3, own, *along_x
    )
    along_z = [shift(sent[e - 1], "zh", e) for e in (2, 1, 3)]
    own, *along_z, pieces = lax.optimization_barrier((own, *along_z, pieces))
    (updated,) = small_call(update_kernel, [(rows, BF16)], value_weight, own, *along_z)
    own = after(own, updated)
    (gradient,) = small_call(gradient_kernel, [(rows, F32)], own, *along_z)

    gathered = jnp.stack([updated] + [shift(updated, "x", -d) for d in (1, 2, 3)])
    other = shift(gathered, "c", 1)
    partial = project(place, pieces, gathered)
    partial = project(place, pieces, other, partial)
    exchanged = lax.all_to_all(partial, "zh", 0, 0, tiled=True)
    new_values, attended = finish(
        exchanged, attended_cache, fresh_weights, row_count, step_count
    )
    return (gradient, new_values, attended)


def solution(mesh):
    inner = Mesh(mesh.devices.reshape(tuple(SIZES.values())), NAMES)
    rows, columns = ("c", "zh", "x"), ("zl", "y")
    return jax.shard_map(
        shards,
        mesh=inner,
        in_specs=(
            P(rows, None),
            P(rows, columns),
            P(rows, columns),
            P(rows, None, columns),
            P(rows, None, columns),
            P(rows, None, columns),
            P(rows, None, columns),
            P(rows, None, columns),
            P(rows),
        ),
        out_specs=(
            P(rows, columns),
            P(rows, None, columns),
            P(rows, None, columns),
        ),
        check_vma=False,
    )
```

```python
import math

import jax
import jax.numpy as jnp
import numpy as np
from jax import lax
from jax.experimental import pallas as pl
from jax.experimental.pallas import tpu as pltpu
from jax.sharding import Mesh, PartitionSpec as P

D = 8192
HEADS = 8
HD = 128
SIZES = {"c": 2, "zh": 4, "x": 4, "zl": 2, "y": 4}
NAMES = tuple(SIZES)
STEP = 0.4 / math.sqrt(D)
MIB = 1 << 20
F32 = jnp.float32
BF16 = jnp.bfloat16
VMEM = pl.BlockSpec(memory_space=pltpu.VMEM)
SMEM = pl.BlockSpec(memory_space=pltpu.SMEM)
HBM = pl.BlockSpec(memory_space=pltpu.HBM)


def shift(value, axis, by):
    n = SIZES[axis]
    return lax.ppermute(value, axis, [(i, (i + by) % n) for i in range(n)])


def swap_places(value):
    names = ("c", "zh", "zl", "y")
    sizes = [SIZES[n] for n in names]
    pairs = []
    for c, zh, zl, y in np.ndindex(*sizes):
        source = int(np.ravel_multi_index((c, zh, zl, y), sizes))
        target = int(np.ravel_multi_index((zl, y, c, (zh + y) % 4), sizes))
        pairs.append((source, target))
    return lax.ppermute(value, names, pairs)


def after(value, *others):
    return lax.optimization_barrier((value, *others))[0]


def partial_kernel(place, x_hbm, v_hbm, theirs_ref, mine_ref, chunks, v_ref, sems):
    core, high, x = place[0], place[1], place[2]
    order = [(1 - core, theirs_ref, e) for e in range(4)] + [(core, mine_ref, e) for e in range(4)]
    copies = [pltpu.make_async_copy(v_hbm, v_ref, sems.at[8])]
    copies[0].start()
    for i, (half, _, e) in enumerate(order):
        column = (half * 4 + lax.rem(high + e, 4)) * 1024
        copies.append(
            pltpu.make_async_copy(
                x_hbm.at[:, pl.ds(pl.multiple_of(column, 1024), 1024)], chunks.at[i], sems.at[i]
            )
        )
        copies[-1].start()
    copies[0].wait()
    for i, (_, out_ref, e) in enumerate(order):
        copies[i + 1].wait()
        product = lax.dot_general(
            v_ref[...], chunks[i], (((0,), (0,)), ((), ())), preferred_element_type=F32
        )
        for block in range(4):
            rows = product[:, block * 256 : (block + 1) * 256].T
            out_ref[lax.rem(block + 4 - x, 4), e] = rows.astype(out_ref.dtype)


def partial_gradient(place, normed_inputs, value_cotangent):
    tokens = normed_inputs.shape[0]
    return pl.pallas_call(
        partial_kernel,
        in_specs=[SMEM, HBM, HBM],
        out_specs=[VMEM, VMEM],
        out_shape=[jax.ShapeDtypeStruct((4, 4, 256, HD), BF16)] * 2,
        scratch_shapes=[
            pltpu.VMEM((8, tokens, 1024), BF16),
            pltpu.VMEM((tokens, HD), BF16),
            pltpu.SemaphoreType.DMA((9,)),
        ],
        compiler_params=pltpu.CompilerParams(vmem_limit_bytes=48 * MIB),
        cost_estimate=pl.CostEstimate(
            flops=2 * tokens * D * HD, bytes_accessed=tokens * D * 2, transcendentals=0
        ),
    )(place, normed_inputs, value_cotangent)


def small_call(kernel, outs, *args):
    return pl.pallas_call(
        kernel,
        in_specs=[VMEM] * len(args),
        out_specs=[VMEM] * len(outs),
        out_shape=[jax.ShapeDtypeStruct(shape, dtype) for shape, dtype in outs],
        compiler_params=pltpu.CompilerParams(vmem_limit_bytes=16 * MIB),
        cost_estimate=pl.CostEstimate(flops=MIB, bytes_accessed=2 * MIB, transcendentals=0),
    )(*args)


def core_sum_kernel(mine, received, o0, o1, o2, o3):
    o0[...] = mine[0].astype(F32) + received[0].astype(F32)
    for d, out in ((1, o1), (2, o2), (3, o3)):
        out[...] = mine[d] + received[d]


def join_kernel(first, second, out):
    rows, steps = first.shape[0], first.shape[1]
    for i, ref in enumerate((first, second)):
        for r in range(rows):
            out[i, r * steps : (r + 1) * steps] = ref[r]


def x_sum_kernel(own, r1, r2, r3, o0, o1, o2, o3):
    for e, out in enumerate((o0, o1, o2, o3)):
        total = own[e] + r1[e].astype(F32) + r2[e].astype(F32) + r3[e].astype(F32)
        out[...] = total.astype(out.dtype)


def total_of(own, r1, r2, r3):
    return own[...] + r1[...].astype(F32) + r2[...].astype(F32) + r3[...].astype(F32)


def update_kernel(weight, own, r1, r2, r3, updated):
    total = total_of(own, r1, r2, r3)
    updated[...] = (weight[...].astype(F32) - STEP * total).astype(BF16)


def gradient_kernel(own, r1, r2, r3, gradient):
    gradient[...] = total_of(own, r1, r2, r3)


def attend_kernel(lengths, queries, new_keys, cache_keys, cache_values, mixed_ref, weights_ref):
    rows = cache_keys.shape[0]
    slots = cache_keys.shape[1]
    steps = queries.shape[0] // rows
    every = HEADS * queries.shape[0]
    factor = 1.0 / math.sqrt(HD)
    heads = jnp.concatenate([queries[:, q * HD : (q + 1) * HD] for q in range(HEADS)], axis=0)
    place = lax.broadcasted_iota(jnp.int32, (every, slots), 0) % (rows * steps)
    lane = lax.broadcasted_iota(jnp.int32, (every, slots), 1)
    row = place // steps
    contract = (((1,), (1,)), ((), ()))
    scores = jnp.full((every, slots), -1e30, F32)
    for r in range(rows):
        product = lax.dot_general(heads, cache_keys[r], contract, preferred_element_type=F32)
        scores = jnp.where((row == r) & (lane < lengths[r]), product * factor, scores)
    fresh = lax.dot_general(heads, new_keys[...], contract, preferred_element_type=F32) * factor
    from_place, to_place = place[:, : rows * steps], lane[:, : rows * steps]
    visible = (from_place // steps == to_place // steps) & (to_place <= from_place)
    fresh = jnp.where(visible, fresh, -1e30)
    highest = jnp.maximum(
        jnp.max(scores, axis=1, keepdims=True), jnp.max(fresh, axis=1, keepdims=True)
    )
    cache_exp = jnp.exp(scores - highest)
    fresh_exp = jnp.exp(fresh - highest)
    total = jnp.sum(cache_exp, axis=1, keepdims=True) + jnp.sum(fresh_exp, axis=1, keepdims=True)
    cache_weights = (cache_exp / total).astype(BF16)
    weights_ref[...] = (fresh_exp / total).astype(BF16)
    mixed = jnp.zeros((every, HD), F32)
    for r in range(rows):
        product = jnp.dot(cache_weights, cache_values[r], preferred_element_type=F32)
        mixed = jnp.where(row == r, product, mixed)
    mixed_ref[...] = mixed


def attend_cache(lengths, queries, new_keys, cache_keys, cache_values):
    places = queries.shape[0]
    return pl.pallas_call(
        attend_kernel,
        in_specs=[SMEM] + [VMEM] * 4,
        out_specs=[VMEM, VMEM],
        out_shape=[
            jax.ShapeDtypeStruct((HEADS * places, HD), F32),
            jax.ShapeDtypeStruct((HEADS * places, places), BF16),
        ],
        compiler_params=pltpu.CompilerParams(vmem_limit_bytes=16 * MIB),
        cost_estimate=pl.CostEstimate(
            flops=MIB, bytes_accessed=MIB // 4, transcendentals=0
        ),
    )(lengths, queries, new_keys, cache_keys, cache_values)


def project_kernel(place, d0, d1, d2, d3, u0, u1, u2, u3, out_ref, rows):
    high, x, y, low = place[1], place[2], place[3], place[4]
    for d, u in enumerate((u0, u1, u2, u3)):
        rows[pl.ds(pl.multiple_of(lax.rem(x + d, 4) * 256, 256), 256), :] = u[...]
    for d, piece in enumerate((d0, d1, d2, d3)):
        zh = lax.rem(y + d + 4 - high, 4)
        for j in range(2):
            core = low if j == 0 else 1 - low
            product = jnp.dot(piece[j], rows[...], preferred_element_type=F32)
            out_ref[core * 4 + zh] = product.astype(out_ref.dtype)


def project(place, pieces, updated):
    places = pieces[0].shape[1]
    return pl.pallas_call(
        project_kernel,
        in_specs=[SMEM] + [VMEM] * 8,
        out_specs=VMEM,
        out_shape=jax.ShapeDtypeStruct((8, places, HD), BF16),
        scratch_shapes=[pltpu.VMEM((1024, HD), BF16)],
        compiler_params=pltpu.CompilerParams(vmem_limit_bytes=16 * MIB),
        cost_estimate=pl.CostEstimate(
            flops=2 * 512 * 1024 * HD, bytes_accessed=3 * MIB // 2, transcendentals=0
        ),
    )(place, *pieces, *updated)


def finish_kernel(parts, mixed, weights, values_ref, attended_ref):
    steps = values_ref.shape[1]
    total = parts[0].astype(F32)
    for i in range(1, 8):
        total += parts[i].astype(F32)
    values = total.astype(BF16)
    for r in range(values_ref.shape[0]):
        values_ref[r] = values[r * steps : (r + 1) * steps]
    places = values.shape[0]
    for q in range(HEADS):
        span = slice(q * places, (q + 1) * places)
        head = mixed[span] + jnp.dot(weights[span], values, preferred_element_type=F32)
        head = head.astype(BF16)
        for r in range(values_ref.shape[0]):
            attended_ref[r, :, q * HD : (q + 1) * HD] = head[r * steps : (r + 1) * steps]


def finish(parts, mixed, weights, rows, steps):
    return pl.pallas_call(
        finish_kernel,
        in_specs=[VMEM] * 3,
        out_specs=[VMEM, VMEM],
        out_shape=[
            jax.ShapeDtypeStruct((rows, steps, HD), BF16),
            jax.ShapeDtypeStruct((rows, steps, HEADS * HD), BF16),
        ],
        compiler_params=pltpu.CompilerParams(vmem_limit_bytes=16 * MIB),
    )(parts, mixed, weights)


def shards(
    normed_inputs,
    value_cotangent,
    value_weight,
    decode_inputs,
    queries,
    new_keys,
    cache_keys,
    cache_values,
    lengths,
):
    core, high, x, low, y = (lax.axis_index(n) for n in NAMES)
    row_count, step_count = decode_inputs.shape[0], decode_inputs.shape[1]
    places = row_count * step_count
    place = jnp.stack([core, high, x, y, low])

    swapped = swap_places(decode_inputs)
    theirs, mine = partial_gradient(place, normed_inputs, value_cotangent)
    theirs, mine, swapped = lax.optimization_barrier((theirs, mine, swapped))
    received = shift(theirs, "c", 1)
    second = shift(swapped, "zl", 1)

    mine, received, swapped = lax.optimization_barrier((mine, received, swapped))
    rows = (4, 256, HD)
    own, *sent = small_call(
        core_sum_kernel, [(rows, F32)] + [(rows, BF16)] * 3, mine, received
    )
    along_x = [shift(sent[d - 1], "x", d) for d in (2, 1, 3)]
    swapped = after(swapped, own)
    (both,) = small_call(join_kernel, [((2, places, D // 8), BF16)], swapped, second)
    pieces = [both] + [shift(both, "y", -d) for d in (1, 3, 2)]
    pieces = [pieces[0], pieces[1], pieces[3], pieces[2]]

    rows = (256, HD)
    own, *sent = small_call(
        x_sum_kernel, [(rows, F32)] + [(rows, BF16)] * 3, own, *along_x
    )
    sent[2], pieces[1] = lax.optimization_barrier((sent[2], pieces[1]))
    along_z = [shift(sent[e - 1], "zh", e) for e in (2, 1, 3)]
    own, *along_z, pieces = lax.optimization_barrier((own, *along_z, pieces))
    (updated,) = small_call(update_kernel, [(rows, BF16)], value_weight, own, *along_z)
    attended_cache, fresh_weights = attend_cache(
        lengths,
        after(queries.reshape(places, -1), updated),
        new_keys.reshape(places, HD),
        cache_keys,
        cache_values,
    )
    own = after(own, updated)
    (gradient,) = small_call(gradient_kernel, [(rows, F32)], own, *along_z)

    gathered = [updated] + [shift(updated, "x", -d) for d in (1, 2, 3)]
    partial = project(place, pieces, gathered)
    exchanged = lax.all_to_all(partial, ("c", "zh"), 0, 0, tiled=True)
    new_values, attended = finish(
        exchanged, attended_cache, fresh_weights, row_count, step_count
    )
    return (gradient, new_values, attended)


def solution(mesh):
    inner = Mesh(mesh.devices.reshape(tuple(SIZES.values())), NAMES)
    rows, columns = ("c", "zh", "x"), ("zl", "y")
    return jax.shard_map(
        shards,
        mesh=inner,
        in_specs=(
            P(rows, None),
            P(rows, columns),
            P(rows, columns),
            P(rows, None, columns),
            P(rows, None, columns),
            P(rows, None, columns),
            P(rows, None, columns),
            P(rows, None, columns),
            P(rows),
        ),
        out_specs=(
            P(rows, columns),
            P(rows, None, columns),
            P(rows, None, columns),
        ),
        check_vma=False,
    )
```

```python
import math

import jax
import jax.numpy as jnp
import numpy as np
from jax import lax
from jax.experimental import pallas as pl
from jax.experimental.pallas import tpu as pltpu
from jax.sharding import Mesh, PartitionSpec as P

D = 8192
HEADS = 8
HD = 128
SIZES = {"c": 2, "zh": 4, "x": 4, "zl": 2, "y": 4}
NAMES = tuple(SIZES)
STEP = 0.4 / math.sqrt(D)
MIB = 1 << 20
F32 = jnp.float32
BF16 = jnp.bfloat16
VMEM = pl.BlockSpec(memory_space=pltpu.VMEM)
SMEM = pl.BlockSpec(memory_space=pltpu.SMEM)
HBM = pl.BlockSpec(memory_space=pltpu.HBM)


def shift(value, axis, by):
    n = SIZES[axis]
    return lax.ppermute(value, axis, [(i, (i + by) % n) for i in range(n)])


def swap_high(value):
    pairs = [(zh * 4 + y, y * 4 + (zh + y) % 4) for zh in range(4) for y in range(4)]
    return lax.ppermute(value, ("zh", "y"), pairs)


def after(value, *others):
    return lax.optimization_barrier((value, *others))[0]


def partial_kernel(place, x_hbm, v_hbm, theirs_ref, mine_ref, chunks, v_ref, sems):
    core, high, x = place[0], place[1], place[2]
    order = [(1 - core, theirs_ref, e) for e in range(4)] + [(core, mine_ref, e) for e in range(4)]
    copies = [pltpu.make_async_copy(v_hbm, v_ref, sems.at[8])]
    copies[0].start()
    for i, (half, _, e) in enumerate(order):
        column = (half * 4 + lax.rem(high + e, 4)) * 1024
        copies.append(
            pltpu.make_async_copy(
                x_hbm.at[:, pl.ds(pl.multiple_of(column, 1024), 1024)], chunks.at[i], sems.at[i]
            )
        )
        copies[-1].start()
    copies[0].wait()
    for i, (_, out_ref, e) in enumerate(order):
        copies[i + 1].wait()
        product = lax.dot_general(
            v_ref[...], chunks[i], (((0,), (0,)), ((), ())), preferred_element_type=F32
        )
        for block in range(4):
            rows = product[:, block * 256 : (block + 1) * 256].T
            out_ref[lax.rem(block + 4 - x, 4), e] = rows.astype(out_ref.dtype)


def partial_gradient(place, normed_inputs, value_cotangent):
    tokens = normed_inputs.shape[0]
    return pl.pallas_call(
        partial_kernel,
        in_specs=[SMEM, HBM, HBM],
        out_specs=[VMEM, VMEM],
        out_shape=[jax.ShapeDtypeStruct((4, 4, 256, HD), BF16)] * 2,
        scratch_shapes=[
            pltpu.VMEM((8, tokens, 1024), BF16),
            pltpu.VMEM((tokens, HD), BF16),
            pltpu.SemaphoreType.DMA((9,)),
        ],
        compiler_params=pltpu.CompilerParams(vmem_limit_bytes=48 * MIB),
        cost_estimate=pl.CostEstimate(
            flops=2 * tokens * D * HD, bytes_accessed=tokens * D * 2, transcendentals=0
        ),
    )(place, normed_inputs, value_cotangent)


def small_call(kernel, outs, *args):
    return pl.pallas_call(
        kernel,
        in_specs=[VMEM] * len(args),
        out_specs=[VMEM] * len(outs),
        out_shape=[jax.ShapeDtypeStruct(shape, dtype) for shape, dtype in outs],
        compiler_params=pltpu.CompilerParams(vmem_limit_bytes=16 * MIB),
        cost_estimate=pl.CostEstimate(flops=MIB, bytes_accessed=2 * MIB, transcendentals=0),
    )(*args)


def core_sum_kernel(mine, received, o0, o1, o2, o3):
    o0[...] = mine[0].astype(F32) + received[0].astype(F32)
    for d, out in ((1, o1), (2, o2), (3, o3)):
        out[...] = mine[d] + received[d]


def join_kernel(first, second, out):
    rows, steps = first.shape[0], first.shape[1]
    for i, ref in enumerate((first, second)):
        for r in range(rows):
            out[i, r * steps : (r + 1) * steps] = ref[r]


def x_sum_kernel(own, r1, r2, r3, o0, o1, o2, o3):
    for e, out in enumerate((o0, o1, o2, o3)):
        total = own[e] + r1[e].astype(F32) + r2[e].astype(F32) + r3[e].astype(F32)
        out[...] = total.astype(out.dtype)


def total_of(own, r1, r2, r3):
    return own[...] + r1[...].astype(F32) + r2[...].astype(F32) + r3[...].astype(F32)


def update_kernel(weight, own, r1, r2, r3, updated):
    total = total_of(own, r1, r2, r3)
    updated[...] = (weight[...].astype(F32) - STEP * total).astype(BF16)


def gradient_kernel(own, r1, r2, r3, gradient):
    gradient[...] = total_of(own, r1, r2, r3)


def attend_kernel(lengths, queries, new_keys, cache_keys, cache_values, mixed_ref, weights_ref):
    rows = cache_keys.shape[0]
    slots = cache_keys.shape[1]
    steps = queries.shape[0] // rows
    every = HEADS * queries.shape[0]
    factor = 1.0 / math.sqrt(HD)
    heads = jnp.concatenate([queries[:, q * HD : (q + 1) * HD] for q in range(HEADS)], axis=0)
    place = lax.broadcasted_iota(jnp.int32, (every, slots), 0) % (rows * steps)
    lane = lax.broadcasted_iota(jnp.int32, (every, slots), 1)
    row = place // steps
    contract = (((1,), (1,)), ((), ()))
    scores = jnp.full((every, slots), -1e30, F32)
    for r in range(rows):
        product = lax.dot_general(heads, cache_keys[r], contract, preferred_element_type=F32)
        scores = jnp.where((row == r) & (lane < lengths[r]), product * factor, scores)
    fresh = lax.dot_general(heads, new_keys[...], contract, preferred_element_type=F32) * factor
    from_place, to_place = place[:, : rows * steps], lane[:, : rows * steps]
    visible = (from_place // steps == to_place // steps) & (to_place <= from_place)
    fresh = jnp.where(visible, fresh, -1e30)
    highest = jnp.maximum(
        jnp.max(scores, axis=1, keepdims=True), jnp.max(fresh, axis=1, keepdims=True)
    )
    cache_exp = jnp.exp(scores - highest)
    fresh_exp = jnp.exp(fresh - highest)
    total = jnp.sum(cache_exp, axis=1, keepdims=True) + jnp.sum(fresh_exp, axis=1, keepdims=True)
    cache_weights = (cache_exp / total).astype(BF16)
    weights_ref[...] = (fresh_exp / total).astype(BF16)
    mixed = jnp.zeros((every, HD), F32)
    for r in range(rows):
        product = jnp.dot(cache_weights, cache_values[r], preferred_element_type=F32)
        mixed = jnp.where(row == r, product, mixed)
    mixed_ref[...] = mixed


def attend_cache(lengths, queries, new_keys, cache_keys, cache_values):
    places = queries.shape[0]
    return pl.pallas_call(
        attend_kernel,
        in_specs=[SMEM] + [VMEM] * 4,
        out_specs=[VMEM, VMEM],
        out_shape=[
            jax.ShapeDtypeStruct((HEADS * places, HD), F32),
            jax.ShapeDtypeStruct((HEADS * places, places), BF16),
        ],
        compiler_params=pltpu.CompilerParams(vmem_limit_bytes=16 * MIB),
        cost_estimate=pl.CostEstimate(
            flops=MIB, bytes_accessed=MIB // 4, transcendentals=0
        ),
    )(lengths, queries, new_keys, cache_keys, cache_values)


def fill_rows(rows, x, updated):
    for d in range(4):
        rows[pl.ds(pl.multiple_of(lax.rem(x + d, 4) * 256, 256), 256), :] = updated[d]


def tokens_of(place, d):
    return lax.rem(place[3] + d + 4 - place[1], 4)


def project_own_kernel(place, d0, d1, d2, u, out_ref, rows):
    own = jnp.where(place[0] == place[4], 0, 1)
    fill_rows(rows, place[2], u)
    for d, piece in enumerate((d0, d1, d2)):
        out_ref[tokens_of(place, d)] = jnp.dot(
            piece[own], rows[...], preferred_element_type=F32
        )


def project_rest_kernel(place, d0, d1, d2, d3, u_own, u_other, start, out_ref, rows, last):
    own = jnp.where(place[0] == place[4], 0, 1)
    fill_rows(last, place[2], u_own)
    fill_rows(rows, place[2], u_other)
    for d, piece in enumerate((d0, d1, d2, d3)):
        zh = tokens_of(place, d)
        product = jnp.dot(piece[1 - own], rows[...], preferred_element_type=F32)
        if d < 3:
            product += start[zh]
        else:
            product += jnp.dot(piece[own], last[...], preferred_element_type=F32)
        out_ref[zh] = product.astype(out_ref.dtype)


def project(kernel, dtype, scratches, place, *args):
    return pl.pallas_call(
        kernel,
        in_specs=[SMEM] + [VMEM] * len(args),
        out_specs=VMEM,
        out_shape=jax.ShapeDtypeStruct((4, 64, HD), dtype),
        scratch_shapes=[pltpu.VMEM((1024, HD), BF16)] * scratches,
        compiler_params=pltpu.CompilerParams(vmem_limit_bytes=16 * MIB),
        cost_estimate=pl.CostEstimate(
            flops=2 * 256 * 1024 * HD, bytes_accessed=3 * MIB // 4, transcendentals=0
        ),
    )(place, *args)


def finish_kernel(parts, mixed, weights, values_ref, attended_ref):
    steps = values_ref.shape[1]
    total = parts[0].astype(F32)
    for i in range(1, 4):
        total += parts[i].astype(F32)
    values = total.astype(BF16)
    for r in range(values_ref.shape[0]):
        values_ref[r] = values[r * steps : (r + 1) * steps]
    places = values.shape[0]
    for q in range(HEADS):
        span = slice(q * places, (q + 1) * places)
        head = mixed[span] + jnp.dot(weights[span], values, preferred_element_type=F32)
        head = head.astype(BF16)
        for r in range(values_ref.shape[0]):
            attended_ref[r, :, q * HD : (q + 1) * HD] = head[r * steps : (r + 1) * steps]


def finish(parts, mixed, weights, rows, steps):
    return pl.pallas_call(
        finish_kernel,
        in_specs=[VMEM] * 3,
        out_specs=[VMEM, VMEM],
        out_shape=[
            jax.ShapeDtypeStruct((rows, steps, HD), BF16),
            jax.ShapeDtypeStruct((rows, steps, HEADS * HD), BF16),
        ],
        compiler_params=pltpu.CompilerParams(vmem_limit_bytes=16 * MIB),
    )(parts, mixed, weights)


def shards(
    normed_inputs,
    value_cotangent,
    value_weight,
    decode_inputs,
    queries,
    new_keys,
    cache_keys,
    cache_values,
    lengths,
):
    core, high, x, low, y = (lax.axis_index(n) for n in NAMES)
    row_count, step_count = decode_inputs.shape[0], decode_inputs.shape[1]
    places = row_count * step_count
    place = jnp.stack([core, high, x, y, low])

    theirs, mine = partial_gradient(place, normed_inputs, value_cotangent)
    received = shift(theirs, "c", 1)
    swapped = swap_high(after(decode_inputs, theirs))

    rows = (4, 256, HD)
    own, *sent = small_call(
        core_sum_kernel, [(rows, F32)] + [(rows, BF16)] * 3, mine, received
    )
    along_x = [shift(sent[d - 1], "x", d) for d in (2, 1, 3)]
    swapped = after(swapped, own)
    (both,) = small_call(
        join_kernel, [((2, places, D // 8), BF16)], swapped, shift(swapped, "zl", 1)
    )
    attended_cache, fresh_weights = attend_cache(
        lengths,
        after(queries.reshape(places, -1), own),
        new_keys.reshape(places, HD),
        cache_keys,
        cache_values,
    )

    own, *along_x, both, attended_cache, fresh_weights = lax.optimization_barrier(
        (own, *along_x, both, attended_cache, fresh_weights)
    )
    rows = (256, HD)
    own, *sent = small_call(
        x_sum_kernel, [(rows, F32)] + [(rows, BF16)] * 3, own, *along_x
    )
    along_z = [shift(sent[e - 1], "zh", e) for e in (2, 1, 3)]
    both = after(both, own)
    from_y2, from_y1, from_y3 = (shift(both, "y", -d) for d in (2, 1, 3))
    own, *along_z, from_y2, from_y1 = lax.optimization_barrier((own, *along_z, from_y2, from_y1))
    (updated,) = small_call(update_kernel, [(rows, BF16)], value_weight, own, *along_z)
    own = after(own, updated)
    (gradient,) = small_call(gradient_kernel, [(rows, F32)], own, *along_z)

    gathered = jnp.stack([updated] + [shift(updated, "x", -d) for d in (1, 2, 3)])
    other = shift(gathered, "c", 1)
    pieces = (both, from_y1, from_y2)
    partial = project(project_own_kernel, F32, 1, place, *pieces, gathered)
    partial = project(
        project_rest_kernel, BF16, 2, place, *pieces, from_y3, gathered, other, partial
    )
    exchanged = lax.all_to_all(partial, "zh", 0, 0, tiled=True)
    new_values, attended = finish(
        exchanged, attended_cache, fresh_weights, row_count, step_count
    )
    return (gradient, new_values, attended)


def solution(mesh):
    inner = Mesh(mesh.devices.reshape(tuple(SIZES.values())), NAMES)
    rows, columns = ("c", "zh", "x"), ("zl", "y")
    return jax.shard_map(
        shards,
        mesh=inner,
        in_specs=(
            P(rows, None),
            P(rows, columns),
            P(rows, columns),
            P(rows, None, columns),
            P(rows, None, columns),
            P(rows, None, columns),
            P(rows, None, columns),
            P(rows, None, columns),
            P(rows),
        ),
        out_specs=(
            P(rows, columns),
            P(rows, None, columns),
            P(rows, None, columns),
        ),
        check_vma=False,
    )
```

```python
import math

import jax
import jax.numpy as jnp
import numpy as np
from jax import lax
from jax.experimental import pallas as pl
from jax.experimental.pallas import tpu as pltpu
from jax.sharding import Mesh, PartitionSpec as P

D = 8192
HEADS = 8
HD = 128
SIZES = {"c": 2, "zh": 4, "x": 4, "zl": 2, "y": 4}
NAMES = tuple(SIZES)
STEP = 0.4 / math.sqrt(D)
MIB = 1 << 20
F32 = jnp.float32
BF16 = jnp.bfloat16
VMEM = pl.BlockSpec(memory_space=pltpu.VMEM)
SMEM = pl.BlockSpec(memory_space=pltpu.SMEM)
HBM = pl.BlockSpec(memory_space=pltpu.HBM)


def shift(value, axis, by):
    n = SIZES[axis]
    return lax.ppermute(value, axis, [(i, (i + by) % n) for i in range(n)])


def swap_high(value):
    pairs = [(zh * 4 + y, y * 4 + (zh + y) % 4) for zh in range(4) for y in range(4)]
    return lax.ppermute(value, ("zh", "y"), pairs)


def after(value, *others):
    return lax.optimization_barrier((value, *others))[0]


def partial_kernel(place, x_hbm, v_hbm, theirs_ref, mine_ref, chunks, v_ref, sems):
    core, high, x = place[0], place[1], place[2]
    order = [(1 - core, theirs_ref, e) for e in range(4)] + [(core, mine_ref, e) for e in range(4)]
    copies = [pltpu.make_async_copy(v_hbm, v_ref, sems.at[8])]
    copies[0].start()
    for i, (half, _, e) in enumerate(order):
        column = (half * 4 + lax.rem(high + e, 4)) * 1024
        copies.append(
            pltpu.make_async_copy(
                x_hbm.at[:, pl.ds(pl.multiple_of(column, 1024), 1024)], chunks.at[i], sems.at[i]
            )
        )
        copies[-1].start()
    copies[0].wait()
    for i, (_, out_ref, e) in enumerate(order):
        copies[i + 1].wait()
        product = lax.dot_general(
            v_ref[...], chunks[i], (((0,), (0,)), ((), ())), preferred_element_type=F32
        )
        for block in range(4):
            rows = product[:, block * 256 : (block + 1) * 256].T
            out_ref[lax.rem(block + 4 - x, 4), e] = rows.astype(out_ref.dtype)


def partial_gradient(place, normed_inputs, value_cotangent):
    tokens = normed_inputs.shape[0]
    normed_inputs = pltpu.with_memory_space_constraint(normed_inputs, pltpu.HBM)
    value_cotangent = pltpu.with_memory_space_constraint(value_cotangent, pltpu.HBM)
    return pl.pallas_call(
        partial_kernel,
        in_specs=[SMEM, HBM, HBM],
        out_specs=[VMEM, VMEM],
        out_shape=[pltpu.VMEM((4, 4, 256, HD), BF16)] * 2,
        scratch_shapes=[
            pltpu.VMEM((8, tokens, 1024), BF16),
            pltpu.VMEM((tokens, HD), BF16),
            pltpu.SemaphoreType.DMA((9,)),
        ],
        compiler_params=pltpu.CompilerParams(vmem_limit_bytes=48 * MIB),
        cost_estimate=pl.CostEstimate(
            flops=2 * tokens * D * HD, bytes_accessed=tokens * D * 2, transcendentals=0
        ),
    )(place, normed_inputs, value_cotangent)


def small_call(kernel, outs, *args, keep=True):
    return pl.pallas_call(
        kernel,
        in_specs=[VMEM] * len(args),
        out_specs=[VMEM] * len(outs),
        out_shape=[
            (pltpu.VMEM if keep else jax.ShapeDtypeStruct)(shape, dtype) for shape, dtype in outs
        ],
        compiler_params=pltpu.CompilerParams(vmem_limit_bytes=16 * MIB),
        cost_estimate=pl.CostEstimate(flops=MIB, bytes_accessed=2 * MIB, transcendentals=0),
    )(*args)


def core_sum_kernel(mine, received, o0, o1, o2, o3):
    o0[...] = mine[0].astype(F32) + received[0].astype(F32)
    for d, out in ((1, o1), (2, o2), (3, o3)):
        out[...] = mine[d] + received[d]


def join_kernel(first, second, out):
    rows, steps = first.shape[0], first.shape[1]
    for i, ref in enumerate((first, second)):
        for r in range(rows):
            out[i, r * steps : (r + 1) * steps] = ref[r]


def x_sum_kernel(own, r1, r2, r3, o0, o1, o2, o3):
    for e, out in enumerate((o0, o1, o2, o3)):
        total = own[e] + r1[e].astype(F32) + r2[e].astype(F32) + r3[e].astype(F32)
        out[...] = total.astype(out.dtype)


def total_of(own, r1, r2, r3):
    return own[...] + r1[...].astype(F32) + r2[...].astype(F32) + r3[...].astype(F32)


def update_kernel(weight, own, r1, r2, r3, updated):
    total = total_of(own, r1, r2, r3)
    updated[...] = (weight[...].astype(F32) - STEP * total).astype(BF16)


def gradient_kernel(own, r1, r2, r3, gradient):
    gradient[...] = total_of(own, r1, r2, r3)


def attend_kernel(lengths, queries, new_keys, cache_keys, cache_values, mixed_ref, weights_ref):
    rows = cache_keys.shape[0]
    slots = cache_keys.shape[1]
    steps = queries.shape[0] // rows
    every = HEADS * queries.shape[0]
    factor = 1.0 / math.sqrt(HD)
    heads = jnp.concatenate([queries[:, q * HD : (q + 1) * HD] for q in range(HEADS)], axis=0)
    place = lax.broadcasted_iota(jnp.int32, (every, slots), 0) % (rows * steps)
    lane = lax.broadcasted_iota(jnp.int32, (every, slots), 1)
    row = place // steps
    contract = (((1,), (1,)), ((), ()))
    scores = jnp.full((every, slots), -1e30, F32)
    for r in range(rows):
        product = lax.dot_general(heads, cache_keys[r], contract, preferred_element_type=F32)
        scores = jnp.where((row == r) & (lane < lengths[r]), product * factor, scores)
    fresh = lax.dot_general(heads, new_keys[...], contract, preferred_element_type=F32) * factor
    from_place, to_place = place[:, : rows * steps], lane[:, : rows * steps]
    visible = (from_place // steps == to_place // steps) & (to_place <= from_place)
    fresh = jnp.where(visible, fresh, -1e30)
    highest = jnp.maximum(
        jnp.max(scores, axis=1, keepdims=True), jnp.max(fresh, axis=1, keepdims=True)
    )
    cache_exp = jnp.exp(scores - highest)
    fresh_exp = jnp.exp(fresh - highest)
    total = jnp.sum(cache_exp, axis=1, keepdims=True) + jnp.sum(fresh_exp, axis=1, keepdims=True)
    cache_weights = (cache_exp / total).astype(BF16)
    weights_ref[...] = (fresh_exp / total).astype(BF16)
    mixed = jnp.zeros((every, HD), F32)
    for r in range(rows):
        product = jnp.dot(cache_weights, cache_values[r], preferred_element_type=F32)
        mixed = jnp.where(row == r, product, mixed)
    mixed_ref[...] = mixed


def attend_cache(lengths, queries, new_keys, cache_keys, cache_values):
    places = queries.shape[0]
    return pl.pallas_call(
        attend_kernel,
        in_specs=[SMEM] + [VMEM] * 4,
        out_specs=[VMEM, VMEM],
        out_shape=[
            jax.ShapeDtypeStruct((HEADS * places, HD), F32),
            jax.ShapeDtypeStruct((HEADS * places, places), BF16),
        ],
        compiler_params=pltpu.CompilerParams(vmem_limit_bytes=16 * MIB),
        cost_estimate=pl.CostEstimate(
            flops=MIB, bytes_accessed=MIB // 4, transcendentals=0
        ),
    )(lengths, queries, new_keys, cache_keys, cache_values)


def fill_rows(rows, x, updated):
    for d in range(4):
        rows[pl.ds(pl.multiple_of(lax.rem(x + d, 4) * 256, 256), 256), :] = updated[d]


def tokens_of(place, d):
    return lax.rem(place[3] + d + 4 - place[1], 4)


def project_own_kernel(place, d0, u, out_ref, rows):
    own = jnp.where(place[0] == place[4], 0, 1)
    fill_rows(rows, place[2], u)
    out_ref[0] = jnp.dot(d0[own], rows[...], preferred_element_type=F32)


def project_rest_kernel(place, d0, d1, d2, d3, u_own, u_other, start, out_ref, rows, last):
    own = jnp.where(place[0] == place[4], 0, 1)
    fill_rows(last, place[2], u_own)
    fill_rows(rows, place[2], u_other)
    pieces = (d0, d1, d2, d3)
    inputs = jnp.concatenate([piece[1 - own] for piece in pieces], axis=0)
    product = jnp.dot(inputs, rows[...], preferred_element_type=F32)
    inputs = jnp.concatenate([piece[own] for piece in pieces[1:]], axis=0)
    more = jnp.dot(inputs, last[...], preferred_element_type=F32)
    for d in range(4):
        rest = start[0] if d == 0 else more[(d - 1) * 64 : d * 64]
        out_ref[tokens_of(place, d)] = (product[d * 64 : (d + 1) * 64] + rest).astype(
            out_ref.dtype
        )


def project(kernel, out_shape, scratches, place, *args):
    return pl.pallas_call(
        kernel,
        in_specs=[SMEM] + [VMEM] * len(args),
        out_specs=VMEM,
        out_shape=out_shape,
        scratch_shapes=[pltpu.VMEM((1024, HD), BF16)] * scratches,
        compiler_params=pltpu.CompilerParams(vmem_limit_bytes=16 * MIB),
        cost_estimate=pl.CostEstimate(
            flops=2 * 256 * 1024 * HD, bytes_accessed=3 * MIB // 4, transcendentals=0
        ),
    )(place, *args)


def finish_kernel(parts, mixed, weights, values_ref, attended_ref):
    steps = values_ref.shape[1]
    total = parts[0].astype(F32)
    for i in range(1, 4):
        total += parts[i].astype(F32)
    values = total.astype(BF16)
    for r in range(values_ref.shape[0]):
        values_ref[r] = values[r * steps : (r + 1) * steps]
    places = values.shape[0]
    for q in range(HEADS):
        span = slice(q * places, (q + 1) * places)
        head = mixed[span] + jnp.dot(weights[span], values, preferred_element_type=F32)
        head = head.astype(BF16)
        for r in range(values_ref.shape[0]):
            attended_ref[r, :, q * HD : (q + 1) * HD] = head[r * steps : (r + 1) * steps]


def finish(parts, mixed, weights, rows, steps):
    return pl.pallas_call(
        finish_kernel,
        in_specs=[VMEM] * 3,
        out_specs=[VMEM, VMEM],
        out_shape=[
            jax.ShapeDtypeStruct((rows, steps, HD), BF16),
            jax.ShapeDtypeStruct((rows, steps, HEADS * HD), BF16),
        ],
        compiler_params=pltpu.CompilerParams(vmem_limit_bytes=16 * MIB),
    )(parts, mixed, weights)


def shards(
    normed_inputs,
    value_cotangent,
    value_weight,
    decode_inputs,
    queries,
    new_keys,
    cache_keys,
    cache_values,
    lengths,
):
    core, high, x, low, y = (lax.axis_index(n) for n in NAMES)
    row_count, step_count = decode_inputs.shape[0], decode_inputs.shape[1]
    places = row_count * step_count
    place = jnp.stack([core, high, x, y, low])

    second = shift(decode_inputs, "zl", 1)
    theirs, mine = partial_gradient(place, normed_inputs, value_cotangent)
    theirs, mine, second = lax.optimization_barrier((theirs, mine, second))
    received = shift(theirs, "c", 1)

    rows = (4, 256, HD)
    own, *sent = small_call(
        core_sum_kernel, [(rows, F32)] + [(rows, BF16)] * 3, mine, received
    )
    along_x = [shift(sent[d - 1], "x", d) for d in (2, 1, 3)]
    (both,) = small_call(
        join_kernel, [((2, places, D // 8), BF16)], after(decode_inputs, own), second
    )
    both = swap_high(both)
    attended_cache, fresh_weights = attend_cache(
        lengths,
        after(queries.reshape(places, -1), own),
        new_keys.reshape(places, HD),
        cache_keys,
        cache_values,
    )

    own, *along_x, attended_cache, fresh_weights = lax.optimization_barrier(
        (own, *along_x, attended_cache, fresh_weights)
    )
    rows = (256, HD)
    own, *sent = small_call(
        x_sum_kernel, [(rows, F32)] + [(rows, BF16)] * 3, own, *along_x
    )
    along_z = [shift(sent[e - 1], "zh", e) for e in (2, 1, 3)]
    from_y2, from_y1, from_y3 = (shift(both, "y", -d) for d in (2, 1, 3))
    (updated,) = small_call(update_kernel, [(rows, BF16)], value_weight, own, *along_z)
    own = after(own, updated)
    (gradient,) = small_call(gradient_kernel, [(rows, F32)], own, *along_z, keep=False)

    gathered = jnp.stack([updated] + [shift(updated, "x", -d) for d in (1, 2, 3)])
    other = shift(gathered, "c", 1)
    partial = project(
        project_own_kernel, pltpu.VMEM((1, places, HD), F32), 1, place, both, gathered
    )
    partial = project(
        project_rest_kernel,
        jax.ShapeDtypeStruct((4, places, HD), BF16),
        2,
        place,
        both,
        from_y1,
        from_y2,
        from_y3,
        gathered,
        other,
        partial,
    )
    exchanged = lax.all_to_all(partial, "zh", 0, 0, tiled=True)
    new_values, attended = finish(
        exchanged, attended_cache, fresh_weights, row_count, step_count
    )
    return (gradient, new_values, attended)


def solution(mesh):
    inner = Mesh(mesh.devices.reshape(tuple(SIZES.values())), NAMES)
    rows, columns = ("c", "zh", "x"), ("zl", "y")
    return jax.shard_map(
        shards,
        mesh=inner,
        in_specs=(
            P(rows, None),
            P(rows, columns),
            P(rows, columns),
            P(rows, None, columns),
            P(rows, None, columns),
            P(rows, None, columns),
            P(rows, None, columns),
            P(rows, None, columns),
            P(rows),
        ),
        out_specs=(
            P(rows, columns),
            P(rows, None, columns),
            P(rows, None, columns),
        ),
        check_vma=False,
    )
```

```python
import math

import jax
import jax.numpy as jnp
import numpy as np
from jax import lax
from jax.experimental import pallas as pl
from jax.experimental.pallas import tpu as pltpu
from jax.sharding import Mesh, PartitionSpec as P

D = 8192
HEADS = 8
HD = 128
SIZES = {"c": 2, "zh": 4, "x": 4, "zl": 2, "y": 4}
NAMES = tuple(SIZES)
STEP = 0.4 / math.sqrt(D)
MIB = 1 << 20
F32 = jnp.float32
BF16 = jnp.bfloat16
VMEM = pl.BlockSpec(memory_space=pltpu.VMEM)
SMEM = pl.BlockSpec(memory_space=pltpu.SMEM)
HBM = pl.BlockSpec(memory_space=pltpu.HBM)


def shift(value, axis, by):
    n = SIZES[axis]
    return lax.ppermute(value, axis, [(i, (i + by) % n) for i in range(n)])


def exchange(value, axis, bit):
    return lax.ppermute(value, axis, [(i, i ^ bit) for i in range(SIZES[axis])])


def swap_high(value):
    pairs = [(zh * 4 + y, y * 4 + (zh + y) % 4) for zh in range(4) for y in range(4)]
    return lax.ppermute(value, ("zh", "y"), pairs)


def after(value, *others):
    return lax.optimization_barrier((value, *others))[0]


def partial_kernel(place, x_hbm, v_hbm, theirs_ref, mine_ref, chunks, v_ref, sems):
    core, high, x = place[0], place[1], place[2]
    order = [(1 - core, theirs_ref, e) for e in range(4)] + [(core, mine_ref, e) for e in range(4)]
    copies = [pltpu.make_async_copy(v_hbm, v_ref, sems.at[8])]
    copies[0].start()
    for i, (half, _, e) in enumerate(order):
        column = (half * 4 + lax.rem(high + e, 4)) * 1024
        copies.append(
            pltpu.make_async_copy(
                x_hbm.at[:, pl.ds(pl.multiple_of(column, 1024), 1024)], chunks.at[i], sems.at[i]
            )
        )
        copies[-1].start()
    copies[0].wait()
    for i, (_, out_ref, e) in enumerate(order):
        copies[i + 1].wait()
        product = lax.dot_general(
            v_ref[...], chunks[i], (((0,), (0,)), ((), ())), preferred_element_type=F32
        )
        for block in range(4):
            rows = product[:, block * 256 : (block + 1) * 256].T
            out_ref[lax.rem(block + 4 - x, 4), e] = rows.astype(out_ref.dtype)


def partial_gradient(place, normed_inputs, value_cotangent):
    tokens = normed_inputs.shape[0]
    normed_inputs = pltpu.with_memory_space_constraint(normed_inputs, pltpu.HBM)
    value_cotangent = pltpu.with_memory_space_constraint(value_cotangent, pltpu.HBM)
    return pl.pallas_call(
        partial_kernel,
        in_specs=[SMEM, HBM, HBM],
        out_specs=[VMEM, VMEM],
        out_shape=[pltpu.VMEM((4, 4, 256, HD), BF16)] * 2,
        scratch_shapes=[
            pltpu.VMEM((8, tokens, 1024), BF16),
            pltpu.VMEM((tokens, HD), BF16),
            pltpu.SemaphoreType.DMA((9,)),
        ],
        compiler_params=pltpu.CompilerParams(vmem_limit_bytes=48 * MIB),
        cost_estimate=pl.CostEstimate(
            flops=2 * tokens * D * HD, bytes_accessed=tokens * D * 2, transcendentals=0
        ),
    )(place, normed_inputs, value_cotangent)


def small_call(kernel, outs, *args, keep=True):
    return pl.pallas_call(
        kernel,
        in_specs=[VMEM] * len(args),
        out_specs=[VMEM] * len(outs),
        out_shape=[
            (pltpu.VMEM if keep else jax.ShapeDtypeStruct)(shape, dtype) for shape, dtype in outs
        ],
        compiler_params=pltpu.CompilerParams(vmem_limit_bytes=16 * MIB),
        cost_estimate=pl.CostEstimate(flops=MIB, bytes_accessed=2 * MIB, transcendentals=0),
    )(*args)


def core_sum_kernel(mine, received, o0, o1, o2, o3):
    o0[...] = mine[0].astype(F32) + received[0].astype(F32)
    for d, out in ((1, o1), (2, o2), (3, o3)):
        out[...] = mine[d] + received[d]


def join_kernel(first, second, out):
    rows, steps = first.shape[0], first.shape[1]
    for i, ref in enumerate((first, second)):
        for r in range(rows):
            out[i, r * steps : (r + 1) * steps] = ref[r]


def pair_kernel(first, second, out):
    out[:2] = first[...]
    out[2:] = second[...]


def x_sum_kernel(own, r1, r2, r3, o0, o1, o2, o3):
    for e, out in enumerate((o0, o1, o2, o3)):
        total = own[e] + r1[e].astype(F32) + r2[e].astype(F32) + r3[e].astype(F32)
        out[...] = total.astype(out.dtype)


def total_of(own, r1, r2, r3):
    return own[...] + r1[...].astype(F32) + r2[...].astype(F32) + r3[...].astype(F32)


def update_kernel(weight, own, r1, r2, r3, updated):
    total = total_of(own, r1, r2, r3)
    updated[...] = (weight[...].astype(F32) - STEP * total).astype(BF16)


def gradient_kernel(own, r1, r2, r3, gradient):
    gradient[...] = total_of(own, r1, r2, r3)


def attend_kernel(lengths, queries, new_keys, cache_keys, cache_values, mixed_ref, weights_ref):
    rows = cache_keys.shape[0]
    slots = cache_keys.shape[1]
    steps = queries.shape[0] // rows
    every = HEADS * queries.shape[0]
    factor = 1.0 / math.sqrt(HD)
    heads = jnp.concatenate([queries[:, q * HD : (q + 1) * HD] for q in range(HEADS)], axis=0)
    place = lax.broadcasted_iota(jnp.int32, (every, slots), 0) % (rows * steps)
    lane = lax.broadcasted_iota(jnp.int32, (every, slots), 1)
    row = place // steps
    contract = (((1,), (1,)), ((), ()))
    scores = jnp.full((every, slots), -1e30, F32)
    for r in range(rows):
        product = lax.dot_general(heads, cache_keys[r], contract, preferred_element_type=F32)
        scores = jnp.where((row == r) & (lane < lengths[r]), product * factor, scores)
    fresh = lax.dot_general(heads, new_keys[...], contract, preferred_element_type=F32) * factor
    from_place, to_place = place[:, : rows * steps], lane[:, : rows * steps]
    visible = (from_place // steps == to_place // steps) & (to_place <= from_place)
    fresh = jnp.where(visible, fresh, -1e30)
    highest = jnp.maximum(
        jnp.max(scores, axis=1, keepdims=True), jnp.max(fresh, axis=1, keepdims=True)
    )
    cache_exp = jnp.exp(scores - highest)
    fresh_exp = jnp.exp(fresh - highest)
    total = jnp.sum(cache_exp, axis=1, keepdims=True) + jnp.sum(fresh_exp, axis=1, keepdims=True)
    cache_weights = (cache_exp / total).astype(BF16)
    weights_ref[...] = (fresh_exp / total).astype(BF16)
    mixed = jnp.zeros((every, HD), F32)
    for r in range(rows):
        product = jnp.dot(cache_weights, cache_values[r], preferred_element_type=F32)
        mixed = jnp.where(row == r, product, mixed)
    mixed_ref[...] = mixed


def attend_cache(lengths, queries, new_keys, cache_keys, cache_values):
    places = queries.shape[0]
    return pl.pallas_call(
        attend_kernel,
        in_specs=[SMEM] + [VMEM] * 4,
        out_specs=[VMEM, VMEM],
        out_shape=[
            jax.ShapeDtypeStruct((HEADS * places, HD), F32),
            jax.ShapeDtypeStruct((HEADS * places, places), BF16),
        ],
        compiler_params=pltpu.CompilerParams(vmem_limit_bytes=16 * MIB),
        cost_estimate=pl.CostEstimate(
            flops=MIB, bytes_accessed=MIB // 4, transcendentals=0
        ),
    )(lengths, queries, new_keys, cache_keys, cache_values)


def fill_rows(rows, x, updated):
    for d in range(4):
        rows[pl.ds(pl.multiple_of(lax.rem(x + d, 4) * 256, 256), 256), :] = updated[d]


def tokens_of(place, bits):
    return lax.rem(jnp.bitwise_xor(place[3], bits) + 4 - place[1], 4)


def project_own_kernel(place, near, u, out_ref, rows):
    own = jnp.where(place[0] == place[4], 0, 1)
    fill_rows(rows, place[2], u)
    inputs = jnp.concatenate([near[own], near[2 + own]], axis=0)
    out_ref[...] = jnp.dot(inputs, rows[...], preferred_element_type=F32)


def project_rest_kernel(place, near, far, u_own, u_other, start, out_ref, rows, last):
    own = jnp.where(place[0] == place[4], 0, 1)
    fill_rows(last, place[2], u_own)
    fill_rows(rows, place[2], u_other)
    inputs = [near[1 - own], near[3 - own], far[1 - own], far[3 - own]]
    product = jnp.dot(
        jnp.concatenate(inputs, axis=0), rows[...], preferred_element_type=F32
    )
    inputs = jnp.concatenate([far[own], far[2 + own]], axis=0)
    more = jnp.dot(inputs, last[...], preferred_element_type=F32)
    size = far.shape[1]
    for i, bits in enumerate((0, 1, 3, 2)):
        rest = start[i * size : (i + 1) * size] if i < 2 else more[(i - 2) * size : (i - 1) * size]
        total = product[i * size : (i + 1) * size] + rest
        out_ref[tokens_of(place, bits)] = total.astype(out_ref.dtype)


def project(kernel, out_shape, scratches, place, *args):
    return pl.pallas_call(
        kernel,
        in_specs=[SMEM] + [VMEM] * len(args),
        out_specs=VMEM,
        out_shape=out_shape,
        scratch_shapes=[pltpu.VMEM((1024, HD), BF16)] * scratches,
        compiler_params=pltpu.CompilerParams(vmem_limit_bytes=16 * MIB),
        cost_estimate=pl.CostEstimate(
            flops=2 * 256 * 1024 * HD, bytes_accessed=3 * MIB // 4, transcendentals=0
        ),
    )(place, *args)


def finish_kernel(parts, mixed, weights, values_ref, attended_ref):
    steps = values_ref.shape[1]
    total = parts[0].astype(F32)
    for i in range(1, 4):
        total += parts[i].astype(F32)
    values = total.astype(BF16)
    for r in range(values_ref.shape[0]):
        values_ref[r] = values[r * steps : (r + 1) * steps]
    places = values.shape[0]
    for q in range(HEADS):
        span = slice(q * places, (q + 1) * places)
        head = mixed[span] + jnp.dot(weights[span], values, preferred_element_type=F32)
        head = head.astype(BF16)
        for r in range(values_ref.shape[0]):
            attended_ref[r, :, q * HD : (q + 1) * HD] = head[r * steps : (r + 1) * steps]


def finish(parts, mixed, weights, rows, steps):
    return pl.pallas_call(
        finish_kernel,
        in_specs=[VMEM] * 3,
        out_specs=[VMEM, VMEM],
        out_shape=[
            jax.ShapeDtypeStruct((rows, steps, HD), BF16),
            jax.ShapeDtypeStruct((rows, steps, HEADS * HD), BF16),
        ],
        compiler_params=pltpu.CompilerParams(vmem_limit_bytes=16 * MIB),
    )(parts, mixed, weights)


def shards(
    normed_inputs,
    value_cotangent,
    value_weight,
    decode_inputs,
    queries,
    new_keys,
    cache_keys,
    cache_values,
    lengths,
):
    core, high, x, low, y = (lax.axis_index(n) for n in NAMES)
    row_count, step_count = decode_inputs.shape[0], decode_inputs.shape[1]
    places = row_count * step_count
    place = jnp.stack([core, high, x, y, low])

    second = shift(decode_inputs, "zl", 1)
    theirs, mine = partial_gradient(place, normed_inputs, value_cotangent)
    theirs, mine, second = lax.optimization_barrier((theirs, mine, second))
    received = shift(theirs, "c", 1)

    rows = (4, 256, HD)
    own, *sent = small_call(
        core_sum_kernel, [(rows, F32)] + [(rows, BF16)] * 3, mine, received
    )
    along_x = [shift(sent[d - 1], "x", d) for d in (2, 1, 3)]
    (both,) = small_call(
        join_kernel, [((2, places, D // 8), BF16)], decode_inputs, second
    )
    both = swap_high(both)
    attended_cache, fresh_weights = attend_cache(
        lengths,
        after(queries.reshape(places, -1), own),
        new_keys.reshape(places, HD),
        cache_keys,
        cache_values,
    )

    both = after(both, attended_cache)
    near = exchange(both, "y", 1)

    own, *along_x, attended_cache, fresh_weights = lax.optimization_barrier(
        (own, *along_x, attended_cache, fresh_weights)
    )
    rows = (256, HD)
    own, *sent = small_call(
        x_sum_kernel, [(rows, F32)] + [(rows, BF16)] * 3, own, *along_x
    )
    along_z = [shift(sent[e - 1], "zh", e) for e in (2, 1, 3)]
    own, *along_z, near = lax.optimization_barrier((own, *along_z, near))
    (updated,) = small_call(update_kernel, [(rows, BF16)], value_weight, own, *along_z)
    own = after(own, updated)
    (gradient,) = small_call(gradient_kernel, [(rows, F32)], own, *along_z, keep=False)

    (near,) = small_call(
        pair_kernel, [((4, places, D // 8), BF16)], after(both, updated), near
    )
    far = exchange(near, "y", 3)
    gathered = jnp.stack([updated] + [shift(updated, "x", -d) for d in (1, 2, 3)])
    gathered, gradient = lax.optimization_barrier((gathered, gradient))
    other = shift(gathered, "c", 1)
    partial = project(
        project_own_kernel, pltpu.VMEM((2 * places, HD), F32), 1, place, near, gathered
    )
    partial = project(
        project_rest_kernel,
        pltpu.VMEM((4, places, HD), BF16),
        2,
        place,
        near,
        far,
        gathered,
        other,
        partial,
    )
    exchanged = lax.all_to_all(partial, "zh", 0, 0, tiled=True)
    new_values, attended = finish(
        exchanged, attended_cache, fresh_weights, row_count, step_count
    )
    return (gradient, new_values, attended)


def solution(mesh):
    inner = Mesh(mesh.devices.reshape(tuple(SIZES.values())), NAMES)
    rows, columns = ("c", "zh", "x"), ("zl", "y")
    return jax.shard_map(
        shards,
        mesh=inner,
        in_specs=(
            P(rows, None),
            P(rows, columns),
            P(rows, columns),
            P(rows, None, columns),
            P(rows, None, columns),
            P(rows, None, columns),
            P(rows, None, columns),
            P(rows, None, columns),
            P(rows),
        ),
        out_specs=(
            P(rows, columns),
            P(rows, None, columns),
            P(rows, None, columns),
        ),
        check_vma=False,
    )
```

```python
import math

import jax
import jax.numpy as jnp
import numpy as np
from jax import lax
from jax.experimental import pallas as pl
from jax.experimental.pallas import tpu as pltpu
from jax.sharding import Mesh, PartitionSpec as P

D = 8192
HEADS = 8
HD = 128
SIZES = {"c": 2, "zh": 4, "x": 4, "zl": 2, "y": 4}
NAMES = tuple(SIZES)
STEP = 0.4 / math.sqrt(D)
MIB = 1 << 20
F32 = jnp.float32
BF16 = jnp.bfloat16
VMEM = pl.BlockSpec(memory_space=pltpu.VMEM)
SMEM = pl.BlockSpec(memory_space=pltpu.SMEM)
HBM = pl.BlockSpec(memory_space=pltpu.HBM)


def shift(value, axis, by):
    n = SIZES[axis]
    return lax.ppermute(value, axis, [(i, (i + by) % n) for i in range(n)])


def exchange(value, axis, bit):
    return lax.ppermute(value, axis, [(i, i ^ bit) for i in range(SIZES[axis])])


def swap_high(value):
    pairs = [(zh * 4 + y, y * 4 + (zh + y) % 4) for zh in range(4) for y in range(4)]
    return lax.ppermute(value, ("zh", "y"), pairs)


def after(value, *others):
    return lax.optimization_barrier((value, *others))[0]


def partial_kernel(place, x_hbm, v_hbm, theirs_ref, mine_ref, chunks, v_ref, sems):
    core, high, x = place[0], place[1], place[2]
    order = [(1 - core, theirs_ref, e) for e in range(4)] + [(core, mine_ref, e) for e in range(4)]
    copies = [pltpu.make_async_copy(v_hbm, v_ref, sems.at[8])]
    copies[0].start()
    for i, (half, _, e) in enumerate(order):
        column = (half * 4 + lax.rem(high + e, 4)) * 1024
        copies.append(
            pltpu.make_async_copy(
                x_hbm.at[:, pl.ds(pl.multiple_of(column, 1024), 1024)], chunks.at[i], sems.at[i]
            )
        )
        copies[-1].start()
    copies[0].wait()
    for i, (_, out_ref, e) in enumerate(order):
        copies[i + 1].wait()
        product = lax.dot_general(
            v_ref[...], chunks[i], (((0,), (0,)), ((), ())), preferred_element_type=F32
        )
        for block in range(4):
            rows = product[:, block * 256 : (block + 1) * 256].T
            out_ref[lax.rem(block + 4 - x, 4), e] = rows.astype(out_ref.dtype)


def partial_gradient(place, normed_inputs, value_cotangent):
    tokens = normed_inputs.shape[0]
    normed_inputs = pltpu.with_memory_space_constraint(normed_inputs, pltpu.HBM)
    value_cotangent = pltpu.with_memory_space_constraint(value_cotangent, pltpu.HBM)
    return pl.pallas_call(
        partial_kernel,
        in_specs=[SMEM, HBM, HBM],
        out_specs=[VMEM, VMEM],
        out_shape=[pltpu.VMEM((4, 4, 256, HD), BF16)] * 2,
        scratch_shapes=[
            pltpu.VMEM((8, tokens, 1024), BF16),
            pltpu.VMEM((tokens, HD), BF16),
            pltpu.SemaphoreType.DMA((9,)),
        ],
        compiler_params=pltpu.CompilerParams(vmem_limit_bytes=48 * MIB),
        cost_estimate=pl.CostEstimate(
            flops=2 * tokens * D * HD, bytes_accessed=tokens * D * 2, transcendentals=0
        ),
    )(place, normed_inputs, value_cotangent)


def small_call(kernel, outs, *args, keep=True):
    return pl.pallas_call(
        kernel,
        in_specs=[VMEM] * len(args),
        out_specs=[VMEM] * len(outs),
        out_shape=[
            (pltpu.VMEM if keep else jax.ShapeDtypeStruct)(shape, dtype) for shape, dtype in outs
        ],
        compiler_params=pltpu.CompilerParams(vmem_limit_bytes=16 * MIB),
        cost_estimate=pl.CostEstimate(flops=MIB, bytes_accessed=2 * MIB, transcendentals=0),
    )(*args)


def core_sum_kernel(mine, received, o0, o1, o2, o3):
    o0[...] = mine[0].astype(F32) + received[0].astype(F32)
    for d, out in ((1, o1), (2, o2), (3, o3)):
        out[...] = mine[d] + received[d]


def join_kernel(first, second, out):
    rows, steps = first.shape[0], first.shape[1]
    for i, ref in enumerate((first, second)):
        for r in range(rows):
            out[i, r * steps : (r + 1) * steps] = ref[r]


def pair_kernel(first, second, out):
    out[:2] = first[...]
    out[2:] = second[...]


def x_sum_kernel(own, r1, r2, r3, o0, o1, o2, o3):
    for e, out in enumerate((o0, o1, o2, o3)):
        total = own[e] + r1[e].astype(F32) + r2[e].astype(F32) + r3[e].astype(F32)
        out[...] = total.astype(out.dtype)


def total_of(own, r1, r2, r3):
    return own[...] + r1[...].astype(F32) + r2[...].astype(F32) + r3[...].astype(F32)


def update_kernel(weight, own, r1, r2, r3, updated):
    total = total_of(own, r1, r2, r3)
    updated[...] = (weight[...].astype(F32) - STEP * total).astype(BF16)


def gradient_kernel(own, r1, r2, r3, gradient):
    gradient[...] = total_of(own, r1, r2, r3)


def attend_kernel(lengths, queries, new_keys, cache_keys, cache_values, mixed_ref, weights_ref):
    rows = cache_keys.shape[0]
    slots = cache_keys.shape[1]
    steps = queries.shape[0] // rows
    every = HEADS * queries.shape[0]
    factor = 1.0 / math.sqrt(HD)
    heads = jnp.concatenate([queries[:, q * HD : (q + 1) * HD] for q in range(HEADS)], axis=0)
    place = lax.broadcasted_iota(jnp.int32, (every, slots), 0) % (rows * steps)
    lane = lax.broadcasted_iota(jnp.int32, (every, slots), 1)
    row = place // steps
    contract = (((1,), (1,)), ((), ()))
    scores = jnp.full((every, slots), -1e30, F32)
    for r in range(rows):
        product = lax.dot_general(heads, cache_keys[r], contract, preferred_element_type=F32)
        scores = jnp.where((row == r) & (lane < lengths[r]), product * factor, scores)
    fresh = lax.dot_general(heads, new_keys[...], contract, preferred_element_type=F32) * factor
    from_place, to_place = place[:, : rows * steps], lane[:, : rows * steps]
    visible = (from_place // steps == to_place // steps) & (to_place <= from_place)
    fresh = jnp.where(visible, fresh, -1e30)
    highest = jnp.maximum(
        jnp.max(scores, axis=1, keepdims=True), jnp.max(fresh, axis=1, keepdims=True)
    )
    cache_exp = jnp.exp(scores - highest)
    fresh_exp = jnp.exp(fresh - highest)
    total = jnp.sum(cache_exp, axis=1, keepdims=True) + jnp.sum(fresh_exp, axis=1, keepdims=True)
    cache_weights = (cache_exp / total).astype(BF16)
    weights_ref[...] = (fresh_exp / total).astype(BF16)
    mixed = jnp.zeros((every, HD), F32)
    for r in range(rows):
        product = jnp.dot(cache_weights, cache_values[r], preferred_element_type=F32)
        mixed = jnp.where(row == r, product, mixed)
    mixed_ref[...] = mixed


def attend_cache(lengths, queries, new_keys, cache_keys, cache_values):
    places = queries.shape[0]
    return pl.pallas_call(
        attend_kernel,
        in_specs=[SMEM] + [VMEM] * 4,
        out_specs=[VMEM, VMEM],
        out_shape=[
            jax.ShapeDtypeStruct((HEADS * places, HD), F32),
            jax.ShapeDtypeStruct((HEADS * places, places), BF16),
        ],
        compiler_params=pltpu.CompilerParams(vmem_limit_bytes=16 * MIB),
        cost_estimate=pl.CostEstimate(
            flops=MIB, bytes_accessed=MIB // 4, transcendentals=0
        ),
    )(lengths, queries, new_keys, cache_keys, cache_values)


def fill_rows(rows, x, updated):
    for d in range(4):
        rows[pl.ds(pl.multiple_of(lax.rem(x + d, 4) * 256, 256), 256), :] = updated[d]


def tokens_of(place, bits):
    return lax.rem(jnp.bitwise_xor(place[3], bits) + 4 - place[1], 4)


def project_own_kernel(place, near, u, out_ref, rows):
    own = jnp.where(place[0] == place[4], 0, 1)
    fill_rows(rows, place[2], u)
    inputs = jnp.concatenate([near[own], near[2 + own]], axis=0)
    out_ref[...] = jnp.dot(inputs, rows[...], preferred_element_type=F32)


def project_rest_kernel(place, near, far, u_own, u_other, start, out_ref, rows, last):
    own = jnp.where(place[0] == place[4], 0, 1)
    fill_rows(last, place[2], u_own)
    fill_rows(rows, place[2], u_other)
    inputs = [near[1 - own], near[3 - own], far[1 - own], far[3 - own]]
    product = jnp.dot(
        jnp.concatenate(inputs, axis=0), rows[...], preferred_element_type=F32
    )
    inputs = jnp.concatenate([far[own], far[2 + own]], axis=0)
    more = jnp.dot(inputs, last[...], preferred_element_type=F32)
    size = far.shape[1]
    for i, bits in enumerate((0, 1, 3, 2)):
        rest = start[i * size : (i + 1) * size] if i < 2 else more[(i - 2) * size : (i - 1) * size]
        total = product[i * size : (i + 1) * size] + rest
        out_ref[tokens_of(place, bits)] = total.astype(out_ref.dtype)


def project(kernel, out_shape, scratches, place, *args):
    return pl.pallas_call(
        kernel,
        in_specs=[SMEM] + [VMEM] * len(args),
        out_specs=VMEM,
        out_shape=out_shape,
        scratch_shapes=[pltpu.VMEM((1024, HD), BF16)] * scratches,
        compiler_params=pltpu.CompilerParams(vmem_limit_bytes=16 * MIB),
        cost_estimate=pl.CostEstimate(
            flops=2 * 256 * 1024 * HD, bytes_accessed=3 * MIB // 4, transcendentals=0
        ),
    )(place, *args)


def finish_kernel(parts, mixed, weights, values_ref, attended_ref):
    steps = values_ref.shape[1]
    total = parts[0].astype(F32)
    for i in range(1, 4):
        total += parts[i].astype(F32)
    values = total.astype(BF16)
    for r in range(values_ref.shape[0]):
        values_ref[r] = values[r * steps : (r + 1) * steps]
    places = values.shape[0]
    for q in range(HEADS):
        span = slice(q * places, (q + 1) * places)
        head = mixed[span] + jnp.dot(weights[span], values, preferred_element_type=F32)
        head = head.astype(BF16)
        for r in range(values_ref.shape[0]):
            attended_ref[r, :, q * HD : (q + 1) * HD] = head[r * steps : (r + 1) * steps]


def finish(parts, mixed, weights, rows, steps):
    return pl.pallas_call(
        finish_kernel,
        in_specs=[VMEM] * 3,
        out_specs=[VMEM, VMEM],
        out_shape=[
            jax.ShapeDtypeStruct((rows, steps, HD), BF16),
            jax.ShapeDtypeStruct((rows, steps, HEADS * HD), BF16),
        ],
        compiler_params=pltpu.CompilerParams(vmem_limit_bytes=16 * MIB),
    )(parts, mixed, weights)


def shards(
    normed_inputs,
    value_cotangent,
    value_weight,
    decode_inputs,
    queries,
    new_keys,
    cache_keys,
    cache_values,
    lengths,
):
    core, high, x, low, y = (lax.axis_index(n) for n in NAMES)
    row_count, step_count = decode_inputs.shape[0], decode_inputs.shape[1]
    places = row_count * step_count
    place = jnp.stack([core, high, x, y, low])

    swapped = swap_high(decode_inputs)
    theirs, mine = partial_gradient(place, normed_inputs, value_cotangent)
    theirs, mine, swapped = lax.optimization_barrier((theirs, mine, swapped))
    received = shift(theirs, "c", 1)
    second = shift(swapped, "zl", 1)

    rows = (4, 256, HD)
    own, *sent = small_call(
        core_sum_kernel, [(rows, F32)] + [(rows, BF16)] * 3, mine, received
    )
    along_x = [shift(sent[d - 1], "x", d) for d in (2, 1, 3)]
    attended_cache, fresh_weights = attend_cache(
        lengths,
        after(queries.reshape(places, -1), own),
        new_keys.reshape(places, HD),
        cache_keys,
        cache_values,
    )
    (both,) = small_call(
        join_kernel, [((2, places, D // 8), BF16)], after(swapped, own), second
    )
    near = exchange(both, "y", 1)

    own, *along_x, attended_cache, fresh_weights = lax.optimization_barrier(
        (own, *along_x, attended_cache, fresh_weights)
    )
    rows = (256, HD)
    own, *sent = small_call(
        x_sum_kernel, [(rows, F32)] + [(rows, BF16)] * 3, own, *along_x
    )
    (near,) = small_call(pair_kernel, [((4, places, D // 8), BF16)], after(both, own), near)
    far = exchange(near, "y", 3)
    along_z = [shift(sent[e - 1], "zh", e) for e in (2, 1, 3)]
    (updated,) = small_call(update_kernel, [(rows, BF16)], value_weight, own, *along_z)
    own = after(own, updated)
    (gradient,) = small_call(gradient_kernel, [(rows, F32)], own, *along_z, keep=False)

    gathered = jnp.stack([updated] + [shift(updated, "x", -d) for d in (1, 2, 3)])
    gathered, gradient, far = lax.optimization_barrier((gathered, gradient, far))
    other = shift(gathered, "c", 1)
    partial = project(
        project_own_kernel, pltpu.VMEM((2 * places, HD), F32), 1, place, near, gathered
    )
    partial = project(
        project_rest_kernel,
        pltpu.VMEM((4, places, HD), BF16),
        2,
        place,
        near,
        far,
        gathered,
        other,
        partial,
    )
    exchanged = lax.all_to_all(partial, "zh", 0, 0, tiled=True)
    new_values, attended = finish(
        exchanged, attended_cache, fresh_weights, row_count, step_count
    )
    return (gradient, new_values, attended)


def solution(mesh):
    inner = Mesh(mesh.devices.reshape(tuple(SIZES.values())), NAMES)
    rows, columns = ("c", "zh", "x"), ("zl", "y")
    return jax.shard_map(
        shards,
        mesh=inner,
        in_specs=(
            P(rows, None),
            P(rows, columns),
            P(rows, columns),
            P(rows, None, columns),
            P(rows, None, columns),
            P(rows, None, columns),
            P(rows, None, columns),
            P(rows, None, columns),
            P(rows),
        ),
        out_specs=(
            P(rows, columns),
            P(rows, None, columns),
            P(rows, None, columns),
        ),
        check_vma=False,
    )
```

```python
import math

import jax
import jax.numpy as jnp
import numpy as np
from jax import lax
from jax.experimental import pallas as pl
from jax.experimental.pallas import tpu as pltpu
from jax.sharding import Mesh, PartitionSpec as P

D = 8192
HEADS = 8
HD = 128
SIZES = {"c": 2, "zh": 4, "x": 4, "zl": 2, "y": 4}
NAMES = tuple(SIZES)
STEP = 0.4 / math.sqrt(D)
MIB = 1 << 20
F32 = jnp.float32
BF16 = jnp.bfloat16
VMEM = pl.BlockSpec(memory_space=pltpu.VMEM)
SMEM = pl.BlockSpec(memory_space=pltpu.SMEM)
HBM = pl.BlockSpec(memory_space=pltpu.HBM)


def shift(value, axis, by):
    n = SIZES[axis]
    return lax.ppermute(value, axis, [(i, (i + by) % n) for i in range(n)])


def exchange(value, axis, bit):
    return lax.ppermute(value, axis, [(i, i ^ bit) for i in range(SIZES[axis])])


def swap_cores(value):
    pairs = [(c * 2 + zl, zl * 2 + c) for c in range(2) for zl in range(2)]
    return lax.ppermute(value, ("c", "zl"), pairs)


def after(value, *others):
    return lax.optimization_barrier((value, *others))[0]


def partial_kernel(place, x_hbm, v_hbm, theirs_ref, mine_ref, chunks, v_ref, sems):
    core, high, x = place[0], place[1], place[2]
    order = [(1 - core, theirs_ref, e) for e in range(4)] + [(core, mine_ref, e) for e in range(4)]
    copies = [pltpu.make_async_copy(v_hbm, v_ref, sems.at[8])]
    copies[0].start()
    for i, (half, _, e) in enumerate(order):
        column = (half * 4 + lax.rem(high + e, 4)) * 1024
        copies.append(
            pltpu.make_async_copy(
                x_hbm.at[:, pl.ds(pl.multiple_of(column, 1024), 1024)], chunks.at[i], sems.at[i]
            )
        )
        copies[-1].start()
    copies[0].wait()
    for i, (_, out_ref, e) in enumerate(order):
        copies[i + 1].wait()
        product = lax.dot_general(
            v_ref[...], chunks[i], (((0,), (0,)), ((), ())), preferred_element_type=F32
        )
        for block in range(4):
            rows = product[:, block * 256 : (block + 1) * 256].T
            out_ref[lax.rem(block + 4 - x, 4), e] = rows.astype(out_ref.dtype)


def partial_gradient(place, normed_inputs, value_cotangent):
    tokens = normed_inputs.shape[0]
    normed_inputs = pltpu.with_memory_space_constraint(normed_inputs, pltpu.HBM)
    value_cotangent = pltpu.with_memory_space_constraint(value_cotangent, pltpu.HBM)
    return pl.pallas_call(
        partial_kernel,
        in_specs=[SMEM, HBM, HBM],
        out_specs=[VMEM, VMEM],
        out_shape=[pltpu.VMEM((4, 4, 256, HD), BF16)] * 2,
        scratch_shapes=[
            pltpu.VMEM((8, tokens, 1024), BF16),
            pltpu.VMEM((tokens, HD), BF16),
            pltpu.SemaphoreType.DMA((9,)),
        ],
        compiler_params=pltpu.CompilerParams(vmem_limit_bytes=48 * MIB),
        cost_estimate=pl.CostEstimate(
            flops=2 * tokens * D * HD, bytes_accessed=tokens * D * 2, transcendentals=0
        ),
    )(place, normed_inputs, value_cotangent)


def small_call(kernel, outs, *args, keep=True):
    return pl.pallas_call(
        kernel,
        in_specs=[VMEM] * len(args),
        out_specs=[VMEM] * len(outs),
        out_shape=[
            (pltpu.VMEM if keep else jax.ShapeDtypeStruct)(shape, dtype) for shape, dtype in outs
        ],
        compiler_params=pltpu.CompilerParams(vmem_limit_bytes=16 * MIB),
        cost_estimate=pl.CostEstimate(flops=MIB, bytes_accessed=2 * MIB, transcendentals=0),
    )(*args)


def core_sum_kernel(mine, received, o0, o1, o2, o3):
    o0[...] = mine[0].astype(F32) + received[0].astype(F32)
    for d, out in ((1, o1), (2, o2), (3, o3)):
        out[...] = mine[d] + received[d]


def join_kernel(first, second, out):
    rows, steps = first.shape[0], first.shape[1]
    for i, ref in enumerate((first, second)):
        for r in range(rows):
            out[i, r * steps : (r + 1) * steps] = ref[r]


def pair_kernel(first, second, out):
    out[:2] = first[...]
    out[2:] = second[...]


def x_sum_kernel(own, r1, r2, r3, o0, o1, o2, o3):
    for e, out in enumerate((o0, o1, o2, o3)):
        total = own[e] + r1[e].astype(F32) + r2[e].astype(F32) + r3[e].astype(F32)
        out[...] = total.astype(out.dtype)


def total_of(own, r1, r2, r3):
    return own[...] + r1[...].astype(F32) + r2[...].astype(F32) + r3[...].astype(F32)


def update_kernel(weight, own, r1, r2, r3, updated):
    total = total_of(own, r1, r2, r3)
    updated[...] = (weight[...].astype(F32) - STEP * total).astype(BF16)


def gradient_kernel(own, r1, r2, r3, gradient):
    gradient[...] = total_of(own, r1, r2, r3)


def attend_kernel(
    lengths, raw_queries, new_keys, cache_keys, cache_values, mixed_ref, weights_ref, queries
):
    rows = cache_keys.shape[0]
    slots = cache_keys.shape[1]
    steps = raw_queries.shape[1]
    every = HEADS * rows * steps
    factor = 1.0 / math.sqrt(HD)
    for r in range(rows):
        queries[r * steps : (r + 1) * steps] = raw_queries[r]
    heads = jnp.concatenate([queries[:, q * HD : (q + 1) * HD] for q in range(HEADS)], axis=0)
    place = lax.broadcasted_iota(jnp.int32, (every, slots), 0) % (rows * steps)
    lane = lax.broadcasted_iota(jnp.int32, (every, slots), 1)
    row = place // steps
    contract = (((1,), (1,)), ((), ()))
    scores = jnp.full((every, slots), -1e30, F32)
    for r in range(rows):
        product = lax.dot_general(heads, cache_keys[r], contract, preferred_element_type=F32)
        scores = jnp.where((row == r) & (lane < lengths[r]), product * factor, scores)
    fresh = lax.dot_general(heads, new_keys[...], contract, preferred_element_type=F32) * factor
    from_place, to_place = place[:, : rows * steps], lane[:, : rows * steps]
    visible = (from_place // steps == to_place // steps) & (to_place <= from_place)
    fresh = jnp.where(visible, fresh, -1e30)
    highest = jnp.maximum(
        jnp.max(scores, axis=1, keepdims=True), jnp.max(fresh, axis=1, keepdims=True)
    )
    cache_exp = jnp.exp(scores - highest)
    fresh_exp = jnp.exp(fresh - highest)
    total = jnp.sum(cache_exp, axis=1, keepdims=True) + jnp.sum(fresh_exp, axis=1, keepdims=True)
    cache_weights = (cache_exp / total).astype(BF16)
    weights_ref[...] = (fresh_exp / total).astype(BF16)
    mixed = jnp.zeros((every, HD), F32)
    for r in range(rows):
        product = jnp.dot(cache_weights, cache_values[r], preferred_element_type=F32)
        mixed = jnp.where(row == r, product, mixed)
    mixed_ref[...] = mixed


def attend_cache(lengths, queries, new_keys, cache_keys, cache_values):
    places = queries.shape[0] * queries.shape[1]
    return pl.pallas_call(
        attend_kernel,
        in_specs=[SMEM] + [VMEM] * 4,
        out_specs=[VMEM, VMEM],
        out_shape=[
            jax.ShapeDtypeStruct((HEADS * places, HD), F32),
            jax.ShapeDtypeStruct((HEADS * places, places), BF16),
        ],
        scratch_shapes=[pltpu.VMEM((places, HEADS * HD), BF16)],
        compiler_params=pltpu.CompilerParams(vmem_limit_bytes=16 * MIB),
        cost_estimate=pl.CostEstimate(
            flops=MIB, bytes_accessed=MIB // 4, transcendentals=0
        ),
    )(lengths, queries, new_keys, cache_keys, cache_values)


def project_kernel(place, near, far, u0, u1, u2, u3, own_ref, other_ref, rows):
    core, high, x, y, low = (place[i] for i in range(5))
    for d, u in enumerate((u0, u1, u2, u3)):
        for e in range(4):
            block = lax.rem(high + e, 4) * 4 + lax.rem(x + d, 4)
            rows[pl.ds(pl.multiple_of(block * 256, 256), 256), :] = u[e]
    total = None
    for bits, piece, first in ((0, near, 0), (1, near, 2), (3, far, 0), (2, far, 2)):
        start = pl.multiple_of(jnp.bitwise_xor(y, bits) * 1024, 1024)
        inputs = jnp.concatenate([piece[first], piece[first + 1]], axis=0)
        product = jnp.dot(inputs, rows[pl.ds(start, 1024), :], preferred_element_type=F32)
        total = product if total is None else total + product
    size = total.shape[0] // 2
    swap = core != low
    own_ref[...] = jnp.where(swap, total[size:], total[:size])
    other_ref[...] = jnp.where(swap, total[:size], total[size:]).astype(BF16)


def project(place, near, far, updated):
    places = near.shape[1]
    return pl.pallas_call(
        project_kernel,
        in_specs=[SMEM] + [VMEM] * 6,
        out_specs=[VMEM, VMEM],
        out_shape=[
            jax.ShapeDtypeStruct((places, HD), F32),
            jax.ShapeDtypeStruct((places, HD), BF16),
        ],
        scratch_shapes=[pltpu.VMEM((D // 2, HD), BF16)],
        compiler_params=pltpu.CompilerParams(vmem_limit_bytes=16 * MIB),
        cost_estimate=pl.CostEstimate(
            flops=2 * 128 * 4096 * HD, bytes_accessed=2 * MIB, transcendentals=0
        ),
    )(place, near, far, *updated)


def finish_kernel(own, received, mixed, weights, values_ref, attended_ref):
    steps = values_ref.shape[1]
    values = (own[...] + received[...].astype(F32)).astype(BF16)
    for r in range(values_ref.shape[0]):
        values_ref[r] = values[r * steps : (r + 1) * steps]
    places = values.shape[0]
    for q in range(HEADS):
        span = slice(q * places, (q + 1) * places)
        head = mixed[span] + jnp.dot(weights[span], values, preferred_element_type=F32)
        head = head.astype(BF16)
        for r in range(values_ref.shape[0]):
            attended_ref[r, :, q * HD : (q + 1) * HD] = head[r * steps : (r + 1) * steps]


def finish(own, received, mixed, weights, rows, steps):
    return pl.pallas_call(
        finish_kernel,
        in_specs=[VMEM] * 4,
        out_specs=[VMEM, VMEM],
        out_shape=[
            jax.ShapeDtypeStruct((rows, steps, HD), BF16),
            jax.ShapeDtypeStruct((rows, steps, HEADS * HD), BF16),
        ],
        compiler_params=pltpu.CompilerParams(vmem_limit_bytes=16 * MIB),
    )(own, received, mixed, weights)


def shards(
    normed_inputs,
    value_cotangent,
    value_weight,
    decode_inputs,
    queries,
    new_keys,
    cache_keys,
    cache_values,
    lengths,
):
    core, high, x, low, y = (lax.axis_index(n) for n in NAMES)
    row_count, step_count = decode_inputs.shape[0], decode_inputs.shape[1]
    places = row_count * step_count
    place = jnp.stack([core, high, x, y, low])

    swapped = swap_cores(decode_inputs)
    theirs, mine = partial_gradient(place, normed_inputs, value_cotangent)
    theirs, mine, swapped = lax.optimization_barrier((theirs, mine, swapped))
    received = shift(theirs, "c", 1)
    second = shift(swapped, "zl", 1)

    rows = (4, 256, HD)
    own, *sent = small_call(
        core_sum_kernel, [(rows, F32)] + [(rows, BF16)] * 3, mine, received
    )
    along_x = [shift(sent[d - 1], "x", d) for d in (2, 1, 3)]
    (both,) = small_call(
        join_kernel, [((2, places, D // 8), BF16)], after(swapped, own), second
    )
    near = exchange(both, "y", 1)

    rows = (256, HD)
    own, *sent = small_call(
        x_sum_kernel, [(rows, F32)] + [(rows, BF16)] * 3, own, *along_x
    )
    along_z = [shift(sent[e - 1], "zh", e) for e in (2, 1, 3)]
    attended_cache, fresh_weights = attend_cache(
        lengths, after(queries, own), new_keys.reshape(places, HD), cache_keys, cache_values
    )
    own, *along_z, near, attended_cache, fresh_weights = lax.optimization_barrier(
        (own, *along_z, near, attended_cache, fresh_weights)
    )
    (updated,) = small_call(update_kernel, [(rows, BF16)], value_weight, own, *along_z)
    own = after(own, updated)
    (gradient,) = small_call(gradient_kernel, [(rows, F32)], own, *along_z, keep=False)

    (near,) = small_call(pair_kernel, [((4, places, D // 8), BF16)], after(both, updated), near)
    far = exchange(near, "y", 3)
    gathered = jnp.stack([updated] + [shift(updated, "zh", -e) for e in (1, 2, 3)])
    gathered, gradient = lax.optimization_barrier((gathered, gradient))
    gathered = [gathered] + [shift(gathered, "x", -d) for d in (1, 2, 3)]
    own, other = project(place, near, far, gathered)
    new_values, attended = finish(
        own, shift(other, "c", 1), attended_cache, fresh_weights, row_count, step_count
    )
    return (gradient, new_values, attended)


def solution(mesh):
    inner = Mesh(mesh.devices.reshape(tuple(SIZES.values())), NAMES)
    rows, columns = ("c", "zh", "x"), ("zl", "y")
    return jax.shard_map(
        shards,
        mesh=inner,
        in_specs=(
            P(rows, None),
            P(rows, columns),
            P(rows, columns),
            P(rows, None, columns),
            P(rows, None, columns),
            P(rows, None, columns),
            P(rows, None, columns),
            P(rows, None, columns),
            P(rows),
        ),
        out_specs=(
            P(rows, columns),
            P(rows, None, columns),
            P(rows, None, columns),
        ),
        check_vma=False,
    )
```

```python
import math

import jax
import jax.numpy as jnp
import numpy as np
from jax import lax
from jax.experimental import pallas as pl
from jax.experimental.pallas import tpu as pltpu
from jax.sharding import Mesh, PartitionSpec as P

D = 8192
HEADS = 8
HD = 128
SIZES = {"c": 2, "zh": 4, "x": 4, "zl": 2, "y": 4}
NAMES = tuple(SIZES)
STEP = 0.4 / math.sqrt(D)
MIB = 1 << 20
F32 = jnp.float32
BF16 = jnp.bfloat16
VMEM = pl.BlockSpec(memory_space=pltpu.VMEM)
SMEM = pl.BlockSpec(memory_space=pltpu.SMEM)
HBM = pl.BlockSpec(memory_space=pltpu.HBM)


def shift(value, axis, by):
    n = SIZES[axis]
    return lax.ppermute(value, axis, [(i, (i + by) % n) for i in range(n)])


def exchange(value, axis, bit):
    return lax.ppermute(value, axis, [(i, i ^ bit) for i in range(SIZES[axis])])


def swap_cores(value):
    pairs = [(c * 2 + zl, zl * 2 + c) for c in range(2) for zl in range(2)]
    return lax.ppermute(value, ("c", "zl"), pairs)


def after(value, *others):
    return lax.optimization_barrier((value, *others))[0]


def partial_kernel(place, x_hbm, v_hbm, theirs_ref, mine_ref, chunks, v_ref, sems):
    core, high, x = place[0], place[1], place[2]
    order = [(1 - core, theirs_ref, e) for e in range(4)] + [(core, mine_ref, e) for e in range(4)]
    copies = [pltpu.make_async_copy(v_hbm, v_ref, sems.at[8])]
    copies[0].start()
    for i, (half, _, e) in enumerate(order):
        column = (half * 4 + lax.rem(high + e, 4)) * 1024
        copies.append(
            pltpu.make_async_copy(
                x_hbm.at[:, pl.ds(pl.multiple_of(column, 1024), 1024)], chunks.at[i], sems.at[i]
            )
        )
        copies[-1].start()
    copies[0].wait()
    for i, (_, out_ref, e) in enumerate(order):
        copies[i + 1].wait()
        product = lax.dot_general(
            v_ref[...], chunks[i], (((0,), (0,)), ((), ())), preferred_element_type=F32
        )
        for block in range(4):
            rows = product[:, block * 256 : (block + 1) * 256].T
            out_ref[lax.rem(block + 4 - x, 4), e] = rows.astype(out_ref.dtype)


def partial_gradient(place, normed_inputs, value_cotangent):
    tokens = normed_inputs.shape[0]
    normed_inputs = pltpu.with_memory_space_constraint(normed_inputs, pltpu.HBM)
    value_cotangent = pltpu.with_memory_space_constraint(value_cotangent, pltpu.HBM)
    return pl.pallas_call(
        partial_kernel,
        in_specs=[SMEM, HBM, HBM],
        out_specs=[VMEM, VMEM],
        out_shape=[pltpu.VMEM((4, 4, 256, HD), BF16)] * 2,
        scratch_shapes=[
            pltpu.VMEM((8, tokens, 1024), BF16),
            pltpu.VMEM((tokens, HD), BF16),
            pltpu.SemaphoreType.DMA((9,)),
        ],
        compiler_params=pltpu.CompilerParams(vmem_limit_bytes=48 * MIB),
        cost_estimate=pl.CostEstimate(
            flops=2 * tokens * D * HD, bytes_accessed=tokens * D * 2, transcendentals=0
        ),
    )(place, normed_inputs, value_cotangent)


def small_call(kernel, outs, *args, keep=True):
    return pl.pallas_call(
        kernel,
        in_specs=[VMEM] * len(args),
        out_specs=[VMEM] * len(outs),
        out_shape=[
            (pltpu.VMEM if keep else jax.ShapeDtypeStruct)(shape, dtype) for shape, dtype in outs
        ],
        compiler_params=pltpu.CompilerParams(vmem_limit_bytes=16 * MIB),
        cost_estimate=pl.CostEstimate(flops=MIB, bytes_accessed=2 * MIB, transcendentals=0),
    )(*args)


def core_sum_kernel(mine, received, own, to_next, to_far, to_last, kept):
    own[...] = mine[0].astype(F32) + received[0].astype(F32)
    to_next[...] = mine[1] + received[1]
    to_far[...] = mine[2, :2] + received[2, :2]
    to_last[:2] = mine[3, :2] + received[3, :2]
    to_last[2:] = mine[2, 2:] + received[2, 2:]
    kept[...] = mine[3, 2:] + received[3, 2:]


def relay_kernel(kept, received, out):
    out[...] = kept[...] + received[2:]


def split_kernel(u0, u1, u2, u3, whole, half):
    for e, u in enumerate((u0, u1, u2, u3)):
        whole[e] = u[...]
    half[0] = u0[...]
    half[1] = u1[...]


def second_half_kernel(whole, half):
    half[...] = whole[2:]


def join_kernel(first, second, out):
    rows, steps = first.shape[0], first.shape[1]
    for i, ref in enumerate((first, second)):
        for r in range(rows):
            out[i, r * steps : (r + 1) * steps] = ref[r]


def pair_kernel(first, second, out):
    out[:2] = first[...]
    out[2:] = second[...]


def x_sum_kernel(own, from_last, from_far, from_next, relayed, o0, o1, o2, o3):
    for e, out in enumerate((o0, o1, o2, o3)):
        total = own[e] + from_last[e].astype(F32)
        if e < 2:
            total += from_far[e].astype(F32) + from_next[e].astype(F32)
        else:
            total += relayed[e - 2].astype(F32)
        out[...] = total.astype(out.dtype)


def total_of(own, r1, r2, r3):
    return own[...] + r1[...].astype(F32) + r2[...].astype(F32) + r3[...].astype(F32)


def update_kernel(weight, own, r1, r2, r3, updated):
    total = total_of(own, r1, r2, r3)
    updated[...] = (weight[...].astype(F32) - STEP * total).astype(BF16)


def gradient_kernel(own, r1, r2, r3, gradient):
    gradient[...] = total_of(own, r1, r2, r3)


def attend_kernel(
    lengths, raw_queries, new_keys, cache_keys, cache_values, mixed_ref, weights_ref, queries
):
    rows = cache_keys.shape[0]
    slots = cache_keys.shape[1]
    steps = raw_queries.shape[1]
    every = HEADS * rows * steps
    factor = 1.0 / math.sqrt(HD)
    for r in range(rows):
        queries[r * steps : (r + 1) * steps] = raw_queries[r]
    heads = jnp.concatenate([queries[:, q * HD : (q + 1) * HD] for q in range(HEADS)], axis=0)
    place = lax.broadcasted_iota(jnp.int32, (every, slots), 0) % (rows * steps)
    lane = lax.broadcasted_iota(jnp.int32, (every, slots), 1)
    row = place // steps
    contract = (((1,), (1,)), ((), ()))
    scores = jnp.full((every, slots), -1e30, F32)
    for r in range(rows):
        product = lax.dot_general(heads, cache_keys[r], contract, preferred_element_type=F32)
        scores = jnp.where((row == r) & (lane < lengths[r]), product * factor, scores)
    fresh = lax.dot_general(heads, new_keys[...], contract, preferred_element_type=F32) * factor
    from_place, to_place = place[:, : rows * steps], lane[:, : rows * steps]
    visible = (from_place // steps == to_place // steps) & (to_place <= from_place)
    fresh = jnp.where(visible, fresh, -1e30)
    highest = jnp.maximum(
        jnp.max(scores, axis=1, keepdims=True), jnp.max(fresh, axis=1, keepdims=True)
    )
    cache_exp = jnp.exp(scores - highest)
    fresh_exp = jnp.exp(fresh - highest)
    total = jnp.sum(cache_exp, axis=1, keepdims=True) + jnp.sum(fresh_exp, axis=1, keepdims=True)
    cache_weights = (cache_exp / total).astype(BF16)
    weights_ref[...] = (fresh_exp / total).astype(BF16)
    mixed = jnp.zeros((every, HD), F32)
    for r in range(rows):
        product = jnp.dot(cache_weights, cache_values[r], preferred_element_type=F32)
        mixed = jnp.where(row == r, product, mixed)
    mixed_ref[...] = mixed


def attend_cache(lengths, queries, new_keys, cache_keys, cache_values):
    places = queries.shape[0] * queries.shape[1]
    return pl.pallas_call(
        attend_kernel,
        in_specs=[SMEM] + [VMEM] * 4,
        out_specs=[VMEM, VMEM],
        out_shape=[
            jax.ShapeDtypeStruct((HEADS * places, HD), F32),
            jax.ShapeDtypeStruct((HEADS * places, places), BF16),
        ],
        scratch_shapes=[pltpu.VMEM((places, HEADS * HD), BF16)],
        compiler_params=pltpu.CompilerParams(vmem_limit_bytes=16 * MIB),
        cost_estimate=pl.CostEstimate(
            flops=MIB, bytes_accessed=MIB // 4, transcendentals=0
        ),
    )(lengths, queries, new_keys, cache_keys, cache_values)


def project_kernel(place, near, far, u0, u1, u2, u2_more, u3, own_ref, other_ref, rows):
    core, high, x, y, low = (place[i] for i in range(5))
    for d, u in enumerate((u0, u1, u2, u3)):
        for e in range(4):
            block = lax.rem(high + e, 4) * 4 + lax.rem(x + d, 4)
            part = u2_more[e - 2] if d == 2 and e >= 2 else u[e]
            rows[pl.ds(pl.multiple_of(block * 256, 256), 256), :] = part
    total = None
    for bits, piece, first in ((0, near, 0), (1, near, 2), (3, far, 0), (2, far, 2)):
        start = pl.multiple_of(jnp.bitwise_xor(y, bits) * 1024, 1024)
        inputs = jnp.concatenate([piece[first], piece[first + 1]], axis=0)
        product = jnp.dot(inputs, rows[pl.ds(start, 1024), :], preferred_element_type=F32)
        total = product if total is None else total + product
    size = total.shape[0] // 2
    swap = core != low
    own_ref[...] = jnp.where(swap, total[size:], total[:size])
    other_ref[...] = jnp.where(swap, total[:size], total[size:]).astype(BF16)


def project(place, near, far, updated):
    places = near.shape[1]
    return pl.pallas_call(
        project_kernel,
        in_specs=[SMEM] + [VMEM] * 7,
        out_specs=[VMEM, VMEM],
        out_shape=[
            jax.ShapeDtypeStruct((places, HD), F32),
            jax.ShapeDtypeStruct((places, HD), BF16),
        ],
        scratch_shapes=[pltpu.VMEM((D // 2, HD), BF16)],
        compiler_params=pltpu.CompilerParams(vmem_limit_bytes=16 * MIB),
        cost_estimate=pl.CostEstimate(
            flops=2 * 128 * 4096 * HD, bytes_accessed=2 * MIB, transcendentals=0
        ),
    )(place, near, far, *updated)


def finish_kernel(own, received, mixed, weights, values_ref, attended_ref):
    steps = values_ref.shape[1]
    values = (own[...] + received[...].astype(F32)).astype(BF16)
    for r in range(values_ref.shape[0]):
        values_ref[r] = values[r * steps : (r + 1) * steps]
    places = values.shape[0]
    for q in range(HEADS):
        span = slice(q * places, (q + 1) * places)
        head = mixed[span] + jnp.dot(weights[span], values, preferred_element_type=F32)
        head = head.astype(BF16)
        for r in range(values_ref.shape[0]):
            attended_ref[r, :, q * HD : (q + 1) * HD] = head[r * steps : (r + 1) * steps]


def finish(own, received, mixed, weights, rows, steps):
    return pl.pallas_call(
        finish_kernel,
        in_specs=[VMEM] * 4,
        out_specs=[VMEM, VMEM],
        out_shape=[
            jax.ShapeDtypeStruct((rows, steps, HD), BF16),
            jax.ShapeDtypeStruct((rows, steps, HEADS * HD), BF16),
        ],
        compiler_params=pltpu.CompilerParams(vmem_limit_bytes=16 * MIB),
    )(own, received, mixed, weights)


def shards(
    normed_inputs,
    value_cotangent,
    value_weight,
    decode_inputs,
    queries,
    new_keys,
    cache_keys,
    cache_values,
    lengths,
):
    core, high, x, low, y = (lax.axis_index(n) for n in NAMES)
    row_count, step_count = decode_inputs.shape[0], decode_inputs.shape[1]
    places = row_count * step_count
    place = jnp.stack([core, high, x, y, low])

    swapped = swap_cores(decode_inputs)
    theirs, mine = partial_gradient(place, normed_inputs, value_cotangent)
    theirs, mine, swapped = lax.optimization_barrier((theirs, mine, swapped))
    received = shift(theirs, "c", 1)
    second = shift(swapped, "zl", 1)

    rows, half = (4, 256, HD), (2, 256, HD)
    own, to_next, to_far, to_last, kept = small_call(
        core_sum_kernel,
        [(rows, F32), (rows, BF16), (half, BF16), (rows, BF16), (half, BF16)],
        mine,
        received,
    )
    from_next = shift(to_last, "x", -1)
    from_far = shift(to_far, "x", 2)
    from_last = shift(to_next, "x", 1)
    kept, from_next, from_far = lax.optimization_barrier((kept, from_next, from_far))
    (passed,) = small_call(relay_kernel, [(half, BF16)], kept, from_next)
    relayed = shift(passed, "x", -1)
    (both,) = small_call(
        join_kernel, [((2, places, D // 8), BF16)], after(swapped, passed), second
    )
    near = exchange(both, "y", 1)

    rows = (256, HD)
    own, *sent = small_call(
        x_sum_kernel,
        [(rows, F32)] + [(rows, BF16)] * 3,
        own,
        from_last,
        from_far,
        from_next,
        relayed,
    )
    along_z = [shift(sent[e - 1], "zh", e) for e in (2, 1, 3)]
    attended_cache, fresh_weights = attend_cache(
        lengths, after(queries, own), new_keys.reshape(places, HD), cache_keys, cache_values
    )
    own, *along_z, near, attended_cache, fresh_weights = lax.optimization_barrier(
        (own, *along_z, near, attended_cache, fresh_weights)
    )
    (updated,) = small_call(update_kernel, [(rows, BF16)], value_weight, own, *along_z)
    own = after(own, updated)
    (gradient,) = small_call(gradient_kernel, [(rows, F32)], own, *along_z, keep=False)

    (near,) = small_call(pair_kernel, [((4, places, D // 8), BF16)], after(both, updated), near)
    far = exchange(near, "y", 3)
    along_z = [updated] + [shift(updated, "zh", -e) for e in (1, 2, 3)]
    along_z, gradient = lax.optimization_barrier((along_z, gradient))
    rows = (4, 256, HD)
    gathered, first = small_call(split_kernel, [(rows, BF16), (half, BF16)], *along_z)
    from_next = shift(gathered, "x", -1)
    from_far = shift(first, "x", 2)
    from_last = shift(gathered, "x", 1)
    (second,) = small_call(second_half_kernel, [(half, BF16)], from_next)
    relayed = shift(second, "x", -1)
    gathered = (gathered, from_next, from_far, relayed, from_last)
    own, other = project(place, near, far, gathered)
    new_values, attended = finish(
        own, shift(other, "c", 1), attended_cache, fresh_weights, row_count, step_count
    )
    return (gradient, new_values, attended)


def solution(mesh):
    inner = Mesh(mesh.devices.reshape(tuple(SIZES.values())), NAMES)
    rows, columns = ("c", "zh", "x"), ("zl", "y")
    return jax.shard_map(
        shards,
        mesh=inner,
        in_specs=(
            P(rows, None),
            P(rows, columns),
            P(rows, columns),
            P(rows, None, columns),
            P(rows, None, columns),
            P(rows, None, columns),
            P(rows, None, columns),
            P(rows, None, columns),
            P(rows),
        ),
        out_specs=(
            P(rows, columns),
            P(rows, None, columns),
            P(rows, None, columns),
        ),
        check_vma=False,
    )
```

```python
import math

import jax
import jax.numpy as jnp
import numpy as np
from jax import lax
from jax.experimental import pallas as pl
from jax.experimental.pallas import tpu as pltpu
from jax.sharding import Mesh, PartitionSpec as P

D = 8192
HEADS = 8
HD = 128
SIZES = {"c": 2, "zh": 4, "x": 4, "zl": 2, "y": 4}
NAMES = tuple(SIZES)
STEP = 0.4 / math.sqrt(D)
MIB = 1 << 20
F32 = jnp.float32
BF16 = jnp.bfloat16
VMEM = pl.BlockSpec(memory_space=pltpu.VMEM)
SMEM = pl.BlockSpec(memory_space=pltpu.SMEM)
HBM = pl.BlockSpec(memory_space=pltpu.HBM)


def shift(value, axis, by):
    n = SIZES[axis]
    return lax.ppermute(value, axis, [(i, (i + by) % n) for i in range(n)])


def exchange(value, axis, bit):
    return lax.ppermute(value, axis, [(i, i ^ bit) for i in range(SIZES[axis])])


def swap_high(value):
    pairs = [(zh * 4 + y, y * 4 + (zh + y) % 4) for zh in range(4) for y in range(4)]
    return lax.ppermute(value, ("zh", "y"), pairs)


def after(value, *others):
    return lax.optimization_barrier((value, *others))[0]


def partial_kernel(place, x_hbm, v_hbm, theirs_ref, mine_ref, chunks, v_ref, sems):
    core, high, x = place[0], place[1], place[2]
    order = [(1 - core, theirs_ref, e) for e in range(4)] + [(core, mine_ref, e) for e in range(4)]
    copies = [pltpu.make_async_copy(v_hbm, v_ref, sems.at[8])]
    copies[0].start()
    for i, (half, _, e) in enumerate(order):
        column = (half * 4 + lax.rem(high + e, 4)) * 1024
        copies.append(
            pltpu.make_async_copy(
                x_hbm.at[:, pl.ds(pl.multiple_of(column, 1024), 1024)], chunks.at[i], sems.at[i]
            )
        )
        copies[-1].start()
    copies[0].wait()
    for i, (_, out_ref, e) in enumerate(order):
        copies[i + 1].wait()
        product = lax.dot_general(
            v_ref[...], chunks[i], (((0,), (0,)), ((), ())), preferred_element_type=F32
        )
        for block in range(4):
            rows = product[:, block * 256 : (block + 1) * 256].T
            out_ref[lax.rem(block + 4 - x, 4), e] = rows.astype(out_ref.dtype)


def partial_gradient(place, normed_inputs, value_cotangent):
    tokens = normed_inputs.shape[0]
    normed_inputs = pltpu.with_memory_space_constraint(normed_inputs, pltpu.HBM)
    value_cotangent = pltpu.with_memory_space_constraint(value_cotangent, pltpu.HBM)
    return pl.pallas_call(
        partial_kernel,
        in_specs=[SMEM, HBM, HBM],
        out_specs=[VMEM, VMEM],
        out_shape=[pltpu.VMEM((4, 4, 256, HD), BF16)] * 2,
        scratch_shapes=[
            pltpu.VMEM((8, tokens, 1024), BF16),
            pltpu.VMEM((tokens, HD), BF16),
            pltpu.SemaphoreType.DMA((9,)),
        ],
        compiler_params=pltpu.CompilerParams(vmem_limit_bytes=48 * MIB),
        cost_estimate=pl.CostEstimate(
            flops=2 * tokens * D * HD, bytes_accessed=tokens * D * 2, transcendentals=0
        ),
    )(place, normed_inputs, value_cotangent)


def small_call(kernel, outs, *args, keep=True):
    return pl.pallas_call(
        kernel,
        in_specs=[VMEM] * len(args),
        out_specs=[VMEM] * len(outs),
        out_shape=[
            (pltpu.VMEM if keep else jax.ShapeDtypeStruct)(shape, dtype) for shape, dtype in outs
        ],
        compiler_params=pltpu.CompilerParams(vmem_limit_bytes=16 * MIB),
        cost_estimate=pl.CostEstimate(flops=MIB, bytes_accessed=2 * MIB, transcendentals=0),
    )(*args)


def core_sum_kernel(mine, received, o0, o1, o2, o3):
    o0[...] = mine[0].astype(F32) + received[0].astype(F32)
    for d, out in ((1, o1), (2, o2), (3, o3)):
        out[...] = mine[d] + received[d]


def join_kernel(first, second, out):
    rows, steps = first.shape[0], first.shape[1]
    for i, ref in enumerate((first, second)):
        for r in range(rows):
            out[i, r * steps : (r + 1) * steps] = ref[r]


def pair_kernel(first, second, out):
    out[:2] = first[...]
    out[2:] = second[...]


def x_sum_kernel(own, r1, r2, r3, o0, o1, o2, o3):
    for e, out in enumerate((o0, o1, o2, o3)):
        total = own[e] + r1[e].astype(F32) + r2[e].astype(F32) + r3[e].astype(F32)
        out[...] = total.astype(out.dtype)


def total_of(own, r1, r2, r3):
    return own[...] + r1[...].astype(F32) + r2[...].astype(F32) + r3[...].astype(F32)


def update_kernel(weight, own, r1, r2, r3, updated):
    total = total_of(own, r1, r2, r3)
    updated[...] = (weight[...].astype(F32) - STEP * total).astype(BF16)


def gradient_kernel(own, r1, r2, r3, gradient):
    gradient[...] = total_of(own, r1, r2, r3)


def attend_kernel(
    lengths, raw_queries, new_keys, cache_keys, cache_values, mixed_ref, weights_ref, queries
):
    rows = cache_keys.shape[0]
    slots = cache_keys.shape[1]
    steps = raw_queries.shape[1]
    every = HEADS * rows * steps
    factor = 1.0 / math.sqrt(HD)
    for r in range(rows):
        queries[r * steps : (r + 1) * steps] = raw_queries[r]
    heads = jnp.concatenate([queries[:, q * HD : (q + 1) * HD] for q in range(HEADS)], axis=0)
    place = lax.broadcasted_iota(jnp.int32, (every, slots), 0) % (rows * steps)
    lane = lax.broadcasted_iota(jnp.int32, (every, slots), 1)
    row = place // steps
    contract = (((1,), (1,)), ((), ()))
    scores = jnp.full((every, slots), -1e30, F32)
    for r in range(rows):
        product = lax.dot_general(heads, cache_keys[r], contract, preferred_element_type=F32)
        scores = jnp.where((row == r) & (lane < lengths[r]), product * factor, scores)
    fresh = lax.dot_general(heads, new_keys[...], contract, preferred_element_type=F32) * factor
    from_place, to_place = place[:, : rows * steps], lane[:, : rows * steps]
    visible = (from_place // steps == to_place // steps) & (to_place <= from_place)
    fresh = jnp.where(visible, fresh, -1e30)
    highest = jnp.maximum(
        jnp.max(scores, axis=1, keepdims=True), jnp.max(fresh, axis=1, keepdims=True)
    )
    cache_exp = jnp.exp(scores - highest)
    fresh_exp = jnp.exp(fresh - highest)
    total = jnp.sum(cache_exp, axis=1, keepdims=True) + jnp.sum(fresh_exp, axis=1, keepdims=True)
    cache_weights = (cache_exp / total).astype(BF16)
    weights_ref[...] = (fresh_exp / total).astype(BF16)
    mixed = jnp.zeros((every, HD), F32)
    for r in range(rows):
        product = jnp.dot(cache_weights, cache_values[r], preferred_element_type=F32)
        mixed = jnp.where(row == r, product, mixed)
    mixed_ref[...] = mixed


def attend_cache(lengths, queries, new_keys, cache_keys, cache_values):
    places = queries.shape[0] * queries.shape[1]
    return pl.pallas_call(
        attend_kernel,
        in_specs=[SMEM] + [VMEM] * 4,
        out_specs=[VMEM, VMEM],
        out_shape=[
            jax.ShapeDtypeStruct((HEADS * places, HD), F32),
            jax.ShapeDtypeStruct((HEADS * places, places), BF16),
        ],
        scratch_shapes=[pltpu.VMEM((places, HEADS * HD), BF16)],
        compiler_params=pltpu.CompilerParams(vmem_limit_bytes=16 * MIB),
        cost_estimate=pl.CostEstimate(
            flops=MIB, bytes_accessed=MIB // 4, transcendentals=0
        ),
    )(lengths, queries, new_keys, cache_keys, cache_values)


def fill_rows(rows, x, updated):
    for d in range(4):
        rows[pl.ds(pl.multiple_of(lax.rem(x + d, 4) * 256, 256), 256), :] = updated[d]


def tokens_of(place, bits):
    return lax.rem(jnp.bitwise_xor(place[3], bits) + 4 - place[1], 4)


def project_own_kernel(place, near, u, out_ref, rows):
    own = jnp.where(place[0] == place[4], 0, 1)
    fill_rows(rows, place[2], u)
    inputs = jnp.concatenate([near[own], near[2 + own]], axis=0)
    out_ref[...] = jnp.dot(inputs, rows[...], preferred_element_type=F32)


def project_rest_kernel(place, near, far, u_own, u_other, start, out_ref, rows, last):
    own = jnp.where(place[0] == place[4], 0, 1)
    fill_rows(last, place[2], u_own)
    fill_rows(rows, place[2], u_other)
    inputs = [near[1 - own], near[3 - own], far[1 - own], far[3 - own]]
    product = jnp.dot(
        jnp.concatenate(inputs, axis=0), rows[...], preferred_element_type=F32
    )
    inputs = jnp.concatenate([far[own], far[2 + own]], axis=0)
    more = jnp.dot(inputs, last[...], preferred_element_type=F32)
    size = far.shape[1]
    for i, bits in enumerate((0, 1, 3, 2)):
        rest = start[i * size : (i + 1) * size] if i < 2 else more[(i - 2) * size : (i - 1) * size]
        total = product[i * size : (i + 1) * size] + rest
        out_ref[tokens_of(place, bits)] = total.astype(out_ref.dtype)


def project(kernel, out_shape, scratches, place, *args):
    return pl.pallas_call(
        kernel,
        in_specs=[SMEM] + [VMEM] * len(args),
        out_specs=VMEM,
        out_shape=out_shape,
        scratch_shapes=[pltpu.VMEM((1024, HD), BF16)] * scratches,
        compiler_params=pltpu.CompilerParams(vmem_limit_bytes=16 * MIB),
        cost_estimate=pl.CostEstimate(
            flops=2 * 256 * 1024 * HD, bytes_accessed=3 * MIB // 4, transcendentals=0
        ),
    )(place, *args)


def finish_kernel(parts, mixed, weights, values_ref, attended_ref):
    steps = values_ref.shape[1]
    total = parts[0].astype(F32)
    for i in range(1, 4):
        total += parts[i].astype(F32)
    values = total.astype(BF16)
    for r in range(values_ref.shape[0]):
        values_ref[r] = values[r * steps : (r + 1) * steps]
    places = values.shape[0]
    for q in range(HEADS):
        span = slice(q * places, (q + 1) * places)
        head = mixed[span] + jnp.dot(weights[span], values, preferred_element_type=F32)
        head = head.astype(BF16)
        for r in range(values_ref.shape[0]):
            attended_ref[r, :, q * HD : (q + 1) * HD] = head[r * steps : (r + 1) * steps]


def finish(parts, mixed, weights, rows, steps):
    return pl.pallas_call(
        finish_kernel,
        in_specs=[VMEM] * 3,
        out_specs=[VMEM, VMEM],
        out_shape=[
            jax.ShapeDtypeStruct((rows, steps, HD), BF16),
            jax.ShapeDtypeStruct((rows, steps, HEADS * HD), BF16),
        ],
        compiler_params=pltpu.CompilerParams(vmem_limit_bytes=16 * MIB),
    )(parts, mixed, weights)


def shards(
    normed_inputs,
    value_cotangent,
    value_weight,
    decode_inputs,
    queries,
    new_keys,
    cache_keys,
    cache_values,
    lengths,
):
    core, high, x, low, y = (lax.axis_index(n) for n in NAMES)
    row_count, step_count = decode_inputs.shape[0], decode_inputs.shape[1]
    places = row_count * step_count
    place = jnp.stack([core, high, x, y, low])

    theirs, mine = partial_gradient(place, normed_inputs, value_cotangent)
    received = shift(theirs, "c", 1)
    swapped = swap_high(after(decode_inputs, theirs))

    rows = (4, 256, HD)
    own, *sent = small_call(
        core_sum_kernel, [(rows, F32)] + [(rows, BF16)] * 3, mine, received
    )
    along_x = [shift(sent[d - 1], "x", d) for d in (2, 1, 3)]
    attended_cache, fresh_weights = attend_cache(
        lengths, after(queries, own), new_keys.reshape(places, HD), cache_keys, cache_values
    )
    swapped = after(swapped, own)
    (both,) = small_call(
        join_kernel, [((2, places, D // 8), BF16)], swapped, shift(swapped, "zl", 1)
    )
    own, *along_x, both, attended_cache, fresh_weights = lax.optimization_barrier(
        (own, *along_x, both, attended_cache, fresh_weights)
    )
    rows = (256, HD)
    own, *sent = small_call(
        x_sum_kernel, [(rows, F32)] + [(rows, BF16)] * 3, own, *along_x
    )
    along_z = [shift(sent[e - 1], "zh", e) for e in (2, 1, 3)]
    both = after(both, own)
    near = exchange(both, "y", 1)
    own, *along_z, near = lax.optimization_barrier((own, *along_z, near))
    (updated,) = small_call(update_kernel, [(rows, BF16)], value_weight, own, *along_z)
    own = after(own, updated)
    (gradient,) = small_call(gradient_kernel, [(rows, F32)], own, *along_z, keep=False)

    (near,) = small_call(pair_kernel, [((4, places, D // 8), BF16)], after(both, updated), near)
    far = exchange(near, "y", 3)
    gathered = jnp.stack([updated] + [shift(updated, "x", -d) for d in (1, 2, 3)])
    gathered, gradient = lax.optimization_barrier((gathered, gradient))
    other = shift(gathered, "c", 1)
    partial = project(
        project_own_kernel, pltpu.VMEM((2 * places, HD), F32), 1, place, near, gathered
    )
    partial = project(
        project_rest_kernel,
        pltpu.VMEM((4, places, HD), BF16),
        2,
        place,
        near,
        far,
        gathered,
        other,
        partial,
    )
    exchanged = lax.all_to_all(partial, "zh", 0, 0, tiled=True)
    new_values, attended = finish(
        exchanged, attended_cache, fresh_weights, row_count, step_count
    )
    return (gradient, new_values, attended)


def solution(mesh):
    inner = Mesh(mesh.devices.reshape(tuple(SIZES.values())), NAMES)
    rows, columns = ("c", "zh", "x"), ("zl", "y")
    return jax.shard_map(
        shards,
        mesh=inner,
        in_specs=(
            P(rows, None),
            P(rows, columns),
            P(rows, columns),
            P(rows, None, columns),
            P(rows, None, columns),
            P(rows, None, columns),
            P(rows, None, columns),
            P(rows, None, columns),
            P(rows),
        ),
        out_specs=(
            P(rows, columns),
            P(rows, None, columns),
            P(rows, None, columns),
        ),
        check_vma=False,
    )
```

```python
import math

import jax
import jax.numpy as jnp
import numpy as np
from jax import lax
from jax.experimental import pallas as pl
from jax.experimental.pallas import tpu as pltpu
from jax.sharding import Mesh, PartitionSpec as P

D = 8192
HEADS = 8
HD = 128
SIZES = {"c": 2, "zh": 4, "x": 4, "zl": 2, "y": 4}
NAMES = tuple(SIZES)
STEP = 0.4 / math.sqrt(D)
MIB = 1 << 20
F32 = jnp.float32
BF16 = jnp.bfloat16
VMEM = pl.BlockSpec(memory_space=pltpu.VMEM)
SMEM = pl.BlockSpec(memory_space=pltpu.SMEM)
HBM = pl.BlockSpec(memory_space=pltpu.HBM)


def shift(value, axis, by):
    n = SIZES[axis]
    return lax.ppermute(value, axis, [(i, (i + by) % n) for i in range(n)])


def exchange(value, axis, bit):
    return lax.ppermute(value, axis, [(i, i ^ bit) for i in range(SIZES[axis])])


def swap_high(value):
    pairs = [(zh * 4 + y, y * 4 + (zh + y) % 4) for zh in range(4) for y in range(4)]
    return lax.ppermute(value, ("zh", "y"), pairs)


def after(value, *others):
    return lax.optimization_barrier((value, *others))[0]


def partial_kernel(place, x_hbm, v_hbm, theirs_ref, mine_ref, chunks, v_ref, sems):
    core, high, x = place[0], place[1], place[2]
    order = [(1 - core, theirs_ref, e) for e in range(4)] + [(core, mine_ref, e) for e in range(4)]
    copies = [pltpu.make_async_copy(v_hbm, v_ref, sems.at[8])]
    copies[0].start()
    for i, (half, _, e) in enumerate(order):
        column = (half * 4 + lax.rem(high + e, 4)) * 1024
        copies.append(
            pltpu.make_async_copy(
                x_hbm.at[:, pl.ds(pl.multiple_of(column, 1024), 1024)], chunks.at[i], sems.at[i]
            )
        )
        copies[-1].start()
    copies[0].wait()
    for i, (_, out_ref, e) in enumerate(order):
        copies[i + 1].wait()
        product = lax.dot_general(
            v_ref[...], chunks[i], (((0,), (0,)), ((), ())), preferred_element_type=F32
        )
        for block in range(4):
            rows = product[:, block * 256 : (block + 1) * 256].T
            out_ref[lax.rem(block + 4 - x, 4), e] = rows.astype(out_ref.dtype)


def partial_gradient(place, normed_inputs, value_cotangent):
    tokens = normed_inputs.shape[0]
    normed_inputs = pltpu.with_memory_space_constraint(normed_inputs, pltpu.HBM)
    value_cotangent = pltpu.with_memory_space_constraint(value_cotangent, pltpu.HBM)
    return pl.pallas_call(
        partial_kernel,
        in_specs=[SMEM, HBM, HBM],
        out_specs=[VMEM, VMEM],
        out_shape=[pltpu.VMEM((4, 4, 256, HD), BF16)] * 2,
        scratch_shapes=[
            pltpu.VMEM((8, tokens, 1024), BF16),
            pltpu.VMEM((tokens, HD), BF16),
            pltpu.SemaphoreType.DMA((9,)),
        ],
        compiler_params=pltpu.CompilerParams(vmem_limit_bytes=48 * MIB),
        cost_estimate=pl.CostEstimate(
            flops=2 * tokens * D * HD, bytes_accessed=tokens * D * 2, transcendentals=0
        ),
    )(place, normed_inputs, value_cotangent)


def small_call(kernel, outs, *args, keep=True):
    return pl.pallas_call(
        kernel,
        in_specs=[VMEM] * len(args),
        out_specs=[VMEM] * len(outs),
        out_shape=[
            (pltpu.VMEM if keep else jax.ShapeDtypeStruct)(shape, dtype) for shape, dtype in outs
        ],
        compiler_params=pltpu.CompilerParams(vmem_limit_bytes=16 * MIB),
        cost_estimate=pl.CostEstimate(flops=MIB, bytes_accessed=2 * MIB, transcendentals=0),
    )(*args)


def core_sum_kernel(mine, received, o0, o1, o2, o3):
    o0[...] = mine[0].astype(F32) + received[0].astype(F32)
    for d, out in ((1, o1), (2, o2), (3, o3)):
        out[...] = mine[d] + received[d]


def join_kernel(first, second, out):
    rows, steps = first.shape[0], first.shape[1]
    for i, ref in enumerate((first, second)):
        for r in range(rows):
            out[i, r * steps : (r + 1) * steps] = ref[r]


def pair_kernel(first, second, out):
    out[:2] = first[...]
    out[2:] = second[...]


def x_sum_kernel(own, r1, r2, r3, o0, o1, o2, o3):
    for e, out in enumerate((o0, o1, o2, o3)):
        total = own[e] + r1[e].astype(F32) + r2[e].astype(F32) + r3[e].astype(F32)
        out[...] = total.astype(out.dtype)


def total_of(own, r1, r2, r3):
    return own[...] + r1[...].astype(F32) + r2[...].astype(F32) + r3[...].astype(F32)


def update_kernel(weight, own, r1, r2, r3, updated):
    total = total_of(own, r1, r2, r3)
    updated[...] = (weight[...].astype(F32) - STEP * total).astype(BF16)


def gradient_kernel(own, r1, r2, r3, gradient):
    gradient[...] = total_of(own, r1, r2, r3)


def attend_kernel(
    lengths, raw_queries, new_keys, cache_keys, cache_values, mixed_ref, weights_ref, queries
):
    rows = cache_keys.shape[0]
    slots = cache_keys.shape[1]
    steps = raw_queries.shape[1]
    every = HEADS * rows * steps
    factor = 1.0 / math.sqrt(HD)
    for r in range(rows):
        queries[r * steps : (r + 1) * steps] = raw_queries[r]
    heads = jnp.concatenate([queries[:, q * HD : (q + 1) * HD] for q in range(HEADS)], axis=0)
    place = lax.broadcasted_iota(jnp.int32, (every, slots), 0) % (rows * steps)
    lane = lax.broadcasted_iota(jnp.int32, (every, slots), 1)
    row = place // steps
    contract = (((1,), (1,)), ((), ()))
    scores = jnp.full((every, slots), -1e30, F32)
    for r in range(rows):
        product = lax.dot_general(heads, cache_keys[r], contract, preferred_element_type=F32)
        scores = jnp.where((row == r) & (lane < lengths[r]), product * factor, scores)
    fresh = lax.dot_general(heads, new_keys[...], contract, preferred_element_type=F32) * factor
    from_place, to_place = place[:, : rows * steps], lane[:, : rows * steps]
    visible = (from_place // steps == to_place // steps) & (to_place <= from_place)
    fresh = jnp.where(visible, fresh, -1e30)
    highest = jnp.maximum(
        jnp.max(scores, axis=1, keepdims=True), jnp.max(fresh, axis=1, keepdims=True)
    )
    cache_exp = jnp.exp(scores - highest)
    fresh_exp = jnp.exp(fresh - highest)
    total = jnp.sum(cache_exp, axis=1, keepdims=True) + jnp.sum(fresh_exp, axis=1, keepdims=True)
    cache_weights = (cache_exp / total).astype(BF16)
    weights_ref[...] = (fresh_exp / total).astype(BF16)
    mixed = jnp.zeros((every, HD), F32)
    for r in range(rows):
        product = jnp.dot(cache_weights, cache_values[r], preferred_element_type=F32)
        mixed = jnp.where(row == r, product, mixed)
    mixed_ref[...] = mixed


def attend_cache(lengths, queries, new_keys, cache_keys, cache_values):
    places = queries.shape[0] * queries.shape[1]
    return pl.pallas_call(
        attend_kernel,
        in_specs=[SMEM] + [VMEM] * 4,
        out_specs=[VMEM, VMEM],
        out_shape=[
            jax.ShapeDtypeStruct((HEADS * places, HD), F32),
            jax.ShapeDtypeStruct((HEADS * places, places), BF16),
        ],
        scratch_shapes=[pltpu.VMEM((places, HEADS * HD), BF16)],
        compiler_params=pltpu.CompilerParams(vmem_limit_bytes=16 * MIB),
        cost_estimate=pl.CostEstimate(
            flops=8000 * MIB, bytes_accessed=20 * MIB, transcendentals=0
        ),
    )(lengths, queries, new_keys, cache_keys, cache_values)


def fill_rows(rows, x, updated):
    for d in range(4):
        rows[pl.ds(pl.multiple_of(lax.rem(x + d, 4) * 256, 256), 256), :] = updated[d]


def tokens_of(place, bits):
    return lax.rem(jnp.bitwise_xor(place[3], bits) + 4 - place[1], 4)


def project_own_kernel(place, near, u, out_ref, rows):
    own = jnp.where(place[0] == place[4], 0, 1)
    fill_rows(rows, place[2], u)
    inputs = jnp.concatenate([near[own], near[2 + own]], axis=0)
    out_ref[...] = jnp.dot(inputs, rows[...], preferred_element_type=F32)


def project_rest_kernel(place, near, far, u_own, u_other, start, out_ref, rows, last):
    own = jnp.where(place[0] == place[4], 0, 1)
    fill_rows(last, place[2], u_own)
    fill_rows(rows, place[2], u_other)
    inputs = [near[1 - own], near[3 - own], far[1 - own], far[3 - own]]
    product = jnp.dot(
        jnp.concatenate(inputs, axis=0), rows[...], preferred_element_type=F32
    )
    inputs = jnp.concatenate([far[own], far[2 + own]], axis=0)
    more = jnp.dot(inputs, last[...], preferred_element_type=F32)
    size = far.shape[1]
    for i, bits in enumerate((0, 1, 3, 2)):
        rest = start[i * size : (i + 1) * size] if i < 2 else more[(i - 2) * size : (i - 1) * size]
        total = product[i * size : (i + 1) * size] + rest
        out_ref[tokens_of(place, bits)] = total.astype(out_ref.dtype)


def project(kernel, out_shape, scratches, place, *args):
    return pl.pallas_call(
        kernel,
        in_specs=[SMEM] + [VMEM] * len(args),
        out_specs=VMEM,
        out_shape=out_shape,
        scratch_shapes=[pltpu.VMEM((1024, HD), BF16)] * scratches,
        compiler_params=pltpu.CompilerParams(vmem_limit_bytes=16 * MIB),
        cost_estimate=pl.CostEstimate(
            flops=2 * 256 * 1024 * HD, bytes_accessed=3 * MIB // 4, transcendentals=0
        ),
    )(place, *args)


def finish_kernel(parts, mixed, weights, values_ref, attended_ref):
    steps = values_ref.shape[1]
    total = parts[0].astype(F32)
    for i in range(1, 4):
        total += parts[i].astype(F32)
    values = total.astype(BF16)
    for r in range(values_ref.shape[0]):
        values_ref[r] = values[r * steps : (r + 1) * steps]
    places = values.shape[0]
    for q in range(HEADS):
        span = slice(q * places, (q + 1) * places)
        head = mixed[span] + jnp.dot(weights[span], values, preferred_element_type=F32)
        head = head.astype(BF16)
        for r in range(values_ref.shape[0]):
            attended_ref[r, :, q * HD : (q + 1) * HD] = head[r * steps : (r + 1) * steps]


def finish(parts, mixed, weights, rows, steps):
    return pl.pallas_call(
        finish_kernel,
        in_specs=[VMEM] * 3,
        out_specs=[VMEM, VMEM],
        out_shape=[
            jax.ShapeDtypeStruct((rows, steps, HD), BF16),
            jax.ShapeDtypeStruct((rows, steps, HEADS * HD), BF16),
        ],
        compiler_params=pltpu.CompilerParams(vmem_limit_bytes=16 * MIB),
    )(parts, mixed, weights)


def shards(
    normed_inputs,
    value_cotangent,
    value_weight,
    decode_inputs,
    queries,
    new_keys,
    cache_keys,
    cache_values,
    lengths,
):
    core, high, x, low, y = (lax.axis_index(n) for n in NAMES)
    row_count, step_count = decode_inputs.shape[0], decode_inputs.shape[1]
    places = row_count * step_count
    place = jnp.stack([core, high, x, y, low])

    theirs, mine = partial_gradient(place, normed_inputs, value_cotangent)
    received = shift(theirs, "c", 1)
    swapped = swap_high(after(decode_inputs, theirs))

    rows = (4, 256, HD)
    own, *sent = small_call(
        core_sum_kernel, [(rows, F32)] + [(rows, BF16)] * 3, mine, received
    )
    along_x = [shift(sent[d - 1], "x", d) for d in (2, 1, 3)]
    swapped = after(swapped, own)
    (both,) = small_call(
        join_kernel, [((2, places, D // 8), BF16)], swapped, shift(swapped, "zl", 1)
    )
    near = exchange(both, "y", 1)

    own, *along_x, both = lax.optimization_barrier((own, *along_x, both))
    rows = (256, HD)
    own, *sent = small_call(
        x_sum_kernel, [(rows, F32)] + [(rows, BF16)] * 3, own, *along_x
    )
    along_z = [shift(sent[e - 1], "zh", e) for e in (2, 1, 3)]
    attended_cache, fresh_weights = attend_cache(
        lengths, after(queries, own), new_keys.reshape(places, HD), cache_keys, cache_values
    )
    own, *along_z, near, attended_cache, fresh_weights = lax.optimization_barrier(
        (own, *along_z, near, attended_cache, fresh_weights)
    )
    (updated,) = small_call(update_kernel, [(rows, BF16)], value_weight, own, *along_z)
    own = after(own, updated)
    (gradient,) = small_call(gradient_kernel, [(rows, F32)], own, *along_z, keep=False)

    (near,) = small_call(pair_kernel, [((4, places, D // 8), BF16)], after(both, updated), near)
    far = exchange(near, "y", 3)
    gathered = jnp.stack([updated] + [shift(updated, "x", -d) for d in (1, 2, 3)])
    gathered, gradient = lax.optimization_barrier((gathered, gradient))
    other = shift(gathered, "c", 1)
    partial = project(
        project_own_kernel, pltpu.VMEM((2 * places, HD), F32), 1, place, near, gathered
    )
    partial = project(
        project_rest_kernel,
        pltpu.VMEM((4, places, HD), BF16),
        2,
        place,
        near,
        far,
        gathered,
        other,
        partial,
    )
    exchanged = lax.all_to_all(partial, "zh", 0, 0, tiled=True)
    new_values, attended = finish(
        exchanged, attended_cache, fresh_weights, row_count, step_count
    )
    return (gradient, new_values, attended)


def solution(mesh):
    inner = Mesh(mesh.devices.reshape(tuple(SIZES.values())), NAMES)
    rows, columns = ("c", "zh", "x"), ("zl", "y")
    return jax.shard_map(
        shards,
        mesh=inner,
        in_specs=(
            P(rows, None),
            P(rows, columns),
            P(rows, columns),
            P(rows, None, columns),
            P(rows, None, columns),
            P(rows, None, columns),
            P(rows, None, columns),
            P(rows, None, columns),
            P(rows),
        ),
        out_specs=(
            P(rows, columns),
            P(rows, None, columns),
            P(rows, None, columns),
        ),
        check_vma=False,
    )
```

```python
import math

import jax
import jax.numpy as jnp
import numpy as np
from jax import lax
from jax.experimental import pallas as pl
from jax.experimental.pallas import tpu as pltpu
from jax.sharding import Mesh, PartitionSpec as P

D = 8192
HEADS = 8
HD = 128
SIZES = {"c": 2, "zh": 4, "x": 4, "zl": 2, "y": 4}
NAMES = tuple(SIZES)
STEP = 0.4 / math.sqrt(D)
MIB = 1 << 20
F32 = jnp.float32
BF16 = jnp.bfloat16
VMEM = pl.BlockSpec(memory_space=pltpu.VMEM)
SMEM = pl.BlockSpec(memory_space=pltpu.SMEM)
HBM = pl.BlockSpec(memory_space=pltpu.HBM)


def shift(value, axis, by):
    n = SIZES[axis]
    return lax.ppermute(value, axis, [(i, (i + by) % n) for i in range(n)])


def exchange(value, axis, bit):
    return lax.ppermute(value, axis, [(i, i ^ bit) for i in range(SIZES[axis])])


def swap_high(value):
    pairs = [(zh * 4 + y, y * 4 + (zh + y) % 4) for zh in range(4) for y in range(4)]
    return lax.ppermute(value, ("zh", "y"), pairs)


def after(value, *others):
    return lax.optimization_barrier((value, *others))[0]


def partial_kernel(place, x_hbm, v_hbm, theirs_ref, mine_ref, chunks, v_ref, sems):
    core, high, x = place[0], place[1], place[2]
    order = [(1 - core, theirs_ref, e) for e in range(4)] + [(core, mine_ref, e) for e in range(4)]
    copies = [pltpu.make_async_copy(v_hbm, v_ref, sems.at[8])]
    copies[0].start()
    for i, (half, _, e) in enumerate(order):
        column = (half * 4 + lax.rem(high + e, 4)) * 1024
        copies.append(
            pltpu.make_async_copy(
                x_hbm.at[:, pl.ds(pl.multiple_of(column, 1024), 1024)], chunks.at[i], sems.at[i]
            )
        )
        copies[-1].start()
    copies[0].wait()
    for i, (_, out_ref, e) in enumerate(order):
        copies[i + 1].wait()
        product = lax.dot_general(
            v_ref[...], chunks[i], (((0,), (0,)), ((), ())), preferred_element_type=F32
        )
        for block in range(4):
            rows = product[:, block * 256 : (block + 1) * 256].T
            out_ref[lax.rem(block + 4 - x, 4), e] = rows.astype(out_ref.dtype)


def partial_gradient(place, normed_inputs, value_cotangent):
    tokens = normed_inputs.shape[0]
    normed_inputs = pltpu.with_memory_space_constraint(normed_inputs, pltpu.HBM)
    value_cotangent = pltpu.with_memory_space_constraint(value_cotangent, pltpu.HBM)
    return pl.pallas_call(
        partial_kernel,
        in_specs=[SMEM, HBM, HBM],
        out_specs=[VMEM, VMEM],
        out_shape=[pltpu.VMEM((4, 4, 256, HD), BF16)] * 2,
        scratch_shapes=[
            pltpu.VMEM((8, tokens, 1024), BF16),
            pltpu.VMEM((tokens, HD), BF16),
            pltpu.SemaphoreType.DMA((9,)),
        ],
        compiler_params=pltpu.CompilerParams(vmem_limit_bytes=48 * MIB),
        cost_estimate=pl.CostEstimate(
            flops=2 * tokens * D * HD, bytes_accessed=tokens * D * 2, transcendentals=0
        ),
    )(place, normed_inputs, value_cotangent)


def small_call(kernel, outs, *args, keep=True, flops=MIB):
    return pl.pallas_call(
        kernel,
        in_specs=[VMEM] * len(args),
        out_specs=[VMEM] * len(outs),
        out_shape=[
            (pltpu.VMEM if keep else jax.ShapeDtypeStruct)(shape, dtype) for shape, dtype in outs
        ],
        compiler_params=pltpu.CompilerParams(vmem_limit_bytes=16 * MIB),
        cost_estimate=pl.CostEstimate(flops=flops, bytes_accessed=2 * MIB, transcendentals=0),
    )(*args)


def core_sum_kernel(mine, received, o0, o1, o2, o3):
    o0[...] = mine[0].astype(F32) + received[0].astype(F32)
    for d, out in ((1, o1), (2, o2), (3, o3)):
        out[...] = mine[d] + received[d]


def join_kernel(first, second, out):
    rows, steps = first.shape[0], first.shape[1]
    for i, ref in enumerate((first, second)):
        for r in range(rows):
            out[i, r * steps : (r + 1) * steps] = ref[r]


def pair_kernel(first, second, out):
    out[:2] = first[...]
    out[2:] = second[...]


def x_sum_kernel(own, r1, r2, r3, o0, o1, o2, o3):
    for e, out in enumerate((o0, o1, o2, o3)):
        total = own[e] + r1[e].astype(F32) + r2[e].astype(F32) + r3[e].astype(F32)
        out[...] = total.astype(out.dtype)


def total_of(own, r1, r2, r3):
    return own[...] + r1[...].astype(F32) + r2[...].astype(F32) + r3[...].astype(F32)


def update_kernel(weight, own, r1, r2, r3, updated):
    total = total_of(own, r1, r2, r3)
    updated[...] = (weight[...].astype(F32) - STEP * total).astype(BF16)


def gradient_kernel(own, r1, r2, r3, gradient):
    gradient[...] = total_of(own, r1, r2, r3)


def attend_kernel(
    lengths, raw_queries, new_keys, cache_keys, cache_values, mixed_ref, weights_ref, queries
):
    rows = cache_keys.shape[0]
    slots = cache_keys.shape[1]
    steps = raw_queries.shape[1]
    every = HEADS * rows * steps
    factor = 1.0 / math.sqrt(HD)
    for r in range(rows):
        queries[r * steps : (r + 1) * steps] = raw_queries[r]
    heads = jnp.concatenate([queries[:, q * HD : (q + 1) * HD] for q in range(HEADS)], axis=0)
    place = lax.broadcasted_iota(jnp.int32, (every, slots), 0) % (rows * steps)
    lane = lax.broadcasted_iota(jnp.int32, (every, slots), 1)
    row = place // steps
    contract = (((1,), (1,)), ((), ()))
    scores = jnp.full((every, slots), -1e30, F32)
    for r in range(rows):
        product = lax.dot_general(heads, cache_keys[r], contract, preferred_element_type=F32)
        scores = jnp.where((row == r) & (lane < lengths[r]), product * factor, scores)
    fresh = lax.dot_general(heads, new_keys[...], contract, preferred_element_type=F32) * factor
    from_place, to_place = place[:, : rows * steps], lane[:, : rows * steps]
    visible = (from_place // steps == to_place // steps) & (to_place <= from_place)
    fresh = jnp.where(visible, fresh, -1e30)
    highest = jnp.maximum(
        jnp.max(scores, axis=1, keepdims=True), jnp.max(fresh, axis=1, keepdims=True)
    )
    cache_exp = jnp.exp(scores - highest)
    fresh_exp = jnp.exp(fresh - highest)
    total = jnp.sum(cache_exp, axis=1, keepdims=True) + jnp.sum(fresh_exp, axis=1, keepdims=True)
    cache_weights = (cache_exp / total).astype(BF16)
    weights_ref[...] = (fresh_exp / total).astype(BF16)
    mixed = jnp.zeros((every, HD), F32)
    for r in range(rows):
        product = jnp.dot(cache_weights, cache_values[r], preferred_element_type=F32)
        mixed = jnp.where(row == r, product, mixed)
    mixed_ref[...] = mixed


def attend_cache(lengths, queries, new_keys, cache_keys, cache_values):
    places = queries.shape[0] * queries.shape[1]
    return pl.pallas_call(
        attend_kernel,
        in_specs=[SMEM] + [VMEM] * 4,
        out_specs=[VMEM, VMEM],
        out_shape=[
            jax.ShapeDtypeStruct((HEADS * places, HD), F32),
            jax.ShapeDtypeStruct((HEADS * places, places), BF16),
        ],
        scratch_shapes=[pltpu.VMEM((places, HEADS * HD), BF16)],
        compiler_params=pltpu.CompilerParams(vmem_limit_bytes=16 * MIB),
        cost_estimate=pl.CostEstimate(
            flops=8000 * MIB, bytes_accessed=20 * MIB, transcendentals=0
        ),
    )(lengths, queries, new_keys, cache_keys, cache_values)


def fill_rows(rows, x, updated):
    for d in range(4):
        rows[pl.ds(pl.multiple_of(lax.rem(x + d, 4) * 256, 256), 256), :] = updated[d]


def tokens_of(place, bits):
    return lax.rem(jnp.bitwise_xor(place[3], bits) + 4 - place[1], 4)


def project_own_kernel(place, near, u, out_ref, rows):
    own = jnp.where(place[0] == place[4], 0, 1)
    fill_rows(rows, place[2], u)
    inputs = jnp.concatenate([near[own], near[2 + own]], axis=0)
    out_ref[...] = jnp.dot(inputs, rows[...], preferred_element_type=F32)


def project_rest_kernel(place, near, far, u_own, u_other, start, out_ref, rows, last):
    own = jnp.where(place[0] == place[4], 0, 1)
    fill_rows(last, place[2], u_own)
    fill_rows(rows, place[2], u_other)
    inputs = [near[1 - own], near[3 - own], far[1 - own], far[3 - own]]
    product = jnp.dot(
        jnp.concatenate(inputs, axis=0), rows[...], preferred_element_type=F32
    )
    inputs = jnp.concatenate([far[own], far[2 + own]], axis=0)
    more = jnp.dot(inputs, last[...], preferred_element_type=F32)
    size = far.shape[1]
    for i, bits in enumerate((0, 1, 3, 2)):
        rest = start[i * size : (i + 1) * size] if i < 2 else more[(i - 2) * size : (i - 1) * size]
        total = product[i * size : (i + 1) * size] + rest
        out_ref[tokens_of(place, bits)] = total.astype(out_ref.dtype)


def project(kernel, out_shape, scratches, place, *args):
    return pl.pallas_call(
        kernel,
        in_specs=[SMEM] + [VMEM] * len(args),
        out_specs=VMEM,
        out_shape=out_shape,
        scratch_shapes=[pltpu.VMEM((1024, HD), BF16)] * scratches,
        compiler_params=pltpu.CompilerParams(vmem_limit_bytes=16 * MIB),
        cost_estimate=pl.CostEstimate(
            flops=2 * 256 * 1024 * HD, bytes_accessed=3 * MIB // 4, transcendentals=0
        ),
    )(place, *args)


def finish_kernel(parts, mixed, weights, values_ref, attended_ref):
    steps = values_ref.shape[1]
    total = parts[0].astype(F32)
    for i in range(1, 4):
        total += parts[i].astype(F32)
    values = total.astype(BF16)
    for r in range(values_ref.shape[0]):
        values_ref[r] = values[r * steps : (r + 1) * steps]
    places = values.shape[0]
    for q in range(HEADS):
        span = slice(q * places, (q + 1) * places)
        head = mixed[span] + jnp.dot(weights[span], values, preferred_element_type=F32)
        head = head.astype(BF16)
        for r in range(values_ref.shape[0]):
            attended_ref[r, :, q * HD : (q + 1) * HD] = head[r * steps : (r + 1) * steps]


def finish(parts, mixed, weights, rows, steps):
    return pl.pallas_call(
        finish_kernel,
        in_specs=[VMEM] * 3,
        out_specs=[VMEM, VMEM],
        out_shape=[
            jax.ShapeDtypeStruct((rows, steps, HD), BF16),
            jax.ShapeDtypeStruct((rows, steps, HEADS * HD), BF16),
        ],
        compiler_params=pltpu.CompilerParams(vmem_limit_bytes=16 * MIB),
    )(parts, mixed, weights)


def shards(
    normed_inputs,
    value_cotangent,
    value_weight,
    decode_inputs,
    queries,
    new_keys,
    cache_keys,
    cache_values,
    lengths,
):
    core, high, x, low, y = (lax.axis_index(n) for n in NAMES)
    row_count, step_count = decode_inputs.shape[0], decode_inputs.shape[1]
    places = row_count * step_count
    place = jnp.stack([core, high, x, y, low])

    theirs, mine = partial_gradient(place, normed_inputs, value_cotangent)
    received = shift(theirs, "c", 1)
    swapped = swap_high(after(decode_inputs, theirs))

    rows = (4, 256, HD)
    own, *sent = small_call(
        core_sum_kernel, [(rows, F32)] + [(rows, BF16)] * 3, mine, received
    )
    along_x = [shift(sent[d - 1], "x", d) for d in (2, 1, 3)]
    swapped = after(swapped, own)
    (both,) = small_call(
        join_kernel, [((2, places, D // 8), BF16)], swapped, shift(swapped, "zl", 1)
    )
    near = exchange(both, "y", 1)

    own, *along_x, both = lax.optimization_barrier((own, *along_x, both))
    rows = (256, HD)
    own, *sent = small_call(
        x_sum_kernel, [(rows, F32)] + [(rows, BF16)] * 3, own, *along_x, flops=8000 * MIB
    )
    along_z = [shift(sent[e - 1], "zh", e) for e in (2, 1, 3)]
    (near,) = small_call(pair_kernel, [((4, places, D // 8), BF16)], after(both, own), near)
    far = exchange(near, "y", 3)
    attended_cache, fresh_weights = attend_cache(
        lengths, after(queries, near), new_keys.reshape(places, HD), cache_keys, cache_values
    )
    own, *along_z, attended_cache, fresh_weights = lax.optimization_barrier(
        (own, *along_z, attended_cache, fresh_weights)
    )
    (updated,) = small_call(update_kernel, [(rows, BF16)], value_weight, own, *along_z)
    own = after(own, updated)
    (gradient,) = small_call(gradient_kernel, [(rows, F32)], own, *along_z, keep=False)

    gathered = jnp.stack([updated] + [shift(updated, "x", -d) for d in (1, 2, 3)])
    gathered, gradient = lax.optimization_barrier((gathered, gradient))
    other = shift(gathered, "c", 1)
    partial = project(
        project_own_kernel, pltpu.VMEM((2 * places, HD), F32), 1, place, near, gathered
    )
    partial = project(
        project_rest_kernel,
        pltpu.VMEM((4, places, HD), BF16),
        2,
        place,
        near,
        far,
        gathered,
        other,
        partial,
    )
    exchanged = lax.all_to_all(partial, "zh", 0, 0, tiled=True)
    new_values, attended = finish(
        exchanged, attended_cache, fresh_weights, row_count, step_count
    )
    return (gradient, new_values, attended)


def solution(mesh):
    inner = Mesh(mesh.devices.reshape(tuple(SIZES.values())), NAMES)
    rows, columns = ("c", "zh", "x"), ("zl", "y")
    return jax.shard_map(
        shards,
        mesh=inner,
        in_specs=(
            P(rows, None),
            P(rows, columns),
            P(rows, columns),
            P(rows, None, columns),
            P(rows, None, columns),
            P(rows, None, columns),
            P(rows, None, columns),
            P(rows, None, columns),
            P(rows),
        ),
        out_specs=(
            P(rows, columns),
            P(rows, None, columns),
            P(rows, None, columns),
        ),
        check_vma=False,
    )
```

```python
import math

import jax
import jax.numpy as jnp
import numpy as np
from jax import lax
from jax.experimental import pallas as pl
from jax.experimental.pallas import tpu as pltpu
from jax.sharding import Mesh, PartitionSpec as P

D = 8192
HEADS = 8
HD = 128
SIZES = {"c": 2, "zh": 4, "x": 4, "zl": 2, "y": 4}
NAMES = tuple(SIZES)
STEP = 0.4 / math.sqrt(D)
MIB = 1 << 20
F32 = jnp.float32
BF16 = jnp.bfloat16
VMEM = pl.BlockSpec(memory_space=pltpu.VMEM)
SMEM = pl.BlockSpec(memory_space=pltpu.SMEM)
HBM = pl.BlockSpec(memory_space=pltpu.HBM)


def shift(value, axis, by):
    n = SIZES[axis]
    return lax.ppermute(value, axis, [(i, (i + by) % n) for i in range(n)])


def exchange(value, axis, bit):
    return lax.ppermute(value, axis, [(i, i ^ bit) for i in range(SIZES[axis])])


def swap_high(value):
    pairs = [(zh * 4 + y, y * 4 + (zh + y) % 4) for zh in range(4) for y in range(4)]
    return lax.ppermute(value, ("zh", "y"), pairs)


def after(value, *others):
    return lax.optimization_barrier((value, *others))[0]


def partial_kernel(place, x_hbm, v_hbm, theirs_ref, mine_ref, chunks, v_ref, sems):
    core, high, x = place[0], place[1], place[2]
    order = [(1 - core, theirs_ref, e) for e in range(4)] + [(core, mine_ref, e) for e in range(4)]
    copies = [pltpu.make_async_copy(v_hbm, v_ref, sems.at[8])]
    copies[0].start()
    for i, (half, _, e) in enumerate(order):
        column = (half * 4 + lax.rem(high + e, 4)) * 1024
        copies.append(
            pltpu.make_async_copy(
                x_hbm.at[:, pl.ds(pl.multiple_of(column, 1024), 1024)], chunks.at[i], sems.at[i]
            )
        )
        copies[-1].start()
    copies[0].wait()
    for i, (_, out_ref, e) in enumerate(order):
        copies[i + 1].wait()
        product = lax.dot_general(
            v_ref[...], chunks[i], (((0,), (0,)), ((), ())), preferred_element_type=F32
        )
        for block in range(4):
            rows = product[:, block * 256 : (block + 1) * 256].T
            out_ref[lax.rem(block + 4 - x, 4), e] = rows.astype(out_ref.dtype)


def partial_gradient(place, normed_inputs, value_cotangent):
    tokens = normed_inputs.shape[0]
    normed_inputs = pltpu.with_memory_space_constraint(normed_inputs, pltpu.HBM)
    value_cotangent = pltpu.with_memory_space_constraint(value_cotangent, pltpu.HBM)
    return pl.pallas_call(
        partial_kernel,
        in_specs=[SMEM, HBM, HBM],
        out_specs=[VMEM, VMEM],
        out_shape=[pltpu.VMEM((4, 4, 256, HD), BF16)] * 2,
        scratch_shapes=[
            pltpu.VMEM((8, tokens, 1024), BF16),
            pltpu.VMEM((tokens, HD), BF16),
            pltpu.SemaphoreType.DMA((9,)),
        ],
        compiler_params=pltpu.CompilerParams(vmem_limit_bytes=48 * MIB),
        cost_estimate=pl.CostEstimate(
            flops=2 * tokens * D * HD, bytes_accessed=tokens * D * 2, transcendentals=0
        ),
    )(place, normed_inputs, value_cotangent)


def small_call(kernel, outs, *args, keep=True, flops=MIB):
    return pl.pallas_call(
        kernel,
        in_specs=[VMEM] * len(args),
        out_specs=[VMEM] * len(outs),
        out_shape=[
            (pltpu.VMEM if keep else jax.ShapeDtypeStruct)(shape, dtype) for shape, dtype in outs
        ],
        compiler_params=pltpu.CompilerParams(vmem_limit_bytes=16 * MIB),
        cost_estimate=pl.CostEstimate(flops=flops, bytes_accessed=2 * MIB, transcendentals=0),
    )(*args)


def core_sum_kernel(mine, received, o0, o1, o2, o3):
    o0[...] = mine[0].astype(F32) + received[0].astype(F32)
    for d, out in ((1, o1), (2, o2), (3, o3)):
        out[...] = mine[d] + received[d]


def join_kernel(first, second, out):
    rows, steps = first.shape[0], first.shape[1]
    for i, ref in enumerate((first, second)):
        for r in range(rows):
            out[i, r * steps : (r + 1) * steps] = ref[r]


def pair_kernel(first, second, out):
    out[:2] = first[...]
    out[2:] = second[...]


def x_sum_kernel(own, r1, r2, r3, o0, o1, o2, o3):
    for e, out in enumerate((o0, o1, o2, o3)):
        total = own[e] + r1[e].astype(F32) + r2[e].astype(F32) + r3[e].astype(F32)
        out[...] = total.astype(out.dtype)


def total_of(own, r1, r2, r3):
    return own[...] + r1[...].astype(F32) + r2[...].astype(F32) + r3[...].astype(F32)


def update_kernel(weight, own, r1, r2, r3, updated):
    total = total_of(own, r1, r2, r3)
    updated[...] = (weight[...].astype(F32) - STEP * total).astype(BF16)


def gradient_kernel(own, r1, r2, r3, gradient):
    gradient[...] = total_of(own, r1, r2, r3)


def attend_kernel(
    lengths, raw_queries, new_keys, cache_keys, cache_values, mixed_ref, weights_ref, queries
):
    rows = cache_keys.shape[0]
    slots = cache_keys.shape[1]
    steps = raw_queries.shape[1]
    every = HEADS * rows * steps
    factor = 1.0 / math.sqrt(HD)
    for r in range(rows):
        queries[r * steps : (r + 1) * steps] = raw_queries[r]
    heads = jnp.concatenate([queries[:, q * HD : (q + 1) * HD] for q in range(HEADS)], axis=0)
    place = lax.broadcasted_iota(jnp.int32, (every, slots), 0) % (rows * steps)
    lane = lax.broadcasted_iota(jnp.int32, (every, slots), 1)
    row = place // steps
    contract = (((1,), (1,)), ((), ()))
    scores = jnp.full((every, slots), -1e30, F32)
    for r in range(rows):
        product = lax.dot_general(heads, cache_keys[r], contract, preferred_element_type=F32)
        scores = jnp.where((row == r) & (lane < lengths[r]), product * factor, scores)
    fresh = lax.dot_general(heads, new_keys[...], contract, preferred_element_type=F32) * factor
    from_place, to_place = place[:, : rows * steps], lane[:, : rows * steps]
    visible = (from_place // steps == to_place // steps) & (to_place <= from_place)
    fresh = jnp.where(visible, fresh, -1e30)
    highest = jnp.maximum(
        jnp.max(scores, axis=1, keepdims=True), jnp.max(fresh, axis=1, keepdims=True)
    )
    cache_exp = jnp.exp(scores - highest)
    fresh_exp = jnp.exp(fresh - highest)
    total = jnp.sum(cache_exp, axis=1, keepdims=True) + jnp.sum(fresh_exp, axis=1, keepdims=True)
    cache_weights = (cache_exp / total).astype(BF16)
    weights_ref[...] = (fresh_exp / total).astype(BF16)
    mixed = jnp.zeros((every, HD), F32)
    for r in range(rows):
        product = jnp.dot(cache_weights, cache_values[r], preferred_element_type=F32)
        mixed = jnp.where(row == r, product, mixed)
    mixed_ref[...] = mixed


def attend_cache(lengths, queries, new_keys, cache_keys, cache_values):
    places = queries.shape[0] * queries.shape[1]
    return pl.pallas_call(
        attend_kernel,
        in_specs=[SMEM] + [VMEM] * 4,
        out_specs=[VMEM, VMEM],
        out_shape=[
            jax.ShapeDtypeStruct((HEADS * places, HD), F32),
            jax.ShapeDtypeStruct((HEADS * places, places), BF16),
        ],
        scratch_shapes=[pltpu.VMEM((places, HEADS * HD), BF16)],
        compiler_params=pltpu.CompilerParams(vmem_limit_bytes=16 * MIB),
        cost_estimate=pl.CostEstimate(
            flops=1 * MIB, bytes_accessed=MIB // 4, transcendentals=0
        ),
    )(lengths, queries, new_keys, cache_keys, cache_values)


def fill_rows(rows, x, updated):
    for d in range(4):
        rows[pl.ds(pl.multiple_of(lax.rem(x + d, 4) * 256, 256), 256), :] = updated[d]


def tokens_of(place, bits):
    return lax.rem(jnp.bitwise_xor(place[3], bits) + 4 - place[1], 4)


def arrange_kernel(place, near, own_ref, rest_ref):
    own = jnp.where(place[0] == place[4], 0, 1)
    size = near.shape[1]
    for i in range(2):
        own_ref[i * size : (i + 1) * size] = near[2 * i + own]
        rest_ref[i * size : (i + 1) * size] = near[2 * i + 1 - own]


def arrange(place, near):
    shape = jax.ShapeDtypeStruct((2 * near.shape[1], near.shape[2]), BF16)
    return pl.pallas_call(
        arrange_kernel,
        in_specs=[SMEM, VMEM],
        out_specs=[VMEM, VMEM],
        out_shape=[shape, shape],
        compiler_params=pltpu.CompilerParams(vmem_limit_bytes=16 * MIB),
        cost_estimate=pl.CostEstimate(
            flops=8000 * MIB, bytes_accessed=2 * MIB, transcendentals=0
        ),
    )(place, near)


def project_own_kernel(place, inputs, u, out_ref, rows):
    fill_rows(rows, place[2], u)
    out_ref[...] = jnp.dot(inputs[...], rows[...], preferred_element_type=F32)


def project_rest_kernel(place, near, far, u_own, u_other, start, out_ref, rows, last):
    own = jnp.where(place[0] == place[4], 0, 1)
    fill_rows(last, place[2], u_own)
    fill_rows(rows, place[2], u_other)
    inputs = jnp.concatenate([near[...], far[1 - own], far[3 - own]], axis=0)
    product = jnp.dot(inputs, rows[...], preferred_element_type=F32)
    inputs = jnp.concatenate([far[own], far[2 + own]], axis=0)
    more = jnp.dot(inputs, last[...], preferred_element_type=F32)
    size = far.shape[1]
    for i, bits in enumerate((0, 1, 3, 2)):
        rest = start[i * size : (i + 1) * size] if i < 2 else more[(i - 2) * size : (i - 1) * size]
        total = product[i * size : (i + 1) * size] + rest
        out_ref[tokens_of(place, bits)] = total.astype(out_ref.dtype)


def project(kernel, out_shape, scratches, place, *args):
    return pl.pallas_call(
        kernel,
        in_specs=[SMEM] + [VMEM] * len(args),
        out_specs=VMEM,
        out_shape=out_shape,
        scratch_shapes=[pltpu.VMEM((1024, HD), BF16)] * scratches,
        compiler_params=pltpu.CompilerParams(vmem_limit_bytes=16 * MIB),
        cost_estimate=pl.CostEstimate(
            flops=2 * 256 * 1024 * HD, bytes_accessed=3 * MIB // 4, transcendentals=0
        ),
    )(place, *args)


def finish_kernel(parts, mixed, weights, values_ref, attended_ref):
    steps = values_ref.shape[1]
    total = parts[0].astype(F32)
    for i in range(1, 4):
        total += parts[i].astype(F32)
    values = total.astype(BF16)
    for r in range(values_ref.shape[0]):
        values_ref[r] = values[r * steps : (r + 1) * steps]
    places = values.shape[0]
    for q in range(HEADS):
        span = slice(q * places, (q + 1) * places)
        head = mixed[span] + jnp.dot(weights[span], values, preferred_element_type=F32)
        head = head.astype(BF16)
        for r in range(values_ref.shape[0]):
            attended_ref[r, :, q * HD : (q + 1) * HD] = head[r * steps : (r + 1) * steps]


def finish(parts, mixed, weights, rows, steps):
    return pl.pallas_call(
        finish_kernel,
        in_specs=[VMEM] * 3,
        out_specs=[VMEM, VMEM],
        out_shape=[
            jax.ShapeDtypeStruct((rows, steps, HD), BF16),
            jax.ShapeDtypeStruct((rows, steps, HEADS * HD), BF16),
        ],
        compiler_params=pltpu.CompilerParams(vmem_limit_bytes=16 * MIB),
    )(parts, mixed, weights)


def shards(
    normed_inputs,
    value_cotangent,
    value_weight,
    decode_inputs,
    queries,
    new_keys,
    cache_keys,
    cache_values,
    lengths,
):
    core, high, x, low, y = (lax.axis_index(n) for n in NAMES)
    row_count, step_count = decode_inputs.shape[0], decode_inputs.shape[1]
    places = row_count * step_count
    place = jnp.stack([core, high, x, y, low])

    theirs, mine = partial_gradient(place, normed_inputs, value_cotangent)
    received = shift(theirs, "c", 1)
    swapped = swap_high(after(decode_inputs, theirs))

    rows = (4, 256, HD)
    own, *sent = small_call(
        core_sum_kernel, [(rows, F32)] + [(rows, BF16)] * 3, mine, received
    )
    along_x = [shift(sent[d - 1], "x", d) for d in (2, 1, 3)]
    swapped = after(swapped, own)
    (both,) = small_call(
        join_kernel, [((2, places, D // 8), BF16)], swapped, shift(swapped, "zl", 1)
    )
    near = exchange(both, "y", 1)

    attended_cache, fresh_weights = attend_cache(
        lengths, after(queries, own), new_keys.reshape(places, HD), cache_keys, cache_values
    )
    own, *along_x, both, attended_cache, fresh_weights = lax.optimization_barrier(
        (own, *along_x, both, attended_cache, fresh_weights)
    )
    rows = (256, HD)
    own, *sent = small_call(
        x_sum_kernel, [(rows, F32)] + [(rows, BF16)] * 3, own, *along_x, flops=8000 * MIB
    )
    along_z = [shift(sent[e - 1], "zh", e) for e in (2, 1, 3)]
    (near,) = small_call(pair_kernel, [((4, places, D // 8), BF16)], after(both, own), near)
    far = exchange(near, "y", 3)
    near_own, near_rest = arrange(place, near)
    own, *along_z, near_own, near_rest = lax.optimization_barrier(
        (own, *along_z, near_own, near_rest)
    )
    (updated,) = small_call(update_kernel, [(rows, BF16)], value_weight, own, *along_z)
    own = after(own, updated)
    (gradient,) = small_call(gradient_kernel, [(rows, F32)], own, *along_z, keep=False)

    gathered = jnp.stack([updated] + [shift(updated, "x", -d) for d in (1, 2, 3)])
    gathered, gradient = lax.optimization_barrier((gathered, gradient))
    other = shift(gathered, "c", 1)
    partial = project(
        project_own_kernel, pltpu.VMEM((2 * places, HD), F32), 1, place, near_own, gathered
    )
    partial = project(
        project_rest_kernel,
        pltpu.VMEM((4, places, HD), BF16),
        2,
        place,
        near_rest,
        far,
        gathered,
        other,
        partial,
    )
    exchanged = lax.all_to_all(partial, "zh", 0, 0, tiled=True)
    new_values, attended = finish(
        exchanged, attended_cache, fresh_weights, row_count, step_count
    )
    return (gradient, new_values, attended)


def solution(mesh):
    inner = Mesh(mesh.devices.reshape(tuple(SIZES.values())), NAMES)
    rows, columns = ("c", "zh", "x"), ("zl", "y")
    return jax.shard_map(
        shards,
        mesh=inner,
        in_specs=(
            P(rows, None),
            P(rows, columns),
            P(rows, columns),
            P(rows, None, columns),
            P(rows, None, columns),
            P(rows, None, columns),
            P(rows, None, columns),
            P(rows, None, columns),
            P(rows),
        ),
        out_specs=(
            P(rows, columns),
            P(rows, None, columns),
            P(rows, None, columns),
        ),
        check_vma=False,
    )
```

```python
import math

import jax
import jax.numpy as jnp
import numpy as np
from jax import lax
from jax.experimental import pallas as pl
from jax.experimental.pallas import tpu as pltpu
from jax.sharding import Mesh, PartitionSpec as P

D = 8192
HEADS = 8
HD = 128
SIZES = {"c": 2, "zh": 4, "x": 4, "zl": 2, "y": 4}
NAMES = tuple(SIZES)
STEP = 0.4 / math.sqrt(D)
MIB = 1 << 20
F32 = jnp.float32
BF16 = jnp.bfloat16
VMEM = pl.BlockSpec(memory_space=pltpu.VMEM)
SMEM = pl.BlockSpec(memory_space=pltpu.SMEM)
HBM = pl.BlockSpec(memory_space=pltpu.HBM)


def shift(value, axis, by):
    n = SIZES[axis]
    return lax.ppermute(value, axis, [(i, (i + by) % n) for i in range(n)])


def exchange(value, axis, bit):
    return lax.ppermute(value, axis, [(i, i ^ bit) for i in range(SIZES[axis])])


def swap_high(value):
    pairs = [(zh * 4 + y, y * 4 + (zh + y) % 4) for zh in range(4) for y in range(4)]
    return lax.ppermute(value, ("zh", "y"), pairs)


def after(value, *others):
    return lax.optimization_barrier((value, *others))[0]


def partial_kernel(place, x_hbm, v_hbm, theirs_ref, mine_ref, chunks, v_ref, sems):
    core, high, x = place[0], place[1], place[2]
    order = [(1 - core, theirs_ref, e) for e in range(4)] + [(core, mine_ref, e) for e in range(4)]
    copies = [pltpu.make_async_copy(v_hbm, v_ref, sems.at[8])]
    copies[0].start()
    for i, (half, _, e) in enumerate(order):
        column = (half * 4 + lax.rem(high + e, 4)) * 1024
        copies.append(
            pltpu.make_async_copy(
                x_hbm.at[:, pl.ds(pl.multiple_of(column, 1024), 1024)], chunks.at[i], sems.at[i]
            )
        )
        copies[-1].start()
    copies[0].wait()
    for i, (_, out_ref, e) in enumerate(order):
        copies[i + 1].wait()
        product = lax.dot_general(
            v_ref[...], chunks[i], (((0,), (0,)), ((), ())), preferred_element_type=F32
        )
        for block in range(4):
            rows = product[:, block * 256 : (block + 1) * 256].T
            out_ref[lax.rem(block + 4 - x, 4), e] = rows.astype(out_ref.dtype)


def partial_gradient(place, normed_inputs, value_cotangent):
    tokens = normed_inputs.shape[0]
    normed_inputs = pltpu.with_memory_space_constraint(normed_inputs, pltpu.HBM)
    value_cotangent = pltpu.with_memory_space_constraint(value_cotangent, pltpu.HBM)
    return pl.pallas_call(
        partial_kernel,
        in_specs=[SMEM, HBM, HBM],
        out_specs=[VMEM, VMEM],
        out_shape=[pltpu.VMEM((4, 4, 256, HD), BF16)] * 2,
        scratch_shapes=[
            pltpu.VMEM((8, tokens, 1024), BF16),
            pltpu.VMEM((tokens, HD), BF16),
            pltpu.SemaphoreType.DMA((9,)),
        ],
        compiler_params=pltpu.CompilerParams(vmem_limit_bytes=48 * MIB),
        cost_estimate=pl.CostEstimate(
            flops=2 * tokens * D * HD, bytes_accessed=tokens * D * 2, transcendentals=0
        ),
    )(place, normed_inputs, value_cotangent)


def small_call(kernel, outs, *args, keep=True, flops=MIB):
    return pl.pallas_call(
        kernel,
        in_specs=[VMEM] * len(args),
        out_specs=[VMEM] * len(outs),
        out_shape=[
            (pltpu.VMEM if keep else jax.ShapeDtypeStruct)(shape, dtype) for shape, dtype in outs
        ],
        compiler_params=pltpu.CompilerParams(vmem_limit_bytes=16 * MIB),
        cost_estimate=pl.CostEstimate(flops=flops, bytes_accessed=2 * MIB, transcendentals=0),
    )(*args)


def core_sum_kernel(mine, received, o0, o1, o2, o3):
    o0[...] = mine[0].astype(F32) + received[0].astype(F32)
    for d, out in ((1, o1), (2, o2), (3, o3)):
        out[...] = mine[d] + received[d]


def join_kernel(first, second, out):
    rows, steps = first.shape[0], first.shape[1]
    for i, ref in enumerate((first, second)):
        for r in range(rows):
            out[i, r * steps : (r + 1) * steps] = ref[r]


def pair_kernel(first, second, out):
    out[:2] = first[...]
    out[2:] = second[...]


def x_sum_kernel(own, r1, r2, r3, o0, o1, o2, o3):
    for e, out in enumerate((o0, o1, o2, o3)):
        total = own[e] + r1[e].astype(F32) + r2[e].astype(F32) + r3[e].astype(F32)
        out[...] = total.astype(out.dtype)


def total_of(own, r1, r2, r3):
    return own[...] + r1[...].astype(F32) + r2[...].astype(F32) + r3[...].astype(F32)


def update_kernel(weight, own, r1, r2, r3, updated):
    total = total_of(own, r1, r2, r3)
    updated[...] = (weight[...].astype(F32) - STEP * total).astype(BF16)


def gradient_kernel(own, r1, r2, r3, gradient):
    gradient[...] = total_of(own, r1, r2, r3)


def attend_kernel(
    lengths, raw_queries, new_keys, cache_keys, cache_values, mixed_ref, weights_ref, queries
):
    rows = cache_keys.shape[0]
    slots = cache_keys.shape[1]
    steps = raw_queries.shape[1]
    every = HEADS * rows * steps
    factor = 1.0 / math.sqrt(HD)
    for r in range(rows):
        queries[r * steps : (r + 1) * steps] = raw_queries[r]
    heads = jnp.concatenate([queries[:, q * HD : (q + 1) * HD] for q in range(HEADS)], axis=0)
    place = lax.broadcasted_iota(jnp.int32, (every, slots), 0) % (rows * steps)
    lane = lax.broadcasted_iota(jnp.int32, (every, slots), 1)
    row = place // steps
    contract = (((1,), (1,)), ((), ()))
    scores = jnp.full((every, slots), -1e30, F32)
    for r in range(rows):
        product = lax.dot_general(heads, cache_keys[r], contract, preferred_element_type=F32)
        scores = jnp.where((row == r) & (lane < lengths[r]), product * factor, scores)
    fresh = lax.dot_general(heads, new_keys[...], contract, preferred_element_type=F32) * factor
    from_place, to_place = place[:, : rows * steps], lane[:, : rows * steps]
    visible = (from_place // steps == to_place // steps) & (to_place <= from_place)
    fresh = jnp.where(visible, fresh, -1e30)
    highest = jnp.maximum(
        jnp.max(scores, axis=1, keepdims=True), jnp.max(fresh, axis=1, keepdims=True)
    )
    cache_exp = jnp.exp(scores - highest)
    fresh_exp = jnp.exp(fresh - highest)
    total = jnp.sum(cache_exp, axis=1, keepdims=True) + jnp.sum(fresh_exp, axis=1, keepdims=True)
    cache_weights = (cache_exp / total).astype(BF16)
    weights_ref[...] = (fresh_exp / total).astype(BF16)
    mixed = jnp.zeros((every, HD), F32)
    for r in range(rows):
        product = jnp.dot(cache_weights, cache_values[r], preferred_element_type=F32)
        mixed = jnp.where(row == r, product, mixed)
    mixed_ref[...] = mixed


def attend_cache(lengths, queries, new_keys, cache_keys, cache_values):
    places = queries.shape[0] * queries.shape[1]
    return pl.pallas_call(
        attend_kernel,
        in_specs=[SMEM] + [VMEM] * 4,
        out_specs=[VMEM, VMEM],
        out_shape=[
            jax.ShapeDtypeStruct((HEADS * places, HD), F32),
            jax.ShapeDtypeStruct((HEADS * places, places), BF16),
        ],
        scratch_shapes=[pltpu.VMEM((places, HEADS * HD), BF16)],
        compiler_params=pltpu.CompilerParams(vmem_limit_bytes=16 * MIB),
        cost_estimate=pl.CostEstimate(
            flops=8000 * MIB, bytes_accessed=20 * MIB, transcendentals=0
        ),
    )(lengths, queries, new_keys, cache_keys, cache_values)


def fill_rows(rows, x, updated):
    for d in range(4):
        rows[pl.ds(pl.multiple_of(lax.rem(x + d, 4) * 256, 256), 256), :] = updated[d]


def tokens_of(place, bits):
    return lax.rem(jnp.bitwise_xor(place[3], bits) + 4 - place[1], 4)


def project_own_kernel(place, near, u, out_ref, rows):
    own = jnp.where(place[0] == place[4], 0, 1)
    fill_rows(rows, place[2], u)
    inputs = jnp.concatenate([near[own], near[2 + own]], axis=0)
    out_ref[...] = jnp.dot(inputs, rows[...], preferred_element_type=F32)


def project_rest_kernel(place, near, far, u_own, u_other, start, o0, o1, o2, o3, rows, last, sums):
    own = jnp.where(place[0] == place[4], 0, 1)
    fill_rows(last, place[2], u_own)
    fill_rows(rows, place[2], u_other)
    inputs = [near[1 - own], near[3 - own], far[1 - own], far[3 - own]]
    product = jnp.dot(
        jnp.concatenate(inputs, axis=0), rows[...], preferred_element_type=F32
    )
    inputs = jnp.concatenate([far[own], far[2 + own]], axis=0)
    more = jnp.dot(inputs, last[...], preferred_element_type=F32)
    size = far.shape[1]
    for i, bits in enumerate((0, 1, 3, 2)):
        rest = start[i * size : (i + 1) * size] if i < 2 else more[(i - 2) * size : (i - 1) * size]
        total = product[i * size : (i + 1) * size] + rest
        sums[lax.rem(tokens_of(place, bits) + 4 - place[1], 4)] = total
    for e, out in enumerate((o0, o1, o2, o3)):
        out[...] = sums[e].astype(out.dtype)


def project(kernel, outs, scratches, place, *args):
    return pl.pallas_call(
        kernel,
        in_specs=[SMEM] + [VMEM] * len(args),
        out_specs=[VMEM] * len(outs),
        out_shape=[jax.ShapeDtypeStruct(shape, dtype) for shape, dtype in outs],
        scratch_shapes=[pltpu.VMEM(shape, dtype) for shape, dtype in scratches],
        compiler_params=pltpu.CompilerParams(vmem_limit_bytes=16 * MIB),
        cost_estimate=pl.CostEstimate(
            flops=2 * 256 * 1024 * HD, bytes_accessed=3 * MIB // 4, transcendentals=0
        ),
    )(place, *args)


def finish_kernel(own, r1, r2, r3, mixed, weights, values_ref, attended_ref):
    steps = values_ref.shape[1]
    values = total_of(own, r1, r2, r3).astype(BF16)
    for r in range(values_ref.shape[0]):
        values_ref[r] = values[r * steps : (r + 1) * steps]
    places = values.shape[0]
    for q in range(HEADS):
        span = slice(q * places, (q + 1) * places)
        head = mixed[span] + jnp.dot(weights[span], values, preferred_element_type=F32)
        head = head.astype(BF16)
        for r in range(values_ref.shape[0]):
            attended_ref[r, :, q * HD : (q + 1) * HD] = head[r * steps : (r + 1) * steps]


def finish(parts, mixed, weights, rows, steps):
    return pl.pallas_call(
        finish_kernel,
        in_specs=[VMEM] * 6,
        out_specs=[VMEM, VMEM],
        out_shape=[
            jax.ShapeDtypeStruct((rows, steps, HD), BF16),
            jax.ShapeDtypeStruct((rows, steps, HEADS * HD), BF16),
        ],
        compiler_params=pltpu.CompilerParams(vmem_limit_bytes=16 * MIB),
    )(*parts, mixed, weights)


def shards(
    normed_inputs,
    value_cotangent,
    value_weight,
    decode_inputs,
    queries,
    new_keys,
    cache_keys,
    cache_values,
    lengths,
):
    core, high, x, low, y = (lax.axis_index(n) for n in NAMES)
    row_count, step_count = decode_inputs.shape[0], decode_inputs.shape[1]
    places = row_count * step_count
    place = jnp.stack([core, high, x, y, low])

    theirs, mine = partial_gradient(place, normed_inputs, value_cotangent)
    received = shift(theirs, "c", 1)
    swapped = swap_high(after(decode_inputs, theirs))

    rows = (4, 256, HD)
    own, *sent = small_call(
        core_sum_kernel, [(rows, F32)] + [(rows, BF16)] * 3, mine, received
    )
    along_x = [shift(sent[d - 1], "x", d) for d in (2, 1, 3)]
    swapped = after(swapped, own)
    (both,) = small_call(
        join_kernel, [((2, places, D // 8), BF16)], swapped, shift(swapped, "zl", 1)
    )
    near = exchange(both, "y", 1)

    own, *along_x, both = lax.optimization_barrier((own, *along_x, both))
    rows = (256, HD)
    own, *sent = small_call(
        x_sum_kernel, [(rows, F32)] + [(rows, BF16)] * 3, own, *along_x, flops=8000 * MIB
    )
    along_z = [shift(sent[e - 1], "zh", e) for e in (2, 1, 3)]
    (near,) = small_call(pair_kernel, [((4, places, D // 8), BF16)], after(both, own), near)
    far = exchange(near, "y", 3)
    attended_cache, fresh_weights = attend_cache(
        lengths, after(queries, near), new_keys.reshape(places, HD), cache_keys, cache_values
    )
    own, *along_z, attended_cache, fresh_weights = lax.optimization_barrier(
        (own, *along_z, attended_cache, fresh_weights)
    )
    (updated,) = small_call(update_kernel, [(rows, BF16)], value_weight, own, *along_z)
    own = after(own, updated)
    (gradient,) = small_call(gradient_kernel, [(rows, F32)], own, *along_z, keep=False)

    gathered = jnp.stack([updated] + [shift(updated, "x", -d) for d in (1, 2, 3)])
    gathered, gradient = lax.optimization_barrier((gathered, gradient))
    other = shift(gathered, "c", 1)
    scratch, tokens = ((1024, HD), BF16), (places, HD)
    (partial,) = project(
        project_own_kernel, [((2 * places, HD), F32)], [scratch], place, near, gathered
    )
    own, *sent = project(
        project_rest_kernel,
        [(tokens, F32)] + [(tokens, BF16)] * 3,
        [scratch, scratch, ((4, places, HD), F32)],
        place,
        near,
        far,
        gathered,
        other,
        partial,
    )
    exchanged = [own] + [shift(sent[e - 1], "zh", e) for e in (2, 1, 3)]
    new_values, attended = finish(
        exchanged, attended_cache, fresh_weights, row_count, step_count
    )
    return (gradient, new_values, attended)


def solution(mesh):
    inner = Mesh(mesh.devices.reshape(tuple(SIZES.values())), NAMES)
    rows, columns = ("c", "zh", "x"), ("zl", "y")
    return jax.shard_map(
        shards,
        mesh=inner,
        in_specs=(
            P(rows, None),
            P(rows, columns),
            P(rows, columns),
            P(rows, None, columns),
            P(rows, None, columns),
            P(rows, None, columns),
            P(rows, None, columns),
            P(rows, None, columns),
            P(rows),
        ),
        out_specs=(
            P(rows, columns),
            P(rows, None, columns),
            P(rows, None, columns),
        ),
        check_vma=False,
    )
```

```python
import math

import jax
import jax.numpy as jnp
import numpy as np
from jax import lax
from jax.experimental import pallas as pl
from jax.experimental.pallas import tpu as pltpu
from jax.sharding import Mesh, PartitionSpec as P

D = 8192
HEADS = 8
HD = 128
SIZES = {"c": 2, "zh": 4, "x": 4, "zl": 2, "y": 4}
NAMES = tuple(SIZES)
STEP = 0.4 / math.sqrt(D)
MIB = 1 << 20
F32 = jnp.float32
BF16 = jnp.bfloat16
VMEM = pl.BlockSpec(memory_space=pltpu.VMEM)
SMEM = pl.BlockSpec(memory_space=pltpu.SMEM)
HBM = pl.BlockSpec(memory_space=pltpu.HBM)


def shift(value, axis, by):
    n = SIZES[axis]
    return lax.ppermute(value, axis, [(i, (i + by) % n) for i in range(n)])


def exchange(value, axis, bit):
    return lax.ppermute(value, axis, [(i, i ^ bit) for i in range(SIZES[axis])])


def swap_high(value):
    pairs = [(zh * 4 + y, y * 4 + (zh + y) % 4) for zh in range(4) for y in range(4)]
    return lax.ppermute(value, ("zh", "y"), pairs)


def after(value, *others):
    return lax.optimization_barrier((value, *others))[0]


def partial_kernel(place, x_hbm, v_hbm, theirs_ref, mine_ref, chunks, v_ref, sems):
    core, high, x = place[0], place[1], place[2]
    order = [(1 - core, theirs_ref, e) for e in range(4)] + [(core, mine_ref, e) for e in range(4)]
    copies = [pltpu.make_async_copy(v_hbm, v_ref, sems.at[8])]
    copies[0].start()
    for i, (half, _, e) in enumerate(order):
        column = (half * 4 + lax.rem(high + e, 4)) * 1024
        copies.append(
            pltpu.make_async_copy(
                x_hbm.at[:, pl.ds(pl.multiple_of(column, 1024), 1024)], chunks.at[i], sems.at[i]
            )
        )
        copies[-1].start()
    copies[0].wait()
    for i, (_, out_ref, e) in enumerate(order):
        copies[i + 1].wait()
        product = lax.dot_general(
            v_ref[...], chunks[i], (((0,), (0,)), ((), ())), preferred_element_type=F32
        )
        for block in range(4):
            rows = product[:, block * 256 : (block + 1) * 256].T
            out_ref[lax.rem(block + 4 - x, 4), e] = rows.astype(out_ref.dtype)


def partial_gradient(place, normed_inputs, value_cotangent):
    tokens = normed_inputs.shape[0]
    normed_inputs = pltpu.with_memory_space_constraint(normed_inputs, pltpu.HBM)
    value_cotangent = pltpu.with_memory_space_constraint(value_cotangent, pltpu.HBM)
    return pl.pallas_call(
        partial_kernel,
        in_specs=[SMEM, HBM, HBM],
        out_specs=[VMEM, VMEM],
        out_shape=[pltpu.VMEM((4, 4, 256, HD), BF16)] * 2,
        scratch_shapes=[
            pltpu.VMEM((8, tokens, 1024), BF16),
            pltpu.VMEM((tokens, HD), BF16),
            pltpu.SemaphoreType.DMA((9,)),
        ],
        compiler_params=pltpu.CompilerParams(vmem_limit_bytes=48 * MIB),
        cost_estimate=pl.CostEstimate(
            flops=2 * tokens * D * HD, bytes_accessed=tokens * D * 2, transcendentals=0
        ),
    )(place, normed_inputs, value_cotangent)


def small_call(kernel, outs, *args, keep=True, flops=MIB):
    return pl.pallas_call(
        kernel,
        in_specs=[VMEM] * len(args),
        out_specs=[VMEM] * len(outs),
        out_shape=[
            (pltpu.VMEM if keep else jax.ShapeDtypeStruct)(shape, dtype) for shape, dtype in outs
        ],
        compiler_params=pltpu.CompilerParams(vmem_limit_bytes=16 * MIB),
        cost_estimate=pl.CostEstimate(flops=flops, bytes_accessed=2 * MIB, transcendentals=0),
    )(*args)


def core_sum_kernel(mine, received, o0, o1, o2, o3):
    o0[...] = mine[0].astype(F32) + received[0].astype(F32)
    for d, out in ((1, o1), (2, o2), (3, o3)):
        out[...] = mine[d] + received[d]


def join_kernel(first, second, out):
    rows, steps = first.shape[0], first.shape[1]
    for i, ref in enumerate((first, second)):
        for r in range(rows):
            out[i, r * steps : (r + 1) * steps] = ref[r]


def pair_kernel(first, second, out):
    out[:2] = first[...]
    out[2:] = second[...]


def x_sum_kernel(own, r1, r2, r3, o0, o1, o2, o3):
    for e, out in enumerate((o0, o1, o2, o3)):
        total = own[e] + r1[e].astype(F32) + r2[e].astype(F32) + r3[e].astype(F32)
        out[...] = total.astype(out.dtype)


def total_of(own, r1, r2, r3):
    return own[...] + r1[...].astype(F32) + r2[...].astype(F32) + r3[...].astype(F32)


def update_kernel(weight, own, r1, r2, r3, updated):
    total = total_of(own, r1, r2, r3)
    updated[...] = (weight[...].astype(F32) - STEP * total).astype(BF16)


def gradient_kernel(own, r1, r2, r3, gradient):
    gradient[...] = total_of(own, r1, r2, r3)


def attend_kernel(
    lengths, raw_queries, new_keys, cache_keys, cache_values, mixed_ref, weights_ref, queries
):
    rows = cache_keys.shape[0]
    slots = cache_keys.shape[1]
    steps = raw_queries.shape[1]
    every = HEADS * rows * steps
    factor = 1.0 / math.sqrt(HD)
    for r in range(rows):
        queries[r * steps : (r + 1) * steps] = raw_queries[r]
    heads = jnp.concatenate([queries[:, q * HD : (q + 1) * HD] for q in range(HEADS)], axis=0)
    place = lax.broadcasted_iota(jnp.int32, (every, slots), 0) % (rows * steps)
    lane = lax.broadcasted_iota(jnp.int32, (every, slots), 1)
    row = place // steps
    contract = (((1,), (1,)), ((), ()))
    scores = jnp.full((every, slots), -1e30, F32)
    for r in range(rows):
        product = lax.dot_general(heads, cache_keys[r], contract, preferred_element_type=F32)
        scores = jnp.where((row == r) & (lane < lengths[r]), product * factor, scores)
    fresh = lax.dot_general(heads, new_keys[...], contract, preferred_element_type=F32) * factor
    from_place, to_place = place[:, : rows * steps], lane[:, : rows * steps]
    visible = (from_place // steps == to_place // steps) & (to_place <= from_place)
    fresh = jnp.where(visible, fresh, -1e30)
    highest = jnp.maximum(
        jnp.max(scores, axis=1, keepdims=True), jnp.max(fresh, axis=1, keepdims=True)
    )
    cache_exp = jnp.exp(scores - highest)
    fresh_exp = jnp.exp(fresh - highest)
    total = jnp.sum(cache_exp, axis=1, keepdims=True) + jnp.sum(fresh_exp, axis=1, keepdims=True)
    cache_weights = (cache_exp / total).astype(BF16)
    weights_ref[...] = (fresh_exp / total).astype(BF16)
    mixed = jnp.zeros((every, HD), F32)
    for r in range(rows):
        product = jnp.dot(cache_weights, cache_values[r], preferred_element_type=F32)
        mixed = jnp.where(row == r, product, mixed)
    mixed_ref[...] = mixed


def attend_cache(lengths, queries, new_keys, cache_keys, cache_values):
    places = queries.shape[0] * queries.shape[1]
    return pl.pallas_call(
        attend_kernel,
        in_specs=[SMEM] + [VMEM] * 4,
        out_specs=[VMEM, VMEM],
        out_shape=[
            jax.ShapeDtypeStruct((HEADS * places, HD), F32),
            jax.ShapeDtypeStruct((HEADS * places, places), BF16),
        ],
        scratch_shapes=[pltpu.VMEM((places, HEADS * HD), BF16)],
        compiler_params=pltpu.CompilerParams(vmem_limit_bytes=16 * MIB),
        cost_estimate=pl.CostEstimate(
            flops=8000 * MIB, bytes_accessed=20 * MIB, transcendentals=0
        ),
    )(lengths, queries, new_keys, cache_keys, cache_values)


def fill_rows(rows, x, updated, core):
    for d, u in enumerate(updated):
        rows[pl.ds(pl.multiple_of(lax.rem(x + d, 4) * 256, 256), 256), :] = u[core]


def tokens_of(place, bits):
    return lax.rem(jnp.bitwise_xor(place[3], bits) + 4 - place[1], 4)


def project_kernel(place, near, far, u0, u1, u2, u3, o0, o1, o2, o3, rows, last, sums):
    own = jnp.where(place[0] == place[4], 0, 1)
    fill_rows(last, place[2], (u0, u1, u2, u3), 0)
    fill_rows(rows, place[2], (u0, u1, u2, u3), 1)
    inputs = [near[1 - own], near[3 - own], far[1 - own], far[3 - own]]
    product = jnp.dot(
        jnp.concatenate(inputs, axis=0), rows[...], preferred_element_type=F32
    )
    inputs = [near[own], near[2 + own], far[own], far[2 + own]]
    product += jnp.dot(
        jnp.concatenate(inputs, axis=0), last[...], preferred_element_type=F32
    )
    size = far.shape[1]
    for i, bits in enumerate((0, 1, 3, 2)):
        total = product[i * size : (i + 1) * size]
        sums[lax.rem(tokens_of(place, bits) + 4 - place[1], 4)] = total
    for e, out in enumerate((o0, o1, o2, o3)):
        out[...] = sums[e].astype(out.dtype)


def project(kernel, outs, scratches, place, *args):
    return pl.pallas_call(
        kernel,
        in_specs=[SMEM] + [VMEM] * len(args),
        out_specs=[VMEM] * len(outs),
        out_shape=[jax.ShapeDtypeStruct(shape, dtype) for shape, dtype in outs],
        scratch_shapes=[pltpu.VMEM(shape, dtype) for shape, dtype in scratches],
        compiler_params=pltpu.CompilerParams(vmem_limit_bytes=16 * MIB),
        cost_estimate=pl.CostEstimate(
            flops=2 * 256 * 1024 * HD, bytes_accessed=3 * MIB // 4, transcendentals=0
        ),
    )(place, *args)


def finish_kernel(own, r1, r2, r3, mixed, weights, values_ref, attended_ref):
    steps = values_ref.shape[1]
    values = total_of(own, r1, r2, r3).astype(BF16)
    for r in range(values_ref.shape[0]):
        values_ref[r] = values[r * steps : (r + 1) * steps]
    places = values.shape[0]
    for q in range(HEADS):
        span = slice(q * places, (q + 1) * places)
        head = mixed[span] + jnp.dot(weights[span], values, preferred_element_type=F32)
        head = head.astype(BF16)
        for r in range(values_ref.shape[0]):
            attended_ref[r, :, q * HD : (q + 1) * HD] = head[r * steps : (r + 1) * steps]


def finish(parts, mixed, weights, rows, steps):
    return pl.pallas_call(
        finish_kernel,
        in_specs=[VMEM] * 6,
        out_specs=[VMEM, VMEM],
        out_shape=[
            jax.ShapeDtypeStruct((rows, steps, HD), BF16),
            jax.ShapeDtypeStruct((rows, steps, HEADS * HD), BF16),
        ],
        compiler_params=pltpu.CompilerParams(vmem_limit_bytes=16 * MIB),
    )(*parts, mixed, weights)


def shards(
    normed_inputs,
    value_cotangent,
    value_weight,
    decode_inputs,
    queries,
    new_keys,
    cache_keys,
    cache_values,
    lengths,
):
    core, high, x, low, y = (lax.axis_index(n) for n in NAMES)
    row_count, step_count = decode_inputs.shape[0], decode_inputs.shape[1]
    places = row_count * step_count
    place = jnp.stack([core, high, x, y, low])

    theirs, mine = partial_gradient(place, normed_inputs, value_cotangent)
    received = shift(theirs, "c", 1)
    swapped = swap_high(after(decode_inputs, theirs))

    rows = (4, 256, HD)
    own, *sent = small_call(
        core_sum_kernel, [(rows, F32)] + [(rows, BF16)] * 3, mine, received
    )
    along_x = [shift(sent[d - 1], "x", d) for d in (2, 1, 3)]
    swapped = after(swapped, own)
    (both,) = small_call(
        join_kernel, [((2, places, D // 8), BF16)], swapped, shift(swapped, "zl", 1)
    )
    near = exchange(both, "y", 1)

    own, *along_x, both = lax.optimization_barrier((own, *along_x, both))
    rows = (256, HD)
    own, *sent = small_call(
        x_sum_kernel, [(rows, F32)] + [(rows, BF16)] * 3, own, *along_x, flops=8000 * MIB
    )
    along_z = [shift(sent[e - 1], "zh", e) for e in (2, 1, 3)]
    (near,) = small_call(pair_kernel, [((4, places, D // 8), BF16)], after(both, own), near)
    far = exchange(near, "y", 3)
    attended_cache, fresh_weights = attend_cache(
        lengths, after(queries, near), new_keys.reshape(places, HD), cache_keys, cache_values
    )
    own, *along_z, attended_cache, fresh_weights = lax.optimization_barrier(
        (own, *along_z, attended_cache, fresh_weights)
    )
    (updated,) = small_call(update_kernel, [(rows, BF16)], value_weight, own, *along_z)
    own = after(own, updated)
    (gradient,) = small_call(gradient_kernel, [(rows, F32)], own, *along_z, keep=False)

    pair = jnp.stack([updated, shift(updated, "c", 1)])
    gathered = [pair] + [shift(pair, "x", -d) for d in (1, 2, 3)]
    gathered, gradient = lax.optimization_barrier((gathered, gradient))
    scratch, tokens = ((1024, HD), BF16), (places, HD)
    own, *sent = project(
        project_kernel,
        [(tokens, F32)] + [(tokens, BF16)] * 3,
        [scratch, scratch, ((4, places, HD), F32)],
        place,
        near,
        far,
        *gathered,
    )
    exchanged = [own] + [shift(sent[e - 1], "zh", e) for e in (2, 1, 3)]
    new_values, attended = finish(
        exchanged, attended_cache, fresh_weights, row_count, step_count
    )
    return (gradient, new_values, attended)


def solution(mesh):
    inner = Mesh(mesh.devices.reshape(tuple(SIZES.values())), NAMES)
    rows, columns = ("c", "zh", "x"), ("zl", "y")
    return jax.shard_map(
        shards,
        mesh=inner,
        in_specs=(
            P(rows, None),
            P(rows, columns),
            P(rows, columns),
            P(rows, None, columns),
            P(rows, None, columns),
            P(rows, None, columns),
            P(rows, None, columns),
            P(rows, None, columns),
            P(rows),
        ),
        out_specs=(
            P(rows, columns),
            P(rows, None, columns),
            P(rows, None, columns),
        ),
        check_vma=False,
    )
```
